128 devices in a mesh: rows: 32 (over y, x_lo, z), cols: 4 (over x_hi, core).
Axes of the slice: x: 4 (x_hi: 2, x_lo: 2; x = x_hi * 2 + x_lo), y: 4, z: 4, core: 2. Of those that a mesh axis runs over, the one named last changes fastest.
Arguments:
- fmap_left: bfloat16 [64, 2048, 256], P('rows', 'cols'), may hold values from -6 to 6
- fmap_right: bfloat16 [64, 2048, 256], P('rows', 'cols'), may hold values from -6 to 6
- hidden_init: bfloat16 [64, 2048, 128], P('rows', 'cols'), may hold values from -3 to 3
- disp_init: int32 [64], P('rows'), may hold values from 0 to 191
- level_offset: int32 [64, 4], P('rows'), may hold values from -4 to 4
- motion_weight: bfloat16 [36, 128], replicated, may hold values from -1 to 1
- gate_weight: bfloat16 [2304, 256], replicated, may hold values from -0.125 to 0.125
- cand_weight: bfloat16 [2304, 128], replicated, may hold values from -0.125 to 0.125
- grad_hidden: bfloat16 [64, 2048, 128], P('rows', 'cols'), may hold values from -6 to 6
Outputs:
- grad_left: bfloat16 [64, 2048, 256], P('rows', 'cols')
- grad_right: bfloat16 [64, 2048, 256], P('rows', 'cols')
- grad_hidden_init: bfloat16 [64, 2048, 128], P('rows', 'cols')
- grad_motion_w: float32 [36, 128], replicated
- grad_gate_w: float32 [2304, 256], replicated
- grad_cand_w: float32 [2304, 128], replicated
The draws below stay inside these ranges and needn't reach their ends.
All inputs are finite; a program needn't handle non-finite values.
Results may differ from the reference program's by a relative error of at most 0.011.
Values may be sent and summed in bfloat16 or wider, within the bound.
No kernel may reach another device: no remote copies, remote signals or barrier semaphores. Data moves between devices by JAX's collectives and lax.ppermute only.
A program may use at most 64 MiB of HBM per device.

```python
import math
import jax
import jax.numpy as jnp
from jax import lax

CH = 256
HID = 128
LEVELS = 4
RADIUS = 4
DISP = 192
ITERS = 2
COLS_DEV = 512
ROWS = 64
COLS = 2048
FEATS = 36


def with_ends(values, stream_key, least, largest):
    extent = values.shape
    index_at = [jax.random.randint(jax.random.fold_in(stream_key, axis), (), 0, extent[axis]) for axis in range(len(extent))]
    values = values.at[tuple(index_at)].set(least)
    longest = extent.index(max(extent))
    index_at[longest] = (index_at[longest] + 1) % extent[longest]
    return values.at[tuple(index_at)].set(largest)


def level_of(own_key, shape, pieces, least, top_value):
    def one(position, blocks):
        steps = jax.random.uniform(jax.random.fold_in(jax.random.fold_in(own_key, 6), position), (blocks,), jnp.float32, least / len(pieces), top_value / len(pieces))
        return jnp.repeat(jnp.exp(steps), shape[position] // blocks).reshape((-1,) + (1,) * (len(shape) - position - 1))

    level = one(*pieces[0])
    for cut in pieces[1:]:
        level = level * one(*cut)
    return level


def noise(own_key, extent, scale, most, pieces=(), held_as=jnp.bfloat16):
    array = jax.random.normal(own_key, extent, jnp.float32) * scale
    if len(pieces) > 0:
        array = level_of(own_key, extent, pieces, -0.22, 0.18) * array
    return jnp.clip(array, min=-most, max=most).astype(held_as)


def setup_inputs(seed: int = 0) -> dict:
    key_of = jax.random.split(jax.random.key(seed), 10)
    return {
        "fmap_left": noise(key_of[0], (ROWS, COLS, CH), 1.0, 6.0, ((0, 32), (1, 4))),
        "fmap_right": noise(key_of[1], (ROWS, COLS, CH), 1.0, 6.0, ((0, 32), (1, 4))),
        "hidden_init": noise(key_of[2], (ROWS, COLS, HID), 0.5, 3.0, ((0, 32), (1, 4))),
        "disp_init": with_ends(jax.random.randint(key_of[3], (ROWS,), 0, DISP), jax.random.fold_in(key_of[3], 1), 0, DISP - 1).astype(jnp.int32),
        "level_offset": with_ends(jax.random.randint(key_of[4], (ROWS, LEVELS), 0 - RADIUS, RADIUS + 1), jax.random.fold_in(key_of[4], 1), 0 - RADIUS, RADIUS).astype(jnp.int32),
        "motion_weight": noise(key_of[5], (FEATS, HID), FEATS ** -0.5, 1.0),
        "gate_weight": noise(key_of[6], (18 * HID, 2 * HID), (18 * HID) ** -0.5, 0.125),
        "cand_weight": noise(key_of[7], (18 * HID, HID), (18 * HID) ** -0.5, 0.125),
        "grad_hidden": noise(key_of[8], (ROWS, COLS, HID), 1.0, 6.0, ((0, 32), (1, 4))),
    }


HIGHEST = lax.Precision.HIGHEST

def lookup_table(row_disparity, row_offsets, disp_range, radius, level_count):
    distance = disp_range - 1 - jnp.arange(disp_range, dtype=jnp.int32)
    tap_count = 2 * radius + 1
    tap_steps = jnp.arange(tap_count, dtype=jnp.int32) - radius
    tables = []
    for level_index in range(level_count):
        factor = 2 ** level_index
        centre = row_disparity // factor + row_offsets[:, level_index]
        wanted = centre[:, None] + tap_steps[None, :]
        bucket = distance // factor
        matches = bucket[None, :, None] == wanted[:, None, :]
        tables.append(jnp.where(matches, jnp.float32(1.0 / factor), jnp.float32(0.0)))
    return jnp.concatenate(tables, axis=2)

def skew_band(scores, disp_range):
    row_count, block_cols, wide = scores.shape
    flattened = scores.reshape(row_count, block_cols * wide)
    flattened = jnp.pad(flattened, ((0, 0), (0, block_cols)))
    return flattened.reshape(row_count, block_cols, wide + 1)[:, :, :disp_range + 1]

def unskew_band(banded, wide):
    row_count, block_cols, band_cols = banded.shape
    widened = jnp.pad(banded, ((0, 0), (0, 0), (0, wide + 1 - band_cols)))
    flattened = widened.reshape(row_count, block_cols * (wide + 1))[:, :block_cols * wide]
    return flattened.reshape(row_count, block_cols, wide)

def band_features(left_map, window, lookup, block_cols):
    row_count, col_count, channels = left_map.shape
    disp_range = window.shape[1] - col_count
    scaling = 1.0 / math.sqrt(channels)

    def one_block(block_index):
        offset = block_index * block_cols
        left_part = lax.dynamic_slice_in_dim(left_map, offset, block_cols, 1).astype(jnp.float32)
        right_part = lax.dynamic_slice_in_dim(window, offset, block_cols + disp_range, 1).astype(jnp.float32)
        scores = jnp.einsum('ric,rec->rie', left_part, right_part, precision=HIGHEST) * scaling
        banded = skew_band(scores, disp_range)[:, :, 1:]
        return jnp.einsum('ric,rcn->rin', banded, lookup, precision=HIGHEST)
    results = lax.map(one_block, jnp.arange(col_count // block_cols, dtype=jnp.int32))
    return jnp.transpose(results, (1, 0, 2, 3)).reshape(row_count, col_count, lookup.shape[2])

def band_backward(left_map, window, lookup, grad_features, block_cols):
    row_count, col_count, channels = left_map.shape
    disp_range = window.shape[1] - col_count
    scaling = 1.0 / math.sqrt(channels)

    def one_block(block_index, carry):
        grad_left, grad_window = carry
        offset = block_index * block_cols
        left_part = lax.dynamic_slice_in_dim(left_map, offset, block_cols, 1).astype(jnp.float32)
        right_part = lax.dynamic_slice_in_dim(window, offset, block_cols + disp_range, 1).astype(jnp.float32)
        grad_part = lax.dynamic_slice_in_dim(grad_features, offset, block_cols, 1)
        grad_band = jnp.einsum('rin,rcn->ric', grad_part, lookup, precision=HIGHEST)
        grad_band = jnp.pad(grad_band, ((0, 0), (0, 0), (1, 0)))
        grad_scores = (unskew_band(grad_band, block_cols + disp_range) * scaling).astype(jnp.bfloat16)
        grad_scores = grad_scores.astype(jnp.float32)
        left_term = jnp.einsum('rie,rec->ric', grad_scores, right_part, precision=HIGHEST)
        right_term = jnp.einsum('rie,ric->rec', grad_scores, left_part, precision=HIGHEST)
        grad_left = lax.dynamic_update_slice_in_dim(grad_left, left_term, offset, 1)
        previous = lax.dynamic_slice_in_dim(grad_window, offset, block_cols + disp_range, 1)
        grad_window = lax.dynamic_update_slice_in_dim(grad_window, previous + right_term, offset, 1)
        return (grad_left, grad_window)
    start_left = jnp.zeros((row_count, col_count, channels), jnp.float32)
    start_window = jnp.zeros((row_count, col_count + disp_range, channels), jnp.float32)
    return lax.fori_loop(0, col_count // block_cols, one_block, (start_left, start_window))

def conv_taps(padded, weight, row_count, col_count):
    channels = padded.shape[2]
    summed = jnp.zeros((row_count * col_count, weight.shape[1]), jnp.float32)
    for tap_index in range(9):
        row_step, col_step = divmod(tap_index, 3)
        sliced = padded[row_step:row_step + row_count, col_step:col_step + col_count].reshape(row_count * col_count, channels)
        summed = summed + jnp.dot(sliced, weight[tap_index * channels:(tap_index + 1) * channels], preferred_element_type=jnp.float32)
    return summed.reshape(row_count, col_count, weight.shape[1])

def conv_grads(grad_pad, in_pad, weight, row_count, col_count):
    channels = in_pad.shape[2]
    out_chans = weight.shape[1]
    centre = grad_pad[1:1 + row_count, 1:1 + col_count].reshape(row_count * col_count, out_chans)
    grad_in = jnp.zeros((row_count * col_count, channels), jnp.float32)
    pieces_list = []
    for tap_index in range(9):
        row_step, col_step = divmod(tap_index, 3)
        shifted = grad_pad[2 - row_step:2 - row_step + row_count, 2 - col_step:2 - col_step + col_count].reshape(row_count * col_count, out_chans)
        tap_weight = weight[tap_index * channels:(tap_index + 1) * channels]
        grad_in = grad_in + lax.dot_general(shifted, tap_weight, (((1,), (1,)), ((), ())), preferred_element_type=jnp.float32)
        source = in_pad[row_step:row_step + row_count, col_step:col_step + col_count].reshape(row_count * col_count, channels)
        pieces_list.append(lax.dot_general(source, centre, (((0,), (0,)), ((), ())), preferred_element_type=jnp.float32))
    return (grad_in.reshape(row_count, col_count, channels), jnp.concatenate(pieces_list, axis=0))

def border(field):
    return jnp.pad(field, ((1, 1), (1, 1), (0, 0)))

def reference(fmap_left, fmap_right, hidden_init, disp_init, level_offset, motion_weight, gate_weight, cand_weight, grad_hidden):
    row_count, col_count, channels = fmap_left.shape
    state_width = hidden_init.shape[2]
    block_cols = min(128, COLS_DEV)
    window = jnp.pad(fmap_right, ((0, 0), (DISP, 0), (0, 0)))
    lookup = lookup_table(disp_init, level_offset, DISP, RADIUS, LEVELS)
    features = band_features(fmap_left, window, lookup, block_cols)
    features_low = features.astype(jnp.bfloat16).reshape(row_count * col_count, FEATS)
    motion_pre = jnp.dot(features_low, motion_weight, preferred_element_type=jnp.float32)
    motion = jax.nn.silu(motion_pre).astype(jnp.bfloat16).reshape(row_count, col_count, state_width)
    motion_pad = border(motion)
    hidden = hidden_init
    history = []
    for iteration in range(ITERS):
        joint_pad = jnp.concatenate([border(hidden), motion_pad], axis=2)
        gate_pre = conv_taps(joint_pad, gate_weight, row_count, col_count)
        update = jax.nn.sigmoid(gate_pre[:, :, :state_width])
        reset_gate = jax.nn.sigmoid(gate_pre[:, :, state_width:])
        previous = hidden.astype(jnp.float32)
        reset_hidden = (reset_gate * previous).astype(jnp.bfloat16)
        cand_pad = jnp.concatenate([border(reset_hidden), motion_pad], axis=2)
        candidate = jnp.tanh(conv_taps(cand_pad, cand_weight, row_count, col_count))
        history.append((previous, joint_pad, cand_pad, update, reset_gate, candidate))
        hidden = ((1.0 - update) * previous + update * candidate).astype(jnp.bfloat16)
    grad_state = grad_hidden.astype(jnp.float32)
    grad_motion = jnp.zeros((row_count, col_count, state_width), jnp.float32)
    grad_gate_w = jnp.zeros(gate_weight.shape, jnp.float32)
    grad_cand_w = jnp.zeros(cand_weight.shape, jnp.float32)
    for iteration in reversed(range(ITERS)):
        previous, joint_pad, cand_pad, update, reset_gate, candidate = history[iteration]
        grad_cand_pre = (grad_state * update * (1.0 - candidate * candidate)).astype(jnp.bfloat16)
        grad_cand_in, cand_part = conv_grads(border(grad_cand_pre), cand_pad, cand_weight, row_count, col_count)
        grad_cand_w = grad_cand_w + cand_part
        grad_reset_hidden = grad_cand_in[:, :, :state_width]
        grad_motion = grad_motion + grad_cand_in[:, :, state_width:]
        grad_update = grad_state * (candidate - previous) * update * (1.0 - update)
        grad_reset = grad_reset_hidden * previous * reset_gate * (1.0 - reset_gate)
        grad_gate_pre = jnp.concatenate([grad_update, grad_reset], axis=2).astype(jnp.bfloat16)
        grad_joint, gate_part = conv_grads(border(grad_gate_pre), joint_pad, gate_weight, row_count, col_count)
        grad_gate_w = grad_gate_w + gate_part
        grad_state = grad_state * (1.0 - update) + grad_reset_hidden * reset_gate + grad_joint[:, :, :state_width]
        grad_motion = grad_motion + grad_joint[:, :, state_width:]
    sigmoid_pre = jax.nn.sigmoid(motion_pre)
    slope = sigmoid_pre * (1.0 + motion_pre * (1.0 - sigmoid_pre))
    grad_motion_pre = (grad_motion.reshape(row_count * col_count, state_width) * slope).astype(jnp.bfloat16)
    grad_features = lax.dot_general(grad_motion_pre, motion_weight, (((1,), (1,)), ((), ())), preferred_element_type=jnp.float32)
    grad_motion_w = lax.dot_general(features_low, grad_motion_pre, (((0,), (0,)), ((), ())), preferred_element_type=jnp.float32)
    grad_left, grad_window = band_backward(fmap_left, window, lookup, grad_features.reshape(row_count, col_count, FEATS), block_cols)
    grad_right = grad_window[:, DISP:]
    normaliser = 1.0 / math.sqrt(ROWS * COLS)
    return (grad_left.astype(jnp.bfloat16), grad_right.astype(jnp.bfloat16), grad_state.astype(jnp.bfloat16), grad_motion_w * normaliser, grad_gate_w * normaliser, grad_cand_w * normaliser)
```

```python
import math

import jax
import jax.numpy as jnp
from jax import lax
from jax.experimental import pallas as pl
from jax.experimental.pallas import tpu as pltpu
from jax.sharding import PartitionSpec as P

LEVELS = 4
RADIUS = 4
DISP = 192
TAPS = 2 * RADIUS + 1
HALO = 16
LANES = 128
CHUNK_ROWS = 64

BF16 = jnp.bfloat16
F32 = jnp.float32
VMEM = pl.BlockSpec(memory_space=pltpu.VMEM)
SMEM = pl.BlockSpec(memory_space=pltpu.SMEM)


def dot(a, b):
    return jnp.dot(a, b, preferred_element_type=F32)


def dot_nt(a, b):
    return lax.dot_general(a, b, (((1,), (1,)), ((), ())), preferred_element_type=F32)


def dot_tn(a, b):
    return lax.dot_general(a, b, (((0,), (0,)), ((), ())), preferred_element_type=F32)


def split_dot(a, table, contract):
    high = a.astype(BF16)
    low = (a - high.astype(F32)).astype(BF16)
    return contract(high, table) + contract(low, table)


def kernel_call(body, outs, ins, scalars, scratch, flops):
    bytes_moved = sum(x.size * x.dtype.itemsize for x in ins) + sum(
        math.prod(o.shape) * o.dtype.itemsize for o in outs
    )
    return pl.pallas_call(
        body,
        out_shape=outs,
        in_specs=[SMEM] * scalars + [VMEM] * (len(ins) - scalars),
        out_specs=[VMEM] * len(outs),
        scratch_shapes=scratch,
        compiler_params=pltpu.CompilerParams(vmem_limit_bytes=48 * 2**20),
        cost_estimate=pl.CostEstimate(flops=flops, bytes_accessed=bytes_moved, transcendentals=0),
    )(*ins)


def array(shape, dtype):
    return jax.ShapeDtypeStruct(shape, dtype)


def lookup_rows(position, valid, disparity, offsets, row):
    count = position.shape[0]
    feature = lax.broadcasted_iota(jnp.int32, (count, LANES), 1)
    table = jnp.zeros((count, LANES), F32)
    for level in range(LEVELS):
        centre = (disparity[row] >> level) + offsets[row, level]
        tap = feature - level * TAPS
        matches = (position >> level) == tap + (centre - RADIUS)
        matches = matches & (tap >= 0) & (tap < TAPS) & valid
        table = jnp.where(matches, 1.0 / 2**level, table)
    return table.astype(BF16)


def sides(odd, first, second):
    return jnp.where(odd, first, second), jnp.where(odd, second, first)


def store_taps(ref, row, lane, step, value, forward):
    wide = value.shape[0]
    left = pltpu.roll(value, 1, 0).astype(BF16)
    right = pltpu.roll(value, wide - 1, 0).astype(BF16)
    taps = (left, value.astype(BF16), right) if forward else (right, value.astype(BF16), left)
    for tap in range(3):
        start = lane + tap * step
        ref[row, :, start : start + LANES] = taps[tap]


def motion_kernel(place, disparity, offsets, left, right, got_a, got_b, weight, motion, pre, feats, ext, window, flipped):
    odd = place[1] % 2 == 1
    cols = left.shape[1]
    wide = cols + 2 * HALO
    block = wide // 2
    span = 512
    tail = DISP + HALO
    flat = (lax.broadcasted_iota(jnp.int32, (LANES, LANES), 0)
            + lax.broadcasted_iota(jnp.int32, (LANES, LANES), 1))
    mirror = jnp.where(flat == LANES - 1, 1.0, 0.0).astype(BF16)
    total = window.shape[0]
    position = lax.broadcasted_iota(jnp.int32, (span, LANES), 0) - (block - 1)
    valid = (position >= 0) & (position < DISP)
    for row in range(2):
        from_left, from_right = sides(odd, got_a[row], got_b[row])
        ext[0:HALO] = from_left[tail : tail + HALO]
        ext[HALO : HALO + cols] = left[row]
        ext[HALO + cols : wide] = from_right[tail + HALO : tail + 2 * HALO]
        window[0:tail] = from_left[0:tail]
        window[tail : tail + cols] = right[row]
        window[tail + cols : tail + cols + HALO] = from_right[tail + 2 * HALO :]
        window[tail + cols + HALO :] = jnp.zeros((total - tail - cols - HALO, window.shape[1]), BF16)
        parts = total // LANES
        for part in range(parts):
            source = window[(parts - 1 - part) * LANES : (parts - part) * LANES]
            flipped[part * LANES : (part + 1) * LANES] = dot(mirror, source).astype(BF16)
        flipped[total:] = jnp.zeros((flipped.shape[0] - total, window.shape[1]), BF16)
        table = lookup_rows(position, valid, disparity, offsets, row)
        for part in range(2):
            start = part * block
            base = total - DISP - start - block
            scores = dot_nt(ext[start : start + block], flipped[base : base + span])
            scores = scores * (1.0 / math.sqrt(left.shape[2]))
            band = pltpu.roll(scores, 0, 1, stride=1, stride_axis=0)
            found = split_dot(band, table, dot).astype(BF16)
            value = dot(found, weight[...])
            feats[row, start : start + block] = found
            pre[row, start : start + block] = value
            motion[row, start : start + block] = (value * jax.nn.sigmoid(value)).astype(BF16)


def image_columns(place, wide, cols, cols_axis):
    column = lax.broadcasted_iota(jnp.int32, (wide, LANES), 0) - HALO + place[1] * cols
    return (column >= 0) & (column < cols * cols_axis)


def fill_rows(store, odd, own, first, second):
    for row in range(2):
        above, below = sides(odd, first[row], second[row])
        store(row, above.astype(F32))
        store(4 + row, below.astype(F32))
        store(2 + row, own[row].astype(F32))


def gates(fields, resets, gate_w, update, reset, reset_hidden, wide):
    block = wide // 2
    deep = gate_w.shape[0] // 3

    def gate_part(step, carry):
        row, start = step // 2, pl.multiple_of((step % 2) * block, 16)
        here = pl.ds(start, block)
        total = sum(dot(fields[row + a, here], gate_w[a * deep : (a + 1) * deep]) for a in range(3))
        reset_part = jax.nn.sigmoid(total[:, LANES:])
        update[row, here] = jax.nn.sigmoid(total[:, :LANES])
        reset[row, here] = reset_part
        hidden = fields[row + 1, here, 2 * LANES : 3 * LANES].astype(F32)
        reset_hidden[row, here] = (reset_part * hidden).astype(BF16)
        return carry

    lax.fori_loop(0, 8, gate_part, 0)
    for row in range(4):
        store_taps(resets, row, 0, 2 * LANES, reset_hidden[row].astype(F32), True)
        for tap in range(3):
            start = (2 * tap + 1) * LANES
            resets[row, :, start : start + LANES] = fields[row + 1, :, start : start + LANES]


def load_fields(odd, fields, hidden, hidden_a, hidden_b, motion, motion_a, motion_b):
    fill_rows(lambda r, v: store_taps(fields, r, 0, 2 * LANES, v, True), odd, hidden, hidden_a, hidden_b)
    fill_rows(lambda r, v: store_taps(fields, r, LANES, 2 * LANES, v, True), odd, motion, motion_a, motion_b)


def candidate_part(resets, cand_w, row, here):
    deep = cand_w.shape[0] // 3
    total = sum(dot(resets[row + a, here], cand_w[a * deep : (a + 1) * deep]) for a in range(3))
    return jnp.tanh(total)


def first_kernel(cols_axis, place, hidden, hidden_a, hidden_b, motion, motion_a, motion_b, gate_w, cand_w,
                 later, update, reset, reset_hidden, candidate, fields, resets):
    odd = place[0] % 2 == 1
    wide = hidden.shape[1]
    block = wide // 2
    load_fields(odd, fields, hidden, hidden_a, hidden_b, motion, motion_a, motion_b)
    gates(fields, resets, gate_w, update, reset, reset_hidden, wide)
    inside = image_columns(place, wide, wide - 2 * HALO, cols_axis)
    for row in range(2):
        for start in (0, block):
            here = pl.ds(start, block)
            new = candidate_part(resets, cand_w, row, here)
            candidate[row, here] = new
            gate = update[row + 1, here]
            old = hidden[row, here].astype(F32)
            value = (1.0 - gate) * old + gate * new
            later[row, here] = jnp.where(inside[start : start + block], value, 0.0).astype(BF16)


def gradients_out(odd, grad, gate, new, old, row, here, grad_cand, grad_update, send_a, send_b):
    cand_part = (grad * gate * (1.0 - new * new)).astype(BF16)
    update_part = (grad * (new - old) * gate * (1.0 - gate)).astype(BF16)
    grad_cand[row, here] = cand_part
    grad_update[row, here] = update_part
    send_a[row, here] = cand_part
    send_b[row, here] = cand_part

    @pl.when(odd == (row == 0))
    def _():
        send_a[2, here] = update_part

    @pl.when(odd == (row == 1))
    def _():
        send_b[2, here] = update_part


def second_kernel(place, hidden, hidden_a, hidden_b, motion, motion_a, motion_b, gate_w, cand_w, grad_hidden,
                  update, reset, reset_hidden, grad_cand, grad_update, send_a, send_b, fields, resets):
    odd = place[0] % 2 == 1
    wide = hidden.shape[1]
    block = wide // 2
    load_fields(odd, fields, hidden, hidden_a, hidden_b, motion, motion_a, motion_b)
    gates(fields, resets, gate_w, update, reset, reset_hidden, wide)
    for row in range(2):
        for start in (0, block):
            here = pl.ds(start, block)
            new = candidate_part(resets, cand_w, row, here)
            gradients_out(odd, grad_hidden[row, here].astype(F32), update[row + 1, here], new,
                          hidden[row, here].astype(F32), row, here, grad_cand, grad_update, send_a, send_b)


def back_step(place, grad_cand, grad_a, grad_b, grad_update, hidden, hidden_a, hidden_b, reset, cand_wt, gate_wt,
              grad_gate, cand_taps, gate_taps, inner, grad_motion, finish):
    odd = place[0] % 2 == 1
    wide = hidden.shape[1]
    block = wide // 2
    fill_rows(lambda r, v: store_taps(cand_taps, r, 0, LANES, v, False), odd, grad_cand, grad_a, grad_b)
    deep = cand_wt.shape[0] // 3
    deeper = gate_wt.shape[0] // 3

    def cand_back(step, carry):
        row, start = step // 2, pl.multiple_of((step % 2) * block, 16)
        here = pl.ds(start, block)
        total = sum(dot(cand_taps[row + 2 - a, here], cand_wt[a * deep : (a + 1) * deep]) for a in range(3))
        inner[row, here] = total[:, :LANES]

        @pl.when((row == 1) | (row == 2))
        def _():
            grad_motion[row - 1, here] = total[:, LANES:]

        return carry

    lax.fori_loop(0, 8, cand_back, 0)
    above_h, below_h = sides(odd, hidden_a[1], hidden_b[1])[0], sides(odd, hidden_a[0], hidden_b[0])[1]
    above_u, below_u = sides(odd, grad_a[2], grad_b[2])
    hiddens = (above_h, hidden[0], hidden[1], below_h)
    updates = (above_u, grad_update[0], grad_update[1], below_u)
    for row in range(4):
        gate = reset[row]
        value = (inner[row] * hiddens[row].astype(F32) * gate * (1.0 - gate)).astype(BF16)
        store_taps(gate_taps, row, 0, 2 * LANES, updates[row].astype(F32), False)
        store_taps(gate_taps, row, LANES, 2 * LANES, value.astype(F32), False)
        if row in (1, 2):
            grad_gate[row - 1, :, :LANES] = updates[row]
            grad_gate[row - 1, :, LANES:] = value
    for row in range(2):
        for start in (0, block):
            here = pl.ds(start, block)
            total = sum(
                dot(gate_taps[row + 2 - a, here], gate_wt[a * deeper : (a + 1) * deeper]) for a in range(3)
            )
            grad_motion[row, here] += total[:, LANES:]
            finish(row, start, here, inner[row + 1, here] * reset[row + 1, here] + total[:, :LANES])


def later_back_kernel(cols_axis, place, grad_cand, grad_a, grad_b, grad_update, hidden, hidden_a, hidden_b, reset,
                      cand_wt, gate_wt, update, grad_hidden, older_hidden, older_update, older_candidate,
                      grad_gate, grad_state, grad_motion, older_cand, older_upd, send_a, send_b,
                      cand_taps, gate_taps, inner):
    odd = place[0] % 2 == 1
    wide = hidden.shape[1]
    block = wide // 2
    inside = image_columns(place, wide, wide - 2 * HALO, cols_axis)

    def finish(row, start, here, terms):
        gate = update[row + 1, here]
        grad = grad_hidden[row, here].astype(F32) * (1.0 - gate) + terms
        grad = jnp.where(inside[start : start + block], grad, 0.0)
        grad_state[row, here] = grad
        gradients_out(odd, grad, older_update[row + 1, here], older_candidate[row, here],
                      older_hidden[row, here].astype(F32), row, here, older_cand, older_upd, send_a, send_b)

    back_step(place, grad_cand, grad_a, grad_b, grad_update, hidden, hidden_a, hidden_b, reset, cand_wt, gate_wt,
              grad_gate, cand_taps, gate_taps, inner, grad_motion, finish)


def first_back_kernel(place, grad_cand, grad_a, grad_b, grad_update, hidden, hidden_a, hidden_b, reset,
                      cand_wt, gate_wt, update, grad_state, motion_so_far,
                      grad_gate, grad_first, grad_motion, cand_taps, gate_taps, inner):
    def finish(row, start, here, terms):
        gate = update[row + 1, here]
        grad = grad_state[row, here] * (1.0 - gate) + terms
        grad_first[row, here] = grad.astype(BF16)
        grad_motion[row, here] += motion_so_far[row, here]

    back_step(place, grad_cand, grad_a, grad_b, grad_update, hidden, hidden_a, hidden_b, reset, cand_wt, gate_wt,
              grad_gate, cand_taps, gate_taps, inner, grad_motion, finish)


def load_pixels(odd, pixels, hiddens, motion, motion_a, motion_b):
    wide = motion.shape[1]
    above, below = sides(odd, motion_a[1], motion_b[1])[0], sides(odd, motion_a[0], motion_b[0])[1]
    for row, value in enumerate((above, motion[0], motion[1], below)):
        pixels[row * wide : (row + 1) * wide, LANES:] = value
    for row, value in enumerate(hiddens):
        pixels[row * wide : (row + 1) * wide, :LANES] = value


def load_grads(taps, grads):
    wide = grads.shape[1]
    column = lax.broadcasted_iota(jnp.int32, (wide, LANES), 0)
    own = (column >= HALO) & (column < wide - HALO)
    depth = grads.shape[2]
    for row in range(2):
        for part in range(depth // LANES):
            value = jnp.where(own, grads[row, :, part * LANES : (part + 1) * LANES].astype(F32), 0.0)
            shifted = (pltpu.roll(value, wide - 1, 0), value, pltpu.roll(value, 1, 0))
            for tap in range(3):
                start = tap * depth + part * LANES
                taps[row * wide : (row + 1) * wide, start : start + LANES] = shifted[tap].astype(BF16)


def weight_products(pixels, taps, wide, depth, finish):
    def one_row(a, carry):
        rows = pixels[pl.ds(pl.multiple_of(a * wide, 16), 2 * wide), :]
        total = dot_tn(rows, taps[...])
        for b in range(3):
            finish(pl.multiple_of((3 * a + b) * 2 * LANES, LANES), total[:, b * depth : (b + 1) * depth])
        return carry

    lax.fori_loop(0, 3, one_row, 0)


def hidden_rows(odd, hidden, hidden_a, hidden_b):
    above, below = sides(odd, hidden_a[1], hidden_b[1])[0], sides(odd, hidden_a[0], hidden_b[0])[1]
    return (above, hidden[0], hidden[1], below)


def cand_weights_kernel(place, resets, motion, motion_a, motion_b, grads, out, pixels, taps):
    odd = place[0] % 2 == 1
    load_pixels(odd, pixels, [resets[row] for row in range(4)], motion, motion_a, motion_b)
    load_grads(taps, grads)

    def finish(start, value):
        out[pl.ds(start, 2 * LANES)] = value

    weight_products(pixels, taps, motion.shape[1], LANES, finish)


def middle_weights_kernel(place, resets, hidden, hidden_a, hidden_b, motion, motion_a, motion_b, cand_grads, gate_grads,
                          so_far, cand_out, gate_out, pixels, cand_taps, gate_taps):
    odd = place[0] % 2 == 1
    wide = motion.shape[1]
    load_pixels(odd, pixels, [resets[row] for row in range(4)], motion, motion_a, motion_b)
    load_grads(cand_taps, cand_grads)
    load_grads(gate_taps, gate_grads)

    def cand_finish(start, value):
        here = pl.ds(start, 2 * LANES)
        cand_out[here] = so_far[here] + value

    weight_products(pixels, cand_taps, wide, LANES, cand_finish)
    for row, value in enumerate(hidden_rows(odd, hidden, hidden_a, hidden_b)):
        pixels[row * wide : (row + 1) * wide, :LANES] = value

    def gate_finish(start, value):
        here = pl.ds(start, 2 * LANES)
        for half in range(2):
            gate_out[half, here] = value[:, half * LANES : (half + 1) * LANES]

    weight_products(pixels, gate_taps, wide, 2 * LANES, gate_finish)


def last_weights_kernel(place, hidden, hidden_a, hidden_b, motion, motion_a, motion_b, gate_grads, gate_so_far, cand,
                        motion_w, out, pixels, taps):
    odd = place[0] % 2 == 1
    load_pixels(odd, pixels, hidden_rows(odd, hidden, hidden_a, hidden_b), motion, motion_a, motion_b)
    load_grads(taps, gate_grads)
    rows = cand.shape[0]

    def finish(start, value):
        here = pl.ds(start, 2 * LANES)
        for half in range(2):
            there = pl.ds(pl.multiple_of(half * rows + start, LANES), 2 * LANES)
            part = value[:, half * LANES : (half + 1) * LANES] + gate_so_far[half, here]
            out[there] = part.astype(BF16)

    weight_products(pixels, taps, motion.shape[1], 2 * LANES, finish)
    out[2 * rows : 3 * rows] = cand[...].astype(BF16)
    out[3 * rows : 3 * rows + LANES] = motion_w[...].astype(BF16)
    out[3 * rows + LANES :] = jnp.zeros((out.shape[0] - 3 * rows - LANES, LANES), BF16)


def band_back_kernel(place, disparity, offsets, left, right, got_a, got_b, weight, grad_motion, pre, feats,
                     grad_left, back, own, motion_w, window, grad_window):
    odd = place[1] % 2 == 1
    cols = left.shape[1]
    block = cols // 2
    span = 512
    scaling = 1.0 / math.sqrt(left.shape[2])
    position = DISP - lax.broadcasted_iota(jnp.int32, (span, LANES), 0)
    valid = (position >= 0) & (position < DISP)
    inner = slice(HALO, HALO + cols)
    total_w = jnp.zeros((LANES, LANES), F32)
    for row in range(2):
        from_left = sides(odd, got_a[row], got_b[row])[0]
        window[0:DISP] = from_left[HALO : HALO + DISP]
        window[DISP : DISP + cols] = right[row]
        window[DISP + cols :] = jnp.zeros((window.shape[0] - DISP - cols, window.shape[1]), BF16)
        grad_window[...] = jnp.zeros(grad_window.shape, F32)
        value = pre[row, inner]
        gate = jax.nn.sigmoid(value)
        slope = gate * (1.0 + value * (1.0 - gate))
        grad_pre = (grad_motion[row, inner] * slope).astype(BF16)
        total_w = total_w + dot_tn(feats[row, inner], grad_pre)
        grad_feats = dot_nt(grad_pre, weight[...])
        table = lookup_rows(position, valid, disparity, offsets, row)
        for part in range(2):
            here = slice(part * block, (part + 1) * block)
            there = slice(part * block, part * block + span)
            band = split_dot(grad_feats[here], table, dot_nt)
            scores = (pltpu.roll(band, 0, 1, stride=1, stride_axis=0) * scaling).astype(BF16)
            grad_left[row, here] = dot(scores, window[there]).astype(BF16)
            grad_window[there] += dot_tn(scores, left[row, here])
        back[row] = grad_window[0:DISP].astype(BF16)
        own[row] = grad_window[DISP : DISP + cols]
    motion_w[...] = total_w


def pairings(count):
    first = [(2 * k, 2 * k + 1) for k in range(count // 2)]
    second = [(2 * k + 1, 2 * k + 2) for k in range(count // 2 - 1)]
    both = lambda pairs: pairs + [(b, a) for a, b in pairs]
    return both(first), both(second)


def exchanged(value, axis):
    first, second = pairings(lax.axis_size(axis))
    return lax.ppermute(value, axis, first), lax.ppermute(value, axis, second)


def exchanged_pair(value_a, value_b, axis):
    first, second = pairings(lax.axis_size(axis))
    return lax.ppermute(value_a, axis, first), lax.ppermute(value_b, axis, second)


def summed_everywhere(parts, cols_index, axes):
    cols_count = lax.axis_size("cols")
    devices = lax.axis_size("rows") * cols_count
    core = cols_index % 2
    swap = [(i, i ^ 1) for i in range(cols_count)]
    groups = [[i for i in range(devices) if i % 2 == c] for c in range(2)]
    kept = lax.dynamic_index_in_dim(parts, core, 0, keepdims=False)
    given = lax.dynamic_index_in_dim(parts, 1 - core, 0, keepdims=False)
    got = lax.ppermute(given, "cols", swap)
    half = (kept.astype(F32) + got.astype(F32)).astype(BF16)
    pieces = lax.all_to_all(half, axes, 0, 0, tiled=True, axis_index_groups=groups)
    piece = jnp.sum(pieces.astype(F32), axis=0).astype(BF16)
    spread = jnp.broadcast_to(piece[None], pieces.shape)
    half = lax.all_to_all(spread, axes, 0, 0, tiled=True, axis_index_groups=groups)
    other = lax.ppermute(half, "cols", swap)
    first = jnp.where(core == 0, half, other)
    second = jnp.where(core == 0, other, half)
    return jnp.stack([first, second])


def on_device(
    fmap_left,
    fmap_right,
    hidden_init,
    disp_init,
    level_offset,
    motion_weight,
    gate_weight,
    cand_weight,
    grad_hidden,
):
    rows, cols, channels = fmap_left.shape
    wide = cols + 2 * HALO
    state = hidden_init.shape[2]
    feats_count = motion_weight.shape[0]
    rows_axis, cols_axis = lax.axis_size("rows"), lax.axis_size("cols")
    rows_index, cols_index = lax.axis_index("rows"), lax.axis_index("cols")
    place = jnp.stack([rows_index, cols_index]).astype(jnp.int32)
    odd_col = cols_index % 2 == 1

    maps = jnp.concatenate(
        [fmap_right[:, cols - DISP - HALO :], fmap_left[:, cols - HALO :], fmap_left[:, :HALO], fmap_right[:, :HALO]],
        axis=1,
    )
    states = jnp.concatenate(
        [hidden_init[:, cols - HALO :], hidden_init[:, :HALO], grad_hidden[:, cols - HALO :], grad_hidden[:, :HALO]],
        axis=1,
    )
    states_a, states_b = exchanged(states, "cols")
    maps_a, maps_b = exchanged(maps, "cols")
    state_left = jnp.where(odd_col, states_a, states_b)
    state_right = jnp.where(odd_col, states_b, states_a)
    hidden = jnp.concatenate(
        [state_left[:, :HALO], hidden_init, state_right[:, HALO : 2 * HALO]], axis=1
    )
    grads = jnp.concatenate(
        [state_left[:, 2 * HALO : 3 * HALO], grad_hidden, state_right[:, 3 * HALO :]], axis=1
    )
    hidden_a, hidden_b = exchanged(hidden, "rows")

    motion_w = jnp.pad(motion_weight, ((0, LANES - feats_count), (0, 0)))
    gate_wt = jnp.transpose(gate_weight.reshape(3, 3, 2 * state, 2 * state), (0, 1, 3, 2)).reshape(-1, 2 * state)
    cand_wt = jnp.transpose(cand_weight.reshape(3, 3, 2 * state, state), (0, 1, 3, 2)).reshape(-1, 2 * state)

    field = lambda count, dtype: array((count, wide, LANES), dtype)
    band_flops = 2 * rows * wide * 512 * channels
    motion, motion_pre, feats = kernel_call(
        motion_kernel,
        [field(2, BF16), field(2, F32), field(2, BF16)],
        [place, disp_init, level_offset, fmap_left, fmap_right, maps_a, maps_b, motion_w],
        3,
        [pltpu.VMEM((wide, channels), BF16), pltpu.VMEM((768, channels), BF16), pltpu.VMEM((832, channels), BF16)],
        2 * band_flops,
    )
    motion_a, motion_b = exchanged(motion, "rows")
    motions = (motion, motion_a, motion_b)
    unit = 2 * wide * 9 * 2 * state * state
    fields = [pltpu.VMEM((6, wide, 6 * LANES), BF16), pltpu.VMEM((4, wide, 6 * LANES), BF16)]

    hidden_1, update_0, reset_0, reset_hidden_0, candidate_0 = kernel_call(
        lambda *refs: first_kernel(cols_axis, *refs),
        [field(2, BF16), field(4, F32), field(4, F32), field(4, BF16), field(2, F32)],
        [place, hidden, hidden_a, hidden_b, *motions, gate_weight, cand_weight],
        1,
        fields,
        10 * unit,
    )
    hidden_1a, hidden_1b = exchanged(hidden_1, "rows")
    update_1, reset_1, reset_hidden_1, grad_cand_1, grad_update_1, send_a, send_b = kernel_call(
        second_kernel,
        [field(4, F32), field(4, F32), field(4, BF16), field(2, BF16), field(2, BF16), field(3, BF16), field(3, BF16)],
        [place, hidden_1, hidden_1a, hidden_1b, *motions, gate_weight, cand_weight, grads],
        1,
        fields,
        10 * unit,
    )
    got_a, got_b = exchanged_pair(send_a, send_b, "rows")
    pixels = pltpu.VMEM((4 * wide, 2 * LANES), BF16)
    cand_taps = pltpu.VMEM((2 * wide, 3 * LANES), BF16)
    gate_taps = pltpu.VMEM((2 * wide, 6 * LANES), BF16)
    (cand_sum_1,) = kernel_call(
        cand_weights_kernel,
        [array(cand_weight.shape, F32)],
        [place, reset_hidden_1, *motions, grad_cand_1],
        1,
        [pixels, cand_taps],
        2 * unit,
    )
    back_scratch = [
        pltpu.VMEM((6, wide, 3 * LANES), BF16),
        pltpu.VMEM((4, wide, 6 * LANES), BF16),
        pltpu.VMEM((4, wide, LANES), F32),
    ]
    grad_gate_1, grad_state, grad_motion_1, grad_cand_0, grad_update_0, send_a, send_b = kernel_call(
        lambda *refs: later_back_kernel(cols_axis, *refs),
        [array((2, wide, 2 * LANES), BF16), field(2, F32), field(2, F32), field(2, BF16), field(2, BF16),
         field(3, BF16), field(3, BF16)],
        [place, grad_cand_1, got_a, got_b, grad_update_1, hidden_1, hidden_1a, hidden_1b, reset_1, cand_wt, gate_wt,
         update_1, grads, hidden, update_0, candidate_0],
        1,
        back_scratch,
        8 * unit,
    )
    got_a, got_b = exchanged_pair(send_a, send_b, "rows")
    cand_sum, gate_sum_1 = kernel_call(
        middle_weights_kernel,
        [array(cand_weight.shape, F32), array((2,) + cand_weight.shape, F32)],
        [place, reset_hidden_0, hidden_1, hidden_1a, hidden_1b, *motions, grad_cand_0, grad_gate_1, cand_sum_1],
        1,
        [pixels, cand_taps, gate_taps],
        6 * unit,
    )
    grad_gate_0, grad_first, grad_motion = kernel_call(
        first_back_kernel,
        [array((2, wide, 2 * LANES), BF16), field(2, BF16), field(2, F32)],
        [place, grad_cand_0, got_a, got_b, grad_update_0, hidden, hidden_a, hidden_b, reset_0, cand_wt, gate_wt,
         update_0, grad_state, grad_motion_1],
        1,
        back_scratch,
        8 * unit,
    )
    grad_left, back, own, motion_sum = kernel_call(
        band_back_kernel,
        [array((2, cols, channels), BF16), array((2, DISP, channels), BF16), array((2, cols, channels), F32),
         array((LANES, LANES), F32)],
        [place, disp_init, level_offset, fmap_left, fmap_right, maps_a, maps_b, motion_w, grad_motion, motion_pre, feats],
        3,
        [pltpu.VMEM((768, channels), BF16), pltpu.VMEM((768, channels), F32)],
        3 * band_flops,
    )
    back_a, back_b = exchanged(back, "cols")
    devices = rows_axis * cols_axis
    (parts,) = kernel_call(
        last_weights_kernel,
        [array((devices * CHUNK_ROWS, LANES), BF16)],
        [place, hidden, hidden_a, hidden_b, *motions, grad_gate_0, gate_sum_1, cand_sum, motion_sum],
        1,
        [pixels, gate_taps],
        4 * unit,
    )
    sums = summed_everywhere(
        parts.reshape(2, devices // 2, CHUNK_ROWS, LANES), cols_index, ("rows", "cols")
    ).reshape(devices * CHUNK_ROWS, LANES)
    returned = jnp.where(odd_col, back_b, back_a).astype(F32)
    grad_right = jnp.concatenate(
        [own[:, : cols - DISP], own[:, cols - DISP :] + returned], axis=1
    ).astype(BF16)
    normaliser = 1.0 / math.sqrt(rows * rows_axis * cols * cols_axis)
    depth = cand_weight.shape[0]
    scaled = lambda start, count: sums[start : start + count].astype(F32) * normaliser
    return (
        grad_left,
        grad_right,
        grad_first[:, HALO : HALO + cols],
        scaled(3 * depth, feats_count),
        jnp.concatenate([scaled(0, depth), scaled(depth, depth)], axis=1),
        scaled(2 * depth, depth),
    )


def solution(mesh):
    in_specs = (
        P("rows", "cols", None),
        P("rows", "cols", None),
        P("rows", "cols", None),
        P("rows"),
        P("rows", None),
        P(),
        P(),
        P(),
        P("rows", "cols", None),
    )
    out_specs = (
        P("rows", "cols", None),
        P("rows", "cols", None),
        P("rows", "cols", None),
        P(),
        P(),
        P(),
    )
    return jax.shard_map(
        on_device, mesh=mesh, in_specs=in_specs, out_specs=out_specs, check_vma=False
    )
```

```python
import math

import jax
import jax.numpy as jnp
from jax import lax
from jax.experimental import pallas as pl
from jax.experimental.pallas import tpu as pltpu
from jax.sharding import PartitionSpec as P

LEVELS = 4
RADIUS = 4
DISP = 192
TAPS = 2 * RADIUS + 1
HALO = 16
LANES = 128
CHUNK_ROWS = 56

BF16 = jnp.bfloat16
F32 = jnp.float32
VMEM = pl.BlockSpec(memory_space=pltpu.VMEM)
SMEM = pl.BlockSpec(memory_space=pltpu.SMEM)


def dot(a, b):
    return jnp.dot(a, b, preferred_element_type=F32)


def dot_nt(a, b):
    return lax.dot_general(a, b, (((1,), (1,)), ((), ())), preferred_element_type=F32)


def dot_tn(a, b):
    return lax.dot_general(a, b, (((0,), (0,)), ((), ())), preferred_element_type=F32)


def split_dot(a, table, contract):
    high = a.astype(BF16)
    low = (a - high.astype(F32)).astype(BF16)
    return contract(high, table) + contract(low, table)


def kernel_call(body, outs, ins, scalars, scratch, flops):
    bytes_moved = sum(math.prod(x.shape) * x.dtype.itemsize for x in (*ins, *outs))
    held = sum(math.prod(x.shape) * jnp.dtype(x.dtype).itemsize for x in scratch)
    return pl.pallas_call(
        body,
        out_shape=outs,
        in_specs=[SMEM] * scalars + [VMEM] * (len(ins) - scalars),
        out_specs=[VMEM] * len(outs),
        scratch_shapes=scratch,
        compiler_params=pltpu.CompilerParams(vmem_limit_bytes=bytes_moved + held + 4 * 2**20),
        cost_estimate=pl.CostEstimate(flops=flops, bytes_accessed=bytes_moved, transcendentals=0),
    )(*ins)


def array(shape, dtype):
    return jax.ShapeDtypeStruct(shape, dtype)


def lookup_rows(position, valid, disparity, offsets, row):
    count = position.shape[0]
    feature = lax.broadcasted_iota(jnp.int32, (count, LANES), 1)
    table = jnp.zeros((count, LANES), F32)
    for level in range(LEVELS):
        centre = (disparity[row] >> level) + offsets[row, level]
        tap = feature - level * TAPS
        matches = (position >> level) == tap + (centre - RADIUS)
        matches = matches & (tap >= 0) & (tap < TAPS) & valid
        table = jnp.where(matches, 1.0 / 2**level, table)
    return table.astype(BF16)


def sides(odd, first, second):
    return jnp.where(odd, first, second), jnp.where(odd, second, first)


def store_taps(ref, row, lane, step, value, forward):
    wide = value.shape[0]
    left = pltpu.roll(value, 1, 0).astype(BF16)
    right = pltpu.roll(value, wide - 1, 0).astype(BF16)
    taps = (left, value.astype(BF16), right) if forward else (right, value.astype(BF16), left)
    for tap in range(3):
        start = lane + tap * step
        ref[row, :, start : start + LANES] = taps[tap]


def pack_kernel(left, right, hidden, grads, out, sems):
    cols = left.shape[1]
    tail = DISP + HALO
    first, last = pl.ds(0, HALO), pl.ds(cols - HALO, HALO)
    low, high = pl.ds(0, LANES), pl.ds(LANES, LANES)
    every = pl.ds(0, 2 * LANES)
    moves = (
        (right, pl.ds(cols - tail, tail), pl.ds(0, tail), every),
        (left, last, pl.ds(tail, HALO), every),
        (left, first, pl.ds(tail + HALO, HALO), every),
        (right, first, pl.ds(tail + 2 * HALO, HALO), every),
        (hidden, last, pl.ds(tail + 3 * HALO, HALO), low),
        (hidden, first, pl.ds(tail + 3 * HALO, HALO), high),
        (grads, last, pl.ds(tail + 4 * HALO, HALO), low),
        (grads, first, pl.ds(tail + 4 * HALO, HALO), high),
    )
    copies = [
        pltpu.make_async_copy(source.at[:, start], out.at[:, stop, lanes], sems.at[number])
        for number, (source, start, stop, lanes) in enumerate(moves)
    ]
    for copy in copies:
        copy.start()
    for copy in copies:
        copy.wait()


def packed(left, right, hidden, grads):
    rows, cols, channels = left.shape
    count = DISP + 6 * HALO
    return pl.pallas_call(
        pack_kernel,
        out_shape=array((rows, count, channels), BF16),
        in_specs=[pl.BlockSpec(memory_space=pltpu.HBM)] * 4,
        out_specs=VMEM,
        scratch_shapes=[pltpu.SemaphoreType.DMA((8,))],
        compiler_params=pltpu.CompilerParams(vmem_limit_bytes=4 * 2**20),
        cost_estimate=pl.CostEstimate(flops=0, bytes_accessed=4 * rows * count * channels, transcendentals=0),
    )(left, right, hidden, grads)


def unpack_kernel(count, scale, place, half, other, gate, cand, motion):
    core = place[1] % 2
    block = gate.shape[0]
    per_half = half.shape[0] // block
    step = pl.program_id(0)

    def part(number):
        start = pl.multiple_of((number % per_half) * block, block)
        mine = half[pl.ds(start, block)]
        theirs = other[pl.ds(start, block)]
        return jnp.where(number // per_half == core, mine, theirs).astype(F32) * scale

    gate[:, :LANES] = part(step)
    gate[:, LANES:] = part(step + count)
    cand[...] = part(step + 2 * count)
    motion[...] = part(3 * count)[: motion.shape[0]]


def unpacked(place, half, other, depth, feats_count, scale):
    block = 256
    count = depth // block
    whole = lambda i: (0, 0)
    return pl.pallas_call(
        lambda *refs: unpack_kernel(count, scale, *refs),
        grid=(count,),
        out_shape=[array((depth, 2 * LANES), F32), array((depth, LANES), F32), array((feats_count, LANES), F32)],
        in_specs=[SMEM, pl.BlockSpec(half.shape, whole), pl.BlockSpec(half.shape, whole)],
        out_specs=[
            pl.BlockSpec((block, 2 * LANES), lambda i: (i, 0)),
            pl.BlockSpec((block, LANES), lambda i: (i, 0)),
            pl.BlockSpec((feats_count, LANES), whole),
        ],
        compiler_params=pltpu.CompilerParams(vmem_limit_bytes=12 * 2**20),
        cost_estimate=pl.CostEstimate(flops=0, bytes_accessed=6 * depth * 384, transcendentals=0),
    )(place, half, other)


def motion_kernel(place, disparity, offsets, left, right, got_a, got_b, weight, motion, pre, feats, ext, window, flipped):
    odd = place[1] % 2 == 1
    cols = left.shape[1]
    wide = cols + 2 * HALO
    block = wide // 2
    span = 512
    tail = DISP + HALO
    flat = (lax.broadcasted_iota(jnp.int32, (LANES, LANES), 0)
            + lax.broadcasted_iota(jnp.int32, (LANES, LANES), 1))
    mirror = jnp.where(flat == LANES - 1, 1.0, 0.0).astype(BF16)
    total = window.shape[0]
    position = lax.broadcasted_iota(jnp.int32, (span, LANES), 0) - (block - 1)
    valid = (position >= 0) & (position < DISP)
    for row in range(2):
        from_left, from_right = sides(odd, got_a[row], got_b[row])
        ext[0:HALO] = from_left[tail : tail + HALO]
        ext[HALO : HALO + cols] = left[row]
        ext[HALO + cols : wide] = from_right[tail + HALO : tail + 2 * HALO]
        window[0:tail] = from_left[0:tail]
        window[tail : tail + cols] = right[row]
        window[tail + cols : tail + cols + HALO] = from_right[tail + 2 * HALO : tail + 3 * HALO]
        window[tail + cols + HALO :] = jnp.zeros((total - tail - cols - HALO, window.shape[1]), BF16)
        parts = total // LANES
        for part in range(parts):
            source = window[(parts - 1 - part) * LANES : (parts - part) * LANES]
            flipped[part * LANES : (part + 1) * LANES] = dot(mirror, source).astype(BF16)
        flipped[total:] = jnp.zeros((flipped.shape[0] - total, window.shape[1]), BF16)
        table = lookup_rows(position, valid, disparity, offsets, row)
        for part in range(2):
            start = part * block
            base = total - DISP - start - block
            scores = dot_nt(ext[start : start + block], flipped[base : base + span])
            scores = scores * (1.0 / math.sqrt(left.shape[2]))
            band = pltpu.roll(scores, 0, 1, stride=1, stride_axis=0)
            found = split_dot(band, table, dot).astype(BF16)
            value = dot(found, weight[...])
            feats[row, start : start + block] = found
            pre[row, start : start + block] = value
            motion[row, start : start + block] = (value * jax.nn.sigmoid(value)).astype(BF16)


def image_columns(place, wide, cols, cols_axis):
    column = lax.broadcasted_iota(jnp.int32, (wide, LANES), 0) - HALO + place[1] * cols
    return (column >= 0) & (column < cols * cols_axis)


def fill_rows(store, odd, own, first, second):
    for row in range(2):
        above, below = sides(odd, first[row], second[row])
        store(row, above.astype(F32))
        store(4 + row, below.astype(F32))
        store(2 + row, own[row].astype(F32))


def gates(fields, resets, gate_w, update, reset, reset_hidden, wide):
    block = wide // 2
    deep = gate_w.shape[0] // 3

    def gate_part(step, carry):
        row, start = step // 2, pl.multiple_of((step % 2) * block, 16)
        here = pl.ds(start, block)
        total = sum(dot(fields[row + a, here], gate_w[a * deep : (a + 1) * deep]) for a in range(3))
        reset_part = jax.nn.sigmoid(total[:, LANES:])
        update[row, here] = jax.nn.sigmoid(total[:, :LANES])
        reset[row, here] = reset_part
        hidden = fields[row + 1, here, 2 * LANES : 3 * LANES].astype(F32)
        reset_hidden[row, here] = (reset_part * hidden).astype(BF16)
        return carry

    lax.fori_loop(0, 8, gate_part, 0)
    for row in range(4):
        store_taps(resets, row, 0, 2 * LANES, reset_hidden[row].astype(F32), True)
        for tap in range(3):
            start = (2 * tap + 1) * LANES
            resets[row, :, start : start + LANES] = fields[row + 1, :, start : start + LANES]


def load_fields(odd, fields, hidden, hidden_a, hidden_b, motion, motion_a, motion_b):
    fill_rows(lambda r, v: store_taps(fields, r, 0, 2 * LANES, v, True), odd, hidden, hidden_a, hidden_b)
    fill_rows(lambda r, v: store_taps(fields, r, LANES, 2 * LANES, v, True), odd, motion, motion_a, motion_b)


def candidate_part(resets, cand_w, row, here):
    deep = cand_w.shape[0] // 3
    total = sum(dot(resets[row + a, here], cand_w[a * deep : (a + 1) * deep]) for a in range(3))
    return jnp.tanh(total)


def first_kernel(cols_axis, place, hidden, hidden_a, hidden_b, motion, motion_a, motion_b, gate_w, cand_w,
                 later, update, reset, reset_hidden, candidate, fields, resets):
    odd = place[0] % 2 == 1
    wide = hidden.shape[1]
    block = wide // 2
    load_fields(odd, fields, hidden, hidden_a, hidden_b, motion, motion_a, motion_b)
    gates(fields, resets, gate_w, update, reset, reset_hidden, wide)
    inside = image_columns(place, wide, wide - 2 * HALO, cols_axis)
    for row in range(2):
        for start in (0, block):
            here = pl.ds(start, block)
            new = candidate_part(resets, cand_w, row, here)
            candidate[row, here] = new
            gate = update[row + 1, here]
            old = hidden[row, here].astype(F32)
            value = (1.0 - gate) * old + gate * new
            later[row, here] = jnp.where(inside[start : start + block], value, 0.0).astype(BF16)


def gradients_out(odd, grad, gate, new, old, row, here, grad_cand, grad_update, send_a, send_b):
    cand_part = (grad * gate * (1.0 - new * new)).astype(BF16)
    update_part = (grad * (new - old) * gate * (1.0 - gate)).astype(BF16)
    grad_cand[row, here] = cand_part
    grad_update[row, here] = update_part
    send_a[row, here] = cand_part
    send_b[row, here] = cand_part

    @pl.when(odd == (row == 0))
    def _():
        send_a[2, here] = update_part

    @pl.when(odd == (row == 1))
    def _():
        send_b[2, here] = update_part


def second_kernel(place, hidden, hidden_a, hidden_b, motion, motion_a, motion_b, gate_w, cand_w, grad_hidden,
                  update, reset, reset_hidden, grad_cand, grad_update, send_a, send_b, fields, resets):
    odd = place[0] % 2 == 1
    wide = hidden.shape[1]
    block = wide // 2
    load_fields(odd, fields, hidden, hidden_a, hidden_b, motion, motion_a, motion_b)
    gates(fields, resets, gate_w, update, reset, reset_hidden, wide)
    for row in range(2):
        for start in (0, block):
            here = pl.ds(start, block)
            new = candidate_part(resets, cand_w, row, here)
            gradients_out(odd, grad_hidden[row, here].astype(F32), update[row + 1, here], new,
                          hidden[row, here].astype(F32), row, here, grad_cand, grad_update, send_a, send_b)


def back_step(place, grad_cand, grad_a, grad_b, grad_update, hidden, hidden_a, hidden_b, reset, cand_wt, gate_wt,
              grad_reset, cand_taps, gate_taps, inner, grad_motion, finish):
    odd = place[0] % 2 == 1
    wide = hidden.shape[1]
    block = wide // 2
    fill_rows(lambda r, v: store_taps(cand_taps, r, 0, LANES, v, False), odd, grad_cand, grad_a, grad_b)
    deep = cand_wt.shape[0] // 3
    deeper = gate_wt.shape[0] // 3

    def cand_back(step, carry):
        row, start = step // 2, pl.multiple_of((step % 2) * block, 16)
        here = pl.ds(start, block)
        total = sum(dot(cand_taps[row + 2 - a, here], cand_wt[a * deep : (a + 1) * deep]) for a in range(3))
        inner[row, here] = total[:, :LANES]

        @pl.when((row == 1) | (row == 2))
        def _():
            grad_motion[row - 1, here] = total[:, LANES:]

        return carry

    lax.fori_loop(0, 8, cand_back, 0)
    above_h, below_h = sides(odd, hidden_a[1], hidden_b[1])[0], sides(odd, hidden_a[0], hidden_b[0])[1]
    above_u, below_u = sides(odd, grad_a[2], grad_b[2])
    hiddens = (above_h, hidden[0], hidden[1], below_h)
    updates = (above_u, grad_update[0], grad_update[1], below_u)
    for row in range(4):
        gate = reset[row]
        value = (inner[row] * hiddens[row].astype(F32) * gate * (1.0 - gate)).astype(BF16)
        store_taps(gate_taps, row, 0, 2 * LANES, updates[row].astype(F32), False)
        store_taps(gate_taps, row, LANES, 2 * LANES, value.astype(F32), False)
        if row in (1, 2):
            grad_reset[row - 1] = value
    for row in range(2):
        for start in (0, block):
            here = pl.ds(start, block)
            total = sum(
                dot(gate_taps[row + 2 - a, here], gate_wt[a * deeper : (a + 1) * deeper]) for a in range(3)
            )
            grad_motion[row, here] += total[:, LANES:]
            finish(row, start, here, inner[row + 1, here] * reset[row + 1, here] + total[:, :LANES])


def later_back_kernel(cols_axis, place, grad_cand, grad_a, grad_b, grad_update, hidden, hidden_a, hidden_b, reset,
                      cand_wt, gate_wt, update, grad_hidden, older_hidden, older_update, older_candidate,
                      grad_reset, grad_state, grad_motion, older_cand, older_upd, send_a, send_b,
                      cand_taps, gate_taps, inner):
    odd = place[0] % 2 == 1
    wide = hidden.shape[1]
    block = wide // 2
    inside = image_columns(place, wide, wide - 2 * HALO, cols_axis)

    def finish(row, start, here, terms):
        gate = update[row + 1, here]
        grad = grad_hidden[row, here].astype(F32) * (1.0 - gate) + terms
        grad = jnp.where(inside[start : start + block], grad, 0.0)
        grad_state[row, here] = grad
        gradients_out(odd, grad, older_update[row + 1, here], older_candidate[row, here],
                      older_hidden[row, here].astype(F32), row, here, older_cand, older_upd, send_a, send_b)

    back_step(place, grad_cand, grad_a, grad_b, grad_update, hidden, hidden_a, hidden_b, reset, cand_wt, gate_wt,
              grad_reset, cand_taps, gate_taps, inner, grad_motion, finish)


def first_back_kernel(place, grad_cand, grad_a, grad_b, grad_update, hidden, hidden_a, hidden_b, reset,
                      cand_wt, gate_wt, update, grad_state, motion_so_far,
                      grad_reset, grad_first, grad_motion, cand_taps, gate_taps, inner):
    def finish(row, start, here, terms):
        gate = update[row + 1, here]
        grad = grad_state[row, here] * (1.0 - gate) + terms
        skip = HALO if start == 0 else 0
        count = grad.shape[0] - HALO
        grad_first[row, (start + skip) - HALO : (start + skip) - HALO + count] = grad[skip : skip + count].astype(BF16)
        grad_motion[row, here] += motion_so_far[row, here]

    back_step(place, grad_cand, grad_a, grad_b, grad_update, hidden, hidden_a, hidden_b, reset, cand_wt, gate_wt,
              grad_reset, cand_taps, gate_taps, inner, grad_motion, finish)


def load_pixels(odd, pixels, hiddens, motion, motion_a, motion_b):
    wide = motion.shape[1]
    above, below = sides(odd, motion_a[1], motion_b[1])[0], sides(odd, motion_a[0], motion_b[0])[1]
    for row, value in enumerate((above, motion[0], motion[1], below)):
        pixels[row * wide : (row + 1) * wide, LANES:] = value
    for row, value in enumerate(hiddens):
        pixels[row * wide : (row + 1) * wide, :LANES] = value


def load_grads(taps, grads):
    wide = grads.shape[1]
    column = lax.broadcasted_iota(jnp.int32, (wide, LANES), 0)
    own = (column >= HALO) & (column < wide - HALO)
    depth = grads.shape[2]
    for row in range(2):
        for part in range(depth // LANES):
            value = jnp.where(own, grads[row, :, part * LANES : (part + 1) * LANES].astype(F32), 0.0)
            shifted = (pltpu.roll(value, wide - 1, 0), value, pltpu.roll(value, 1, 0))
            for tap in range(3):
                start = tap * depth + part * LANES
                taps[row * wide : (row + 1) * wide, start : start + LANES] = shifted[tap].astype(BF16)


def weight_products(pixels, taps, wide, depth, finish):
    def one_row(a, carry):
        rows = pixels[pl.ds(pl.multiple_of(a * wide, 16), 2 * wide), :]
        total = dot_tn(rows, taps[...])
        for b in range(3):
            finish(pl.multiple_of((3 * a + b) * 2 * LANES, LANES), total[:, b * depth : (b + 1) * depth])
        return carry

    lax.fori_loop(0, 3, one_row, 0)


def hidden_rows(odd, hidden, hidden_a, hidden_b):
    above, below = sides(odd, hidden_a[1], hidden_b[1])[0], sides(odd, hidden_a[0], hidden_b[0])[1]
    return (above, hidden[0], hidden[1], below)


def load_hidden(pixels, rows, wide):
    for row, value in enumerate(rows):
        pixels[row * wide : (row + 1) * wide, :LANES] = value


def second_weights_kernel(place, resets, hidden, hidden_a, hidden_b, motion, motion_a, motion_b, cand_grads, update_grads,
                          cand_out, update_out, pixels, taps):
    odd = place[0] % 2 == 1
    wide = motion.shape[1]
    load_pixels(odd, pixels, [resets[row] for row in range(4)], motion, motion_a, motion_b)
    load_grads(taps, cand_grads)

    def cand_finish(start, value):
        cand_out[pl.ds(start, 2 * LANES)] = value

    def update_finish(start, value):
        update_out[pl.ds(start, 2 * LANES)] = value

    weight_products(pixels, taps, wide, LANES, cand_finish)
    load_hidden(pixels, hidden_rows(odd, hidden, hidden_a, hidden_b), wide)
    load_grads(taps, update_grads)
    weight_products(pixels, taps, wide, LANES, update_finish)


def first_weights_kernel(place, resets, older, older_a, older_b, hidden, hidden_a, hidden_b, motion, motion_a, motion_b,
                         cand_grads, update_grads, reset_grads, cand_sum, update_sum,
                         cand_out, update_out, reset_out, pixels, taps):
    odd = place[0] % 2 == 1
    wide = motion.shape[1]
    load_pixels(odd, pixels, [resets[row] for row in range(4)], motion, motion_a, motion_b)
    load_grads(taps, cand_grads)

    def cand_finish(start, value):
        here = pl.ds(start, 2 * LANES)
        cand_out[here] = cand_sum[here] + value

    def update_finish(start, value):
        here = pl.ds(start, 2 * LANES)
        update_out[here] = update_sum[here] + value

    def reset_finish(start, value):
        reset_out[pl.ds(start, 2 * LANES)] = value

    weight_products(pixels, taps, wide, LANES, cand_finish)
    load_hidden(pixels, hidden_rows(odd, older, older_a, older_b), wide)
    load_grads(taps, update_grads)
    weight_products(pixels, taps, wide, LANES, update_finish)
    load_hidden(pixels, hidden_rows(odd, hidden, hidden_a, hidden_b), wide)
    load_grads(taps, reset_grads)
    weight_products(pixels, taps, wide, LANES, reset_finish)


def last_weights_kernel(place, hidden, hidden_a, hidden_b, motion, motion_a, motion_b, reset_grads, reset_sum,
                        update_sum, cand_sum, motion_w, kept, given, pixels, taps, parts):
    odd = place[0] % 2 == 1
    load_pixels(odd, pixels, hidden_rows(odd, hidden, hidden_a, hidden_b), motion, motion_a, motion_b)
    load_grads(taps, reset_grads)
    rows = cand_sum.shape[0]

    def finish(start, value):
        there = pl.ds(pl.multiple_of(rows + start, LANES), 2 * LANES)
        parts[there] = (value + reset_sum[pl.ds(start, 2 * LANES)]).astype(BF16)

    weight_products(pixels, taps, motion.shape[1], LANES, finish)
    parts[0:rows] = update_sum[...].astype(BF16)
    parts[2 * rows : 3 * rows] = cand_sum[...].astype(BF16)
    parts[3 * rows : 3 * rows + LANES] = motion_w[...].astype(BF16)
    parts[3 * rows + LANES :] = jnp.zeros((parts.shape[0] - 3 * rows - LANES, LANES), BF16)
    half = parts.shape[0] // 2
    core = place[1] % 2
    kept[...] = parts[pl.ds(pl.multiple_of(core * half, LANES), half)]
    given[...] = parts[pl.ds(pl.multiple_of((1 - core) * half, LANES), half)]


def right_kernel(place, own, back_a, back_b, grad_right):
    odd = place[1] % 2 == 1
    split = own.shape[1] - DISP
    for row in range(2):
        grad_right[row, :split] = own[row, :split].astype(BF16)
        returned = sides(odd, back_a[row], back_b[row])[1].astype(F32)
        grad_right[row, split:] = (own[row, split:] + returned).astype(BF16)


def band_back_kernel(place, disparity, offsets, left, right, got_a, got_b, weight, grad_motion, pre, feats,
                     grad_left, back, own, motion_w, window, grad_window):
    odd = place[1] % 2 == 1
    cols = left.shape[1]
    block = cols // 2
    span = 512
    scaling = 1.0 / math.sqrt(left.shape[2])
    position = DISP - lax.broadcasted_iota(jnp.int32, (span, LANES), 0)
    valid = (position >= 0) & (position < DISP)
    inner = slice(HALO, HALO + cols)
    total_w = jnp.zeros((LANES, LANES), F32)
    for row in range(2):
        from_left = sides(odd, got_a[row], got_b[row])[0]
        window[0:DISP] = from_left[HALO : HALO + DISP]
        window[DISP : DISP + cols] = right[row]
        window[DISP + cols :] = jnp.zeros((window.shape[0] - DISP - cols, window.shape[1]), BF16)
        grad_window[...] = jnp.zeros(grad_window.shape, F32)
        value = pre[row, inner]
        gate = jax.nn.sigmoid(value)
        slope = gate * (1.0 + value * (1.0 - gate))
        grad_pre = (grad_motion[row, inner] * slope).astype(BF16)
        total_w = total_w + dot_tn(feats[row, inner], grad_pre)
        grad_feats = dot_nt(grad_pre, weight[...])
        table = lookup_rows(position, valid, disparity, offsets, row)
        for part in range(2):
            here = slice(part * block, (part + 1) * block)
            there = slice(part * block, part * block + span)
            band = split_dot(grad_feats[here], table, dot_nt)
            scores = (pltpu.roll(band, 0, 1, stride=1, stride_axis=0) * scaling).astype(BF16)
            grad_left[row, here] = dot(scores, window[there]).astype(BF16)
            grad_window[there] += dot_tn(scores, left[row, here])
        back[row] = grad_window[0:DISP].astype(BF16)
        own[row] = grad_window[DISP : DISP + cols]
    motion_w[...] = total_w


def pairings(count):
    first = [(2 * k, 2 * k + 1) for k in range(count // 2)]
    second = [(2 * k + 1, 2 * k + 2) for k in range(count // 2 - 1)]
    both = lambda pairs: pairs + [(b, a) for a, b in pairs]
    return both(first), both(second)


def exchanged(value, axis):
    first, second = pairings(lax.axis_size(axis))
    return lax.ppermute(value, axis, first), lax.ppermute(value, axis, second)


def exchanged_pair(value_a, value_b, axis):
    first, second = pairings(lax.axis_size(axis))
    return lax.ppermute(value_a, axis, first), lax.ppermute(value_b, axis, second)


def summed_everywhere(kept, given, axes, meanwhile):
    cols_count = lax.axis_size("cols")
    devices = lax.axis_size("rows") * cols_count
    swap = [(i, i ^ 1) for i in range(cols_count)]
    groups = [[i for i in range(devices) if i % 2 == c] for c in range(2)]
    got = lax.ppermute(given, "cols", swap)
    got, meanwhile = lax.optimization_barrier((got, meanwhile))
    half = (kept.astype(F32) + got.astype(F32)).astype(BF16).reshape(devices // 2, -1, LANES)
    pieces = lax.all_to_all(half, axes, 0, 0, tiled=True, axis_index_groups=groups)
    piece = jnp.sum(pieces.astype(F32), axis=0).astype(BF16)
    spread = jnp.broadcast_to(piece[None], pieces.shape)
    half = lax.all_to_all(spread, axes, 0, 0, tiled=True, axis_index_groups=groups)
    other = lax.ppermute(half, "cols", swap)
    return half.reshape(-1, LANES), other.reshape(-1, LANES), meanwhile


def on_device(
    fmap_left,
    fmap_right,
    hidden_init,
    disp_init,
    level_offset,
    motion_weight,
    gate_weight,
    cand_weight,
    grad_hidden,
):
    rows, cols, channels = fmap_left.shape
    wide = cols + 2 * HALO
    state = hidden_init.shape[2]
    feats_count = motion_weight.shape[0]
    rows_axis, cols_axis = lax.axis_size("rows"), lax.axis_size("cols")
    rows_index, cols_index = lax.axis_index("rows"), lax.axis_index("cols")
    place = jnp.stack([rows_index, cols_index]).astype(jnp.int32)
    odd_col = cols_index % 2 == 1

    halos = packed(fmap_left, fmap_right, hidden_init, grad_hidden)
    maps_a, maps_b = exchanged(halos, "cols")
    init_a, init_b = exchanged(hidden_init, "rows")
    base = DISP + 4 * HALO
    from_left = jnp.where(odd_col, maps_a[:, base:], maps_b[:, base:])
    from_right = jnp.where(odd_col, maps_b[:, base:], maps_a[:, base:])
    edges = jnp.concatenate([from_left[:, :HALO, :state], from_right[:, :HALO, state:]], axis=1)
    hidden = jnp.concatenate([edges[:, :HALO], hidden_init, edges[:, HALO:]], axis=1)
    grads = jnp.concatenate([from_left[:, HALO:, :state], grad_hidden, from_right[:, HALO:, state:]], axis=1)

    motion_w = jnp.pad(motion_weight, ((0, LANES - feats_count), (0, 0)))
    gate_wt = jnp.transpose(gate_weight.reshape(3, 3, 2 * state, 2 * state), (0, 1, 3, 2)).reshape(-1, 2 * state)
    cand_wt = jnp.transpose(cand_weight.reshape(3, 3, 2 * state, state), (0, 1, 3, 2)).reshape(-1, 2 * state)
    motion_w, gate_wt, cand_wt, init_a, init_b, edges, hidden, grads = lax.optimization_barrier(
        (motion_w, gate_wt, cand_wt, init_a, init_b, edges, hidden, grads)
    )

    field = lambda count, dtype: array((count, wide, LANES), dtype)
    band_flops = 2 * rows * wide * 512 * channels
    motion, motion_pre, feats = kernel_call(
        motion_kernel,
        [field(2, BF16), field(2, F32), field(2, BF16)],
        [place, disp_init, level_offset, fmap_left, fmap_right, maps_a, maps_b, motion_w],
        3,
        [pltpu.VMEM((wide, channels), BF16), pltpu.VMEM((768, channels), BF16), pltpu.VMEM((832, channels), BF16)],
        2 * band_flops,
    )
    sent = jnp.concatenate([motion, edges], axis=1)
    sent_a, sent_b = exchanged(sent, "rows")
    motion_a, motion_b = sent_a[:, :wide], sent_b[:, :wide]
    with_edges = lambda inner, got: jnp.concatenate(
        [got[:, wide : wide + HALO], inner, got[:, wide + HALO :]], axis=1
    )
    hidden_a, hidden_b = with_edges(init_a, sent_a), with_edges(init_b, sent_b)
    motions = (motion, motion_a, motion_b)
    unit = 2 * wide * 9 * 2 * state * state
    fields = [pltpu.VMEM((6, wide, 6 * LANES), BF16), pltpu.VMEM((4, wide, 6 * LANES), BF16)]

    hidden_1, update_0, reset_0, reset_hidden_0, candidate_0 = kernel_call(
        lambda *refs: first_kernel(cols_axis, *refs),
        [field(2, BF16), field(4, F32), field(4, F32), field(4, BF16), field(2, F32)],
        [place, hidden, hidden_a, hidden_b, *motions, gate_weight, cand_weight],
        1,
        fields,
        10 * unit,
    )
    hidden_1a, hidden_1b = exchanged(hidden_1, "rows")
    update_1, reset_1, reset_hidden_1, grad_cand_1, grad_update_1, send_a, send_b = kernel_call(
        second_kernel,
        [field(4, F32), field(4, F32), field(4, BF16), field(2, BF16), field(2, BF16), field(3, BF16), field(3, BF16)],
        [place, hidden_1, hidden_1a, hidden_1b, *motions, gate_weight, cand_weight, grads],
        1,
        fields,
        10 * unit,
    )
    got_a, got_b = exchanged_pair(send_a, send_b, "rows")
    pixels = pltpu.VMEM((4 * wide, 2 * LANES), BF16)
    taps = pltpu.VMEM((2 * wide, 3 * LANES), BF16)
    weights = array(cand_weight.shape, F32)
    cand_sum, update_sum = kernel_call(
        second_weights_kernel,
        [weights, weights],
        [place, reset_hidden_1, hidden_1, hidden_1a, hidden_1b, *motions, grad_cand_1, grad_update_1],
        1,
        [pixels, taps],
        4 * unit,
    )
    got_a, got_b, cand_sum, update_sum = lax.optimization_barrier((got_a, got_b, cand_sum, update_sum))
    back_scratch = [
        pltpu.VMEM((6, wide, 3 * LANES), BF16),
        pltpu.VMEM((4, wide, 6 * LANES), BF16),
        pltpu.VMEM((4, wide, LANES), F32),
    ]
    grad_reset_1, grad_state, grad_motion_1, grad_cand_0, grad_update_0, send_a, send_b = kernel_call(
        lambda *refs: later_back_kernel(cols_axis, *refs),
        [field(2, BF16), field(2, F32), field(2, F32), field(2, BF16), field(2, BF16),
         field(3, BF16), field(3, BF16)],
        [place, grad_cand_1, got_a, got_b, grad_update_1, hidden_1, hidden_1a, hidden_1b, reset_1, cand_wt, gate_wt,
         update_1, grads, hidden, update_0, candidate_0],
        1,
        back_scratch,
        8 * unit,
    )
    got_a, got_b = exchanged_pair(send_a, send_b, "rows")
    cand_sum, update_sum, reset_sum = kernel_call(
        first_weights_kernel,
        [weights, weights, weights],
        [place, reset_hidden_0, hidden, hidden_a, hidden_b, hidden_1, hidden_1a, hidden_1b, *motions,
         grad_cand_0, grad_update_0, grad_reset_1, cand_sum, update_sum],
        1,
        [pixels, taps],
        6 * unit,
    )
    got_a, got_b, cand_sum, update_sum, reset_sum = lax.optimization_barrier(
        (got_a, got_b, cand_sum, update_sum, reset_sum)
    )
    grad_reset_0, grad_first, grad_motion = kernel_call(
        first_back_kernel,
        [field(2, BF16), array((2, cols, LANES), BF16), field(2, F32)],
        [place, grad_cand_0, got_a, got_b, grad_update_0, hidden, hidden_a, hidden_b, reset_0, cand_wt, gate_wt,
         update_0, grad_state, grad_motion_1],
        1,
        back_scratch,
        8 * unit,
    )
    grad_left, back, own, motion_sum = kernel_call(
        band_back_kernel,
        [array((2, cols, channels), BF16), array((2, DISP, channels), BF16), array((2, cols, channels), F32),
         array((LANES, LANES), F32)],
        [place, disp_init, level_offset, fmap_left, fmap_right, maps_a, maps_b, motion_w, grad_motion, motion_pre, feats],
        3,
        [pltpu.VMEM((768, channels), BF16), pltpu.VMEM((768, channels), F32)],
        3 * band_flops,
    )
    back_a, back_b = exchanged(back, "cols")
    devices = rows_axis * cols_axis
    total = devices * CHUNK_ROWS
    kept, given = kernel_call(
        last_weights_kernel,
        [array((total // 2, LANES), BF16), array((total // 2, LANES), BF16)],
        [place, hidden, hidden_a, hidden_b, *motions, grad_reset_0, reset_sum, update_sum, cand_sum, motion_sum],
        1,
        [pixels, taps, pltpu.VMEM((total, LANES), BF16)],
        2 * unit,
    )
    (grad_right,) = kernel_call(
        right_kernel, [array((2, cols, channels), BF16)], [place, own, back_a, back_b], 1, [], 0
    )
    half, other, (grad_left, grad_right, grad_first) = summed_everywhere(
        kept, given, ("rows", "cols"), (grad_left, grad_right, grad_first)
    )
    normaliser = 1.0 / math.sqrt(rows * rows_axis * cols * cols_axis)
    grad_gate_w, grad_cand_w, grad_motion_w = unpacked(
        place, half, other, cand_weight.shape[0], feats_count, normaliser
    )
    return (grad_left, grad_right, grad_first, grad_motion_w, grad_gate_w, grad_cand_w)


def solution(mesh):
    in_specs = (
        P("rows", "cols", None),
        P("rows", "cols", None),
        P("rows", "cols", None),
        P("rows"),
        P("rows", None),
        P(),
        P(),
        P(),
        P("rows", "cols", None),
    )
    out_specs = (
        P("rows", "cols", None),
        P("rows", "cols", None),
        P("rows", "cols", None),
        P(),
        P(),
        P(),
    )
    return jax.shard_map(
        on_device, mesh=mesh, in_specs=in_specs, out_specs=out_specs, check_vma=False
    )
```

```python
import math

import jax
import jax.numpy as jnp
from jax import lax
from jax.experimental import pallas as pl
from jax.experimental.pallas import tpu as pltpu
from jax.sharding import PartitionSpec as P

LEVELS = 4
RADIUS = 4
DISP = 192
TAPS = 2 * RADIUS + 1
HALO = 16
LANES = 128
SPLIT = 2
CHUNK_ROWS = 56

BF16 = jnp.bfloat16
F32 = jnp.float32
VMEM = pl.BlockSpec(memory_space=pltpu.VMEM)
SMEM = pl.BlockSpec(memory_space=pltpu.SMEM)


def dot(a, b):
    return jnp.dot(a, b, preferred_element_type=F32)


def dot_nt(a, b):
    return lax.dot_general(a, b, (((1,), (1,)), ((), ())), preferred_element_type=F32)


def dot_tn(a, b):
    return lax.dot_general(a, b, (((0,), (0,)), ((), ())), preferred_element_type=F32)


def split_dot(a, table, contract):
    high = a.astype(BF16)
    low = (a - high.astype(F32)).astype(BF16)
    return contract(high, table) + contract(low, table)


def kernel_call(body, outs, ins, scalars, scratch, flops):
    bytes_moved = sum(math.prod(x.shape) * x.dtype.itemsize for x in (*ins, *outs))
    held = sum(math.prod(x.shape) * jnp.dtype(x.dtype).itemsize for x in scratch)
    return pl.pallas_call(
        body,
        out_shape=outs,
        in_specs=[SMEM] * scalars + [VMEM] * (len(ins) - scalars),
        out_specs=[VMEM] * len(outs),
        scratch_shapes=scratch,
        compiler_params=pltpu.CompilerParams(vmem_limit_bytes=bytes_moved + held + 4 * 2**20),
        cost_estimate=pl.CostEstimate(flops=flops, bytes_accessed=bytes_moved, transcendentals=0),
    )(*ins)


def array(shape, dtype):
    return jax.ShapeDtypeStruct(shape, dtype)


def lookup_rows(position, valid, disparity, offsets, row):
    count = position.shape[0]
    feature = lax.broadcasted_iota(jnp.int32, (count, LANES), 1)
    table = jnp.zeros((count, LANES), F32)
    for level in range(LEVELS):
        centre = (disparity[row] >> level) + offsets[row, level]
        tap = feature - level * TAPS
        matches = (position >> level) == tap + (centre - RADIUS)
        matches = matches & (tap >= 0) & (tap < TAPS) & valid
        table = jnp.where(matches, 1.0 / 2**level, table)
    return table.astype(BF16)


def sides(odd, first, second):
    return jnp.where(odd, first, second), jnp.where(odd, second, first)


def store_taps(ref, row, lane, step, value, forward):
    wide = value.shape[0]
    left = pltpu.roll(value, 1, 0).astype(BF16)
    right = pltpu.roll(value, wide - 1, 0).astype(BF16)
    taps = (left, value.astype(BF16), right) if forward else (right, value.astype(BF16), left)
    for tap in range(3):
        start = lane + tap * step
        ref[row, :, start : start + LANES] = taps[tap]


def pack_kernel(left, right, hidden, grads, out, sems):
    cols = left.shape[1]
    tail = DISP + HALO
    first, last = pl.ds(0, HALO), pl.ds(cols - HALO, HALO)
    low, high = pl.ds(0, LANES), pl.ds(LANES, LANES)
    every = pl.ds(0, 2 * LANES)
    moves = (
        (right, pl.ds(cols - tail, tail), pl.ds(0, tail), every),
        (left, last, pl.ds(tail, HALO), every),
        (left, first, pl.ds(tail + HALO, HALO), every),
        (right, first, pl.ds(tail + 2 * HALO, HALO), every),
        (hidden, last, pl.ds(tail + 3 * HALO, HALO), low),
        (hidden, first, pl.ds(tail + 3 * HALO, HALO), high),
        (grads, last, pl.ds(tail + 4 * HALO, HALO), low),
        (grads, first, pl.ds(tail + 4 * HALO, HALO), high),
    )
    copies = [
        pltpu.make_async_copy(source.at[:, start], out.at[:, stop, lanes], sems.at[number])
        for number, (source, start, stop, lanes) in enumerate(moves)
    ]
    for copy in copies:
        copy.start()
    for copy in copies:
        copy.wait()


def packed(left, right, hidden, grads):
    rows, cols, channels = left.shape
    count = DISP + 6 * HALO
    return pl.pallas_call(
        pack_kernel,
        out_shape=array((rows, count, channels), BF16),
        in_specs=[pl.BlockSpec(memory_space=pltpu.HBM)] * 4,
        out_specs=VMEM,
        scratch_shapes=[pltpu.SemaphoreType.DMA((8,))],
        compiler_params=pltpu.CompilerParams(vmem_limit_bytes=56 * 2**20),
        cost_estimate=pl.CostEstimate(flops=0, bytes_accessed=4 * rows * count * channels, transcendentals=0),
    )(left, right, hidden, grads)


def unpack_kernel(count, scale, place, half, other, gate, cand, motion):
    core = place[1] % 2
    block = gate.shape[0]
    per_half = half.shape[0] // block
    step = pl.program_id(0)

    def part(number):
        start = pl.multiple_of((number % per_half) * block, block)
        mine = half[pl.ds(start, block)]
        theirs = other[pl.ds(start, block)]
        return jnp.where(number // per_half == core, mine, theirs).astype(F32) * scale

    gate[:, :LANES] = part(step)
    gate[:, LANES:] = part(step + count)
    cand[...] = part(step + 2 * count)
    motion[...] = part(3 * count)[: motion.shape[0]]


def unpacked(place, half, other, depth, feats_count, scale):
    block = 256
    count = depth // block
    whole = lambda i: (0, 0)
    return pl.pallas_call(
        lambda *refs: unpack_kernel(count, scale, *refs),
        grid=(count,),
        out_shape=[array((depth, 2 * LANES), F32), array((depth, LANES), F32), array((feats_count, LANES), F32)],
        in_specs=[SMEM, pl.BlockSpec(half.shape, whole), pl.BlockSpec(half.shape, whole)],
        out_specs=[
            pl.BlockSpec((block, 2 * LANES), lambda i: (i, 0)),
            pl.BlockSpec((block, LANES), lambda i: (i, 0)),
            pl.BlockSpec((feats_count, LANES), whole),
        ],
        compiler_params=pltpu.CompilerParams(vmem_limit_bytes=12 * 2**20),
        cost_estimate=pl.CostEstimate(flops=0, bytes_accessed=6 * depth * 384, transcendentals=0),
    )(place, half, other)


def motion_kernel(place, disparity, offsets, left, right, got_a, got_b, weight, hidden, grads,
                  motion, pre, feats, hidden_ext, grads_ext, ext, window, flipped):
    odd = place[1] % 2 == 1
    cols = left.shape[1]
    wide = cols + 2 * HALO
    block = wide // 2
    span = 512
    tail = DISP + HALO
    flat = (lax.broadcasted_iota(jnp.int32, (LANES, LANES), 0)
            + lax.broadcasted_iota(jnp.int32, (LANES, LANES), 1))
    mirror = jnp.where(flat == LANES - 1, 1.0, 0.0).astype(BF16)
    total = window.shape[0]
    position = lax.broadcasted_iota(jnp.int32, (span, LANES), 0) - (block - 1)
    valid = (position >= 0) & (position < DISP)
    for row in range(2):
        from_left, from_right = sides(odd, got_a[row], got_b[row])
        state, last = tail + 3 * HALO, HALO + cols
        hidden_ext[row, 0:HALO] = from_left[state : state + HALO, :LANES]
        hidden_ext[row, HALO:last] = hidden[row]
        hidden_ext[row, last:] = from_right[state : state + HALO, LANES:]
        grads_ext[row, 0:HALO] = from_left[state + HALO :, :LANES]
        grads_ext[row, HALO:last] = grads[row]
        grads_ext[row, last:] = from_right[state + HALO :, LANES:]
        motion[row, wide : wide + HALO] = from_left[state : state + HALO, :LANES]
        motion[row, wide + HALO :] = from_right[state : state + HALO, LANES:]
        ext[0:HALO] = from_left[tail : tail + HALO]
        ext[HALO : HALO + cols] = left[row]
        ext[HALO + cols : wide] = from_right[tail + HALO : tail + 2 * HALO]
        window[0:tail] = from_left[0:tail]
        window[tail : tail + cols] = right[row]
        window[tail + cols : tail + cols + HALO] = from_right[tail + 2 * HALO : tail + 3 * HALO]
        window[tail + cols + HALO :] = jnp.zeros((total - tail - cols - HALO, window.shape[1]), BF16)
        parts = total // LANES
        for part in range(parts):
            source = window[(parts - 1 - part) * LANES : (parts - part) * LANES]
            flipped[part * LANES : (part + 1) * LANES] = dot(mirror, source).astype(BF16)
        flipped[total:] = jnp.zeros((flipped.shape[0] - total, window.shape[1]), BF16)
        table = lookup_rows(position, valid, disparity, offsets, row)
        for part in range(2):
            start = part * block
            base = total - DISP - start - block
            scores = dot_nt(ext[start : start + block], flipped[base : base + span])
            scores = scores * (1.0 / math.sqrt(left.shape[2]))
            band = pltpu.roll(scores, 0, 1, stride=1, stride_axis=0)
            found = split_dot(band, table, dot).astype(BF16)
            value = dot(found, weight[...])
            feats[row, start : start + block] = found
            pre[row, start : start + block] = value
            motion[row, start : start + block] = (value * jax.nn.sigmoid(value)).astype(BF16)


def image_columns(place, wide, cols, cols_axis):
    column = lax.broadcasted_iota(jnp.int32, (wide, LANES), 0) - HALO + place[1] * cols
    return (column >= 0) & (column < cols * cols_axis)


def fill_rows(store, odd, own, first, second, wide):
    for row in range(2):
        above, below = sides(odd, first[row, :wide], second[row, :wide])
        store(row, above.astype(F32))
        store(4 + row, below.astype(F32))
        store(2 + row, own[row, :wide].astype(F32))


def gates(fields, resets, gate_w, update, reset, reset_hidden, wide):
    block = wide // SPLIT
    deep = gate_w.shape[0] // 3

    for step in range(4 * SPLIT):
        row, start = step // SPLIT, (step % SPLIT) * block
        here = pl.ds(start, block)
        total = sum(dot(fields[row + a, here], gate_w[a * deep : (a + 1) * deep]) for a in range(3))
        reset_part = jax.nn.sigmoid(total[:, LANES:])
        update[row, here] = jax.nn.sigmoid(total[:, :LANES])
        reset[row, here] = reset_part
        hidden = fields[row + 1, here, 2 * LANES : 3 * LANES].astype(F32)
        reset_hidden[row, here] = (reset_part * hidden).astype(BF16)
    for row in range(4):
        store_taps(resets, row, 0, 2 * LANES, reset_hidden[row].astype(F32), True)
        for tap in range(3):
            start = (2 * tap + 1) * LANES
            resets[row, :, start : start + LANES] = fields[row + 1, :, start : start + LANES]


def load_field(odd, fields, lane, own, first, second):
    wide = fields.shape[1]
    fill_rows(lambda r, v: store_taps(fields, r, lane, 2 * LANES, v, True), odd, own, first, second, wide)


def candidate_part(resets, cand_w, row, here):
    deep = cand_w.shape[0] // 3
    total = sum(dot(resets[row + a, here], cand_w[a * deep : (a + 1) * deep]) for a in range(3))
    return jnp.tanh(total)


def first_kernel(cols_axis, place, hidden, init_a, init_b, motion, motion_a, motion_b, gate_w, cand_w,
                 later, update, reset, reset_hidden, candidate, hiddens, fields, resets):
    odd = place[0] % 2 == 1
    wide = hidden.shape[1]
    block = wide // SPLIT
    load_field(odd, fields, LANES, motion, motion_a, motion_b)
    for row in range(2):
        got_a, got_b = (
            jnp.concatenate(
                [sent[row, wide : wide + HALO], inner[row], sent[row, wide + HALO :]], axis=0
            )
            for sent, inner in ((motion_a, init_a), (motion_b, init_b))
        )
        above, below = sides(odd, got_a, got_b)
        for there, value in ((row, above), (2 + row, hidden[row]), (4 + row, below)):
            store_taps(fields, there, 0, 2 * LANES, value.astype(F32), True)
            if 0 < there < 5:
                hiddens[there - 1] = value
    gates(fields, resets, gate_w, update, reset, reset_hidden, wide)
    inside = image_columns(place, wide, wide - 2 * HALO, cols_axis)
    for row in range(2):
        for start in range(0, wide, block):
            here = pl.ds(start, block)
            new = candidate_part(resets, cand_w, row, here)
            candidate[row, here] = new
            gate = update[row + 1, here]
            old = hidden[row, here].astype(F32)
            value = (1.0 - gate) * old + gate * new
            later[row, here] = jnp.where(inside[start : start + block], value, 0.0).astype(BF16)


def gradients_out(grad, gate, new, old, row, here, grad_cand, grad_update, send_a, send_b):
    cand_part = (grad * gate * (1.0 - new * new)).astype(BF16)
    grad_cand[row, here] = cand_part
    send_a[row, here] = cand_part
    send_b[row, here] = cand_part
    grad_update[row, here] = (grad * (new - old) * gate * (1.0 - gate)).astype(BF16)


def send_updates(odd, grad_update, send_a, send_b):
    send_a[2], send_b[2] = sides(odd, grad_update[0], grad_update[1])


def second_kernel(place, hidden, hidden_a, hidden_b, motion, motion_a, motion_b, gate_w, cand_w, grad_hidden,
                  update, reset, reset_hidden, grad_cand, grad_update, send_a, send_b, fields, resets):
    odd = place[0] % 2 == 1
    wide = hidden.shape[1]
    block = wide // SPLIT
    load_field(odd, fields, LANES, motion, motion_a, motion_b)
    load_field(odd, fields, 0, hidden, hidden_a, hidden_b)
    gates(fields, resets, gate_w, update, reset, reset_hidden, wide)
    for row in range(2):
        for start in range(0, wide, block):
            here = pl.ds(start, block)
            new = candidate_part(resets, cand_w, row, here)
            gradients_out(grad_hidden[row, here].astype(F32), update[row + 1, here], new,
                          hidden[row, here].astype(F32), row, here, grad_cand, grad_update, send_a, send_b)
    send_updates(odd, grad_update, send_a, send_b)


def back_step(place, grad_cand, grad_a, grad_b, grad_update, hiddens, reset, cand_wt, gate_wt,
              grad_reset, cand_taps, gate_taps, inner, grad_motion, finish):
    odd = place[0] % 2 == 1
    wide = grad_cand.shape[1]
    block = wide // SPLIT
    fill_rows(lambda r, v: store_taps(cand_taps, r, 0, LANES, v, False), odd, grad_cand, grad_a, grad_b, wide)
    deep = cand_wt.shape[0] // 3
    deeper = gate_wt.shape[0] // 3

    for step in range(4 * SPLIT):
        row, start = step // SPLIT, (step % SPLIT) * block
        here = pl.ds(start, block)
        total = sum(dot(cand_taps[row + 2 - a, here], cand_wt[a * deep : (a + 1) * deep]) for a in range(3))
        inner[row, here] = total[:, :LANES]
        if row in (1, 2):
            grad_motion[row - 1, here] = total[:, LANES:]
    above_u, below_u = sides(odd, grad_a[2], grad_b[2])
    updates = (above_u, grad_update[0], grad_update[1], below_u)
    for row in range(4):
        gate = reset[row]
        value = (inner[row] * hiddens[row].astype(F32) * gate * (1.0 - gate)).astype(BF16)
        store_taps(gate_taps, row, 0, 2 * LANES, updates[row].astype(F32), False)
        store_taps(gate_taps, row, LANES, 2 * LANES, value.astype(F32), False)
        if row in (1, 2):
            grad_reset[row - 1] = value
    for row in range(2):
        for start in range(0, wide, block):
            here = pl.ds(start, block)
            total = sum(
                dot(gate_taps[row + 2 - a, here], gate_wt[a * deeper : (a + 1) * deeper]) for a in range(3)
            )
            grad_motion[row, here] += total[:, LANES:]
            finish(row, start, here, inner[row + 1, here] * reset[row + 1, here] + total[:, :LANES])


def later_back_kernel(cols_axis, place, grad_cand, grad_a, grad_b, grad_update, hidden, hidden_a, hidden_b, reset,
                      cand_wt, gate_wt, update, grad_hidden, older_hiddens, older_update, older_candidate,
                      grad_reset, grad_state, grad_motion, older_cand, older_upd, send_a, send_b,
                      cand_taps, gate_taps, inner):
    odd = place[0] % 2 == 1
    wide = hidden.shape[1]
    block = wide // SPLIT
    inside = image_columns(place, wide, wide - 2 * HALO, cols_axis)

    def finish(row, start, here, terms):
        gate = update[row + 1, here]
        grad = grad_hidden[row, here].astype(F32) * (1.0 - gate) + terms
        grad = jnp.where(inside[start : start + block], grad, 0.0)
        grad_state[row, here] = grad
        gradients_out(grad, older_update[row + 1, here], older_candidate[row, here],
                      older_hiddens[row + 1, here].astype(F32), row, here, older_cand, older_upd, send_a, send_b)

    hiddens = hidden_rows(odd, hidden, hidden_a, hidden_b)
    back_step(place, grad_cand, grad_a, grad_b, grad_update, hiddens, reset, cand_wt, gate_wt,
              grad_reset, cand_taps, gate_taps, inner, grad_motion, finish)
    send_updates(odd, older_upd, send_a, send_b)


def first_back_kernel(place, grad_cand, grad_a, grad_b, grad_update, hiddens, reset,
                      cand_wt, gate_wt, update, grad_state, motion_so_far,
                      grad_reset, grad_first, grad_motion, cand_taps, gate_taps, inner):
    def finish(row, start, here, terms):
        gate = update[row + 1, here]
        grad = grad_state[row, here] * (1.0 - gate) + terms
        first, last = max(start, HALO), min(start + grad.shape[0], HALO + grad_first.shape[1])
        grad_first[row, first - HALO : last - HALO] = grad[first - start : last - start].astype(BF16)
        grad_motion[row, here] += motion_so_far[row, here]

    back_step(place, grad_cand, grad_a, grad_b, grad_update, hiddens, reset, cand_wt, gate_wt,
              grad_reset, cand_taps, gate_taps, inner, grad_motion, finish)


def load_pixels(odd, pixels, hiddens, motion, motion_a, motion_b):
    wide = pixels.shape[0] // 4
    for row, value in enumerate(hidden_rows(odd, motion, motion_a, motion_b)):
        pixels[row * wide : (row + 1) * wide, LANES:] = value[:wide]
    for row, value in enumerate(hiddens):
        pixels[row * wide : (row + 1) * wide, :LANES] = value


def load_grads(taps, grads):
    wide = grads.shape[1]
    column = lax.broadcasted_iota(jnp.int32, (wide, LANES), 0)
    own = (column >= HALO) & (column < wide - HALO)
    depth = grads.shape[2]
    for row in range(2):
        for part in range(depth // LANES):
            value = jnp.where(own, grads[row, :, part * LANES : (part + 1) * LANES].astype(F32), 0.0)
            shifted = (pltpu.roll(value, wide - 1, 0), value, pltpu.roll(value, 1, 0))
            for tap in range(3):
                start = tap * depth + part * LANES
                taps[row * wide : (row + 1) * wide, start : start + LANES] = shifted[tap].astype(BF16)


def weight_products(pixels, taps, wide, depth, finish):
    for a in range(3):
        total = dot_tn(pixels[a * wide : (a + 2) * wide], taps[...])
        for b in range(3):
            finish((3 * a + b) * 2 * LANES, total[:, b * depth : (b + 1) * depth])


def hidden_rows(odd, hidden, hidden_a, hidden_b):
    above, below = sides(odd, hidden_a[1], hidden_b[1])[0], sides(odd, hidden_a[0], hidden_b[0])[1]
    return (above, hidden[0], hidden[1], below)


def load_hidden(pixels, rows, wide):
    for row, value in enumerate(rows):
        pixels[row * wide : (row + 1) * wide, :LANES] = value


def second_weights_kernel(place, resets, hidden, hidden_a, hidden_b, motion, motion_a, motion_b, cand_grads, update_grads,
                          cand_out, update_out, pixels, taps):
    odd = place[0] % 2 == 1
    wide = taps.shape[0] // 2
    load_pixels(odd, pixels, [resets[row] for row in range(4)], motion, motion_a, motion_b)
    load_grads(taps, cand_grads)

    def cand_finish(start, value):
        cand_out[pl.ds(start, 2 * LANES)] = value

    def update_finish(start, value):
        update_out[pl.ds(start, 2 * LANES)] = value

    weight_products(pixels, taps, wide, LANES, cand_finish)
    load_hidden(pixels, hidden_rows(odd, hidden, hidden_a, hidden_b), wide)
    load_grads(taps, update_grads)
    weight_products(pixels, taps, wide, LANES, update_finish)


def first_weights_kernel(place, resets, older, hidden, hidden_a, hidden_b, motion, motion_a, motion_b,
                         cand_grads, update_grads, reset_grads, cand_sum, update_sum,
                         cand_out, update_out, reset_out, pixels, taps):
    odd = place[0] % 2 == 1
    wide = taps.shape[0] // 2
    load_pixels(odd, pixels, [resets[row] for row in range(4)], motion, motion_a, motion_b)
    load_grads(taps, cand_grads)

    def cand_finish(start, value):
        here = pl.ds(start, 2 * LANES)
        cand_out[here] = cand_sum[here] + value

    def update_finish(start, value):
        here = pl.ds(start, 2 * LANES)
        update_out[here] = update_sum[here] + value

    def reset_finish(start, value):
        reset_out[pl.ds(start, 2 * LANES)] = value

    weight_products(pixels, taps, wide, LANES, cand_finish)
    load_hidden(pixels, [older[row] for row in range(4)], wide)
    load_grads(taps, update_grads)
    weight_products(pixels, taps, wide, LANES, update_finish)
    load_hidden(pixels, hidden_rows(odd, hidden, hidden_a, hidden_b), wide)
    load_grads(taps, reset_grads)
    weight_products(pixels, taps, wide, LANES, reset_finish)


def last_weights_kernel(place, hiddens, motion, motion_a, motion_b, reset_grads, reset_sum,
                        update_sum, cand_sum, motion_w, kept, given, pixels, taps, parts):
    odd = place[0] % 2 == 1
    load_pixels(odd, pixels, [hiddens[row] for row in range(4)], motion, motion_a, motion_b)
    load_grads(taps, reset_grads)
    rows = cand_sum.shape[0]

    def finish(start, value):
        parts[rows + start : rows + start + 2 * LANES] = (value + reset_sum[pl.ds(start, 2 * LANES)]).astype(BF16)

    weight_products(pixels, taps, taps.shape[0] // 2, LANES, finish)
    parts[0:rows] = update_sum[...].astype(BF16)
    parts[2 * rows : 3 * rows] = cand_sum[...].astype(BF16)
    parts[3 * rows : 3 * rows + LANES] = motion_w[...].astype(BF16)
    parts[3 * rows + LANES :] = jnp.zeros((parts.shape[0] - 3 * rows - LANES, LANES), BF16)
    half = parts.shape[0] // 2
    core = place[1] % 2
    kept[...] = parts[pl.ds(pl.multiple_of(core * half, LANES), half)]
    given[...] = parts[pl.ds(pl.multiple_of((1 - core) * half, LANES), half)]


def right_kernel(place, own, back_a, back_b, grad_right):
    odd = place[1] % 2 == 1
    split = own.shape[1] - DISP
    for row in range(2):
        grad_right[row, :split] = own[row, :split].astype(BF16)
        returned = sides(odd, back_a[row], back_b[row])[1].astype(F32)
        grad_right[row, split:] = (own[row, split:] + returned).astype(BF16)


def band_back_kernel(place, disparity, offsets, left, right, got_a, got_b, weight, grad_motion, pre, feats,
                     grad_left, back, own, motion_w, window, grad_window):
    odd = place[1] % 2 == 1
    cols = left.shape[1]
    block = cols // 2
    span = 512
    scaling = 1.0 / math.sqrt(left.shape[2])
    position = DISP - lax.broadcasted_iota(jnp.int32, (span, LANES), 0)
    valid = (position >= 0) & (position < DISP)
    inner = slice(HALO, HALO + cols)
    total_w = jnp.zeros((LANES, LANES), F32)
    for row in range(2):
        from_left = sides(odd, got_a[row], got_b[row])[0]
        window[0:DISP] = from_left[HALO : HALO + DISP]
        window[DISP : DISP + cols] = right[row]
        window[DISP + cols :] = jnp.zeros((window.shape[0] - DISP - cols, window.shape[1]), BF16)
        grad_window[...] = jnp.zeros(grad_window.shape, F32)
        value = pre[row, inner]
        gate = jax.nn.sigmoid(value)
        slope = gate * (1.0 + value * (1.0 - gate))
        grad_pre = (grad_motion[row, inner] * slope).astype(BF16)
        total_w = total_w + dot_tn(feats[row, inner], grad_pre)
        grad_feats = dot_nt(grad_pre, weight[...])
        table = lookup_rows(position, valid, disparity, offsets, row)
        for part in range(2):
            here = slice(part * block, (part + 1) * block)
            there = slice(part * block, part * block + span)
            band = split_dot(grad_feats[here], table, dot_nt)
            scores = (pltpu.roll(band, 0, 1, stride=1, stride_axis=0) * scaling).astype(BF16)
            grad_left[row, here] = dot(scores, window[there]).astype(BF16)
            grad_window[there] += dot_tn(scores, left[row, here])
        back[row] = grad_window[0:DISP].astype(BF16)
        own[row] = grad_window[DISP : DISP + cols]
    motion_w[...] = total_w


def pairings(count):
    first = [(2 * k, 2 * k + 1) for k in range(count // 2)]
    second = [(2 * k + 1, 2 * k + 2) for k in range(count // 2 - 1)]
    both = lambda pairs: pairs + [(b, a) for a, b in pairs]
    return both(first), both(second)


def exchanged(value, axis):
    first, second = pairings(lax.axis_size(axis))
    return lax.ppermute(value, axis, first), lax.ppermute(value, axis, second)


def exchanged_pair(value_a, value_b, axis):
    first, second = pairings(lax.axis_size(axis))
    return lax.ppermute(value_a, axis, first), lax.ppermute(value_b, axis, second)


def summed_everywhere(kept, given, axes, meanwhile):
    cols_count = lax.axis_size("cols")
    devices = lax.axis_size("rows") * cols_count
    swap = [(i, i ^ 1) for i in range(cols_count)]
    groups = [[i for i in range(devices) if i % 2 == c] for c in range(2)]
    got = lax.ppermute(given, "cols", swap)
    got, meanwhile = lax.optimization_barrier((got, meanwhile))
    half = (kept.astype(F32) + got.astype(F32)).astype(BF16).reshape(devices // 2, -1, LANES)
    pieces = lax.all_to_all(half, axes, 0, 0, tiled=True, axis_index_groups=groups)
    piece = jnp.sum(pieces.astype(F32), axis=0).astype(BF16)
    spread = jnp.broadcast_to(piece[None], pieces.shape)
    half = lax.all_to_all(spread, axes, 0, 0, tiled=True, axis_index_groups=groups)
    other = lax.ppermute(half, "cols", swap)
    return half.reshape(-1, LANES), other.reshape(-1, LANES), meanwhile


def on_device(
    fmap_left,
    fmap_right,
    hidden_init,
    disp_init,
    level_offset,
    motion_weight,
    gate_weight,
    cand_weight,
    grad_hidden,
):
    rows, cols, channels = fmap_left.shape
    wide = cols + 2 * HALO
    state = hidden_init.shape[2]
    feats_count = motion_weight.shape[0]
    rows_axis, cols_axis = lax.axis_size("rows"), lax.axis_size("cols")
    rows_index, cols_index = lax.axis_index("rows"), lax.axis_index("cols")
    place = jnp.stack([rows_index, cols_index]).astype(jnp.int32)

    halos = packed(fmap_left, fmap_right, hidden_init, grad_hidden)
    maps_a, maps_b = exchanged(halos, "cols")
    init_a, init_b = exchanged(hidden_init, "rows")
    motion_w = jnp.pad(motion_weight, ((0, LANES - feats_count), (0, 0)))
    gate_wt = jnp.transpose(gate_weight.reshape(3, 3, 2 * state, 2 * state), (0, 1, 3, 2)).reshape(-1, 2 * state)
    cand_wt = jnp.transpose(cand_weight.reshape(3, 3, 2 * state, state), (0, 1, 3, 2)).reshape(-1, 2 * state)
    motion_w, gate_wt, cand_wt, init_a, init_b = lax.optimization_barrier(
        (motion_w, gate_wt, cand_wt, init_a, init_b)
    )

    field = lambda count, dtype: array((count, wide, LANES), dtype)
    band_flops = 2 * rows * wide * 512 * channels
    motion, motion_pre, feats, hidden, grads = kernel_call(
        motion_kernel,
        [array((2, wide + 2 * HALO, LANES), BF16), field(2, F32), field(2, BF16), field(2, BF16), field(2, BF16)],
        [place, disp_init, level_offset, fmap_left, fmap_right, maps_a, maps_b, motion_w, hidden_init, grad_hidden],
        3,
        [pltpu.VMEM((wide, channels), BF16), pltpu.VMEM((768, channels), BF16), pltpu.VMEM((832, channels), BF16)],
        2 * band_flops,
    )
    motions = (motion, *exchanged(motion, "rows"))
    unit = 2 * wide * 9 * 2 * state * state
    fields = [pltpu.VMEM((6, wide, 6 * LANES), BF16), pltpu.VMEM((4, wide, 6 * LANES), BF16)]

    hidden_1, update_0, reset_0, reset_hidden_0, candidate_0, hiddens_0 = kernel_call(
        lambda *refs: first_kernel(cols_axis, *refs),
        [field(2, BF16), field(4, F32), field(4, F32), field(4, BF16), field(2, F32), field(4, BF16)],
        [place, hidden, init_a, init_b, *motions, gate_weight, cand_weight],
        1,
        fields,
        10 * unit,
    )
    hidden_1a, hidden_1b = exchanged(hidden_1, "rows")
    update_1, reset_1, reset_hidden_1, grad_cand_1, grad_update_1, send_a, send_b = kernel_call(
        second_kernel,
        [field(4, F32), field(4, F32), field(4, BF16), field(2, BF16), field(2, BF16), field(3, BF16), field(3, BF16)],
        [place, hidden_1, hidden_1a, hidden_1b, *motions, gate_weight, cand_weight, grads],
        1,
        fields,
        10 * unit,
    )
    got_a, got_b = exchanged_pair(send_a, send_b, "rows")
    pixels = pltpu.VMEM((4 * wide, 2 * LANES), BF16)
    taps = pltpu.VMEM((2 * wide, 3 * LANES), BF16)
    weights = array(cand_weight.shape, F32)
    cand_sum, update_sum = kernel_call(
        second_weights_kernel,
        [weights, weights],
        [place, reset_hidden_1, hidden_1, hidden_1a, hidden_1b, *motions, grad_cand_1, grad_update_1],
        1,
        [pixels, taps],
        4 * unit,
    )
    got_a, got_b, cand_sum, update_sum = lax.optimization_barrier((got_a, got_b, cand_sum, update_sum))
    back_scratch = [
        pltpu.VMEM((6, wide, 3 * LANES), BF16),
        pltpu.VMEM((4, wide, 6 * LANES), BF16),
        pltpu.VMEM((4, wide, LANES), F32),
    ]
    grad_reset_1, grad_state, grad_motion_1, grad_cand_0, grad_update_0, send_a, send_b = kernel_call(
        lambda *refs: later_back_kernel(cols_axis, *refs),
        [field(2, BF16), field(2, F32), field(2, F32), field(2, BF16), field(2, BF16),
         field(3, BF16), field(3, BF16)],
        [place, grad_cand_1, got_a, got_b, grad_update_1, hidden_1, hidden_1a, hidden_1b, reset_1, cand_wt, gate_wt,
         update_1, grads, hiddens_0, update_0, candidate_0],
        1,
        back_scratch,
        8 * unit,
    )
    got_a, got_b = exchanged_pair(send_a, send_b, "rows")
    cand_sum, update_sum, reset_sum = kernel_call(
        first_weights_kernel,
        [weights, weights, weights],
        [place, reset_hidden_0, hiddens_0, hidden_1, hidden_1a, hidden_1b, *motions,
         grad_cand_0, grad_update_0, grad_reset_1, cand_sum, update_sum],
        1,
        [pixels, taps],
        6 * unit,
    )
    got_a, got_b, cand_sum, update_sum, reset_sum = lax.optimization_barrier(
        (got_a, got_b, cand_sum, update_sum, reset_sum)
    )
    grad_reset_0, grad_first, grad_motion = kernel_call(
        first_back_kernel,
        [field(2, BF16), array((2, cols, LANES), BF16), field(2, F32)],
        [place, grad_cand_0, got_a, got_b, grad_update_0, hiddens_0, reset_0, cand_wt, gate_wt,
         update_0, grad_state, grad_motion_1],
        1,
        back_scratch,
        8 * unit,
    )
    grad_left, back, own, motion_sum = kernel_call(
        band_back_kernel,
        [array((2, cols, channels), BF16), array((2, DISP, channels), BF16), array((2, cols, channels), F32),
         array((LANES, LANES), F32)],
        [place, disp_init, level_offset, fmap_left, fmap_right, maps_a, maps_b, motion_w, grad_motion, motion_pre, feats],
        3,
        [pltpu.VMEM((768, channels), BF16), pltpu.VMEM((768, channels), F32)],
        3 * band_flops,
    )
    back_a, back_b = exchanged(back, "cols")
    devices = rows_axis * cols_axis
    total = devices * CHUNK_ROWS
    kept, given = kernel_call(
        last_weights_kernel,
        [array((total // 2, LANES), BF16), array((total // 2, LANES), BF16)],
        [place, hiddens_0, *motions, grad_reset_0, reset_sum, update_sum, cand_sum, motion_sum],
        1,
        [pixels, taps, pltpu.VMEM((total, LANES), BF16)],
        2 * unit,
    )
    (grad_right,) = kernel_call(
        right_kernel, [array((2, cols, channels), BF16)], [place, own, back_a, back_b], 1, [], 0
    )
    half, other, (grad_left, grad_right, grad_first) = summed_everywhere(
        kept, given, ("rows", "cols"), (grad_left, grad_right, grad_first)
    )
    normaliser = 1.0 / math.sqrt(rows * rows_axis * cols * cols_axis)
    grad_gate_w, grad_cand_w, grad_motion_w = unpacked(
        place, half, other, cand_weight.shape[0], feats_count, normaliser
    )
    return (grad_left, grad_right, grad_first, grad_motion_w, grad_gate_w, grad_cand_w)


def solution(mesh):
    in_specs = (
        P("rows", "cols", None),
        P("rows", "cols", None),
        P("rows", "cols", None),
        P("rows"),
        P("rows", None),
        P(),
        P(),
        P(),
        P("rows", "cols", None),
    )
    out_specs = (
        P("rows", "cols", None),
        P("rows", "cols", None),
        P("rows", "cols", None),
        P(),
        P(),
        P(),
    )
    return jax.shard_map(
        on_device, mesh=mesh, in_specs=in_specs, out_specs=out_specs, check_vma=False
    )
```

```python
import math

import jax
import jax.numpy as jnp
from jax import lax
from jax.experimental import pallas as pl
from jax.experimental.pallas import tpu as pltpu
from jax.sharding import PartitionSpec as P

LEVELS = 4
RADIUS = 4
DISP = 192
TAPS = 2 * RADIUS + 1
HALO = 16
LANES = 128
SPLIT = 2
CHUNK_ROWS = 56

BF16 = jnp.bfloat16
F32 = jnp.float32
VMEM = pl.BlockSpec(memory_space=pltpu.VMEM)
SMEM = pl.BlockSpec(memory_space=pltpu.SMEM)


def dot(a, b):
    return jnp.dot(a, b, preferred_element_type=F32)


def dot_nt(a, b):
    return lax.dot_general(a, b, (((1,), (1,)), ((), ())), preferred_element_type=F32)


def dot_tn(a, b):
    return lax.dot_general(a, b, (((0,), (0,)), ((), ())), preferred_element_type=F32)


def split_dot(a, table, contract):
    high = a.astype(BF16)
    low = (a - high.astype(F32)).astype(BF16)
    return contract(high, table) + contract(low, table)


def kernel_call(body, outs, ins, scalars, scratch, flops):
    bytes_moved = sum(math.prod(x.shape) * x.dtype.itemsize for x in (*ins, *outs))
    held = sum(math.prod(x.shape) * jnp.dtype(x.dtype).itemsize for x in scratch)
    return pl.pallas_call(
        body,
        out_shape=outs,
        in_specs=[SMEM] * scalars + [VMEM] * (len(ins) - scalars),
        out_specs=[VMEM] * len(outs),
        scratch_shapes=scratch,
        compiler_params=pltpu.CompilerParams(vmem_limit_bytes=bytes_moved + held + 4 * 2**20),
        cost_estimate=pl.CostEstimate(flops=flops, bytes_accessed=bytes_moved, transcendentals=0),
    )(*ins)


def array(shape, dtype):
    return jax.ShapeDtypeStruct(shape, dtype)


def lookup_rows(position, valid, disparity, offsets, row):
    count = position.shape[0]
    feature = lax.broadcasted_iota(jnp.int32, (count, LANES), 1)
    table = jnp.zeros((count, LANES), F32)
    for level in range(LEVELS):
        centre = (disparity[row] >> level) + offsets[row, level]
        tap = feature - level * TAPS
        matches = (position >> level) == tap + (centre - RADIUS)
        matches = matches & (tap >= 0) & (tap < TAPS) & valid
        table = jnp.where(matches, 1.0 / 2**level, table)
    return table.astype(BF16)


def sides(odd, first, second):
    return jnp.where(odd, first, second), jnp.where(odd, second, first)


def store_taps(ref, row, lane, step, value, forward):
    wide = value.shape[0]
    left = pltpu.roll(value, 1, 0).astype(BF16)
    right = pltpu.roll(value, wide - 1, 0).astype(BF16)
    taps = (left, value.astype(BF16), right) if forward else (right, value.astype(BF16), left)
    for tap in range(3):
        start = lane + tap * step
        ref[row, :, start : start + LANES] = taps[tap]


def pack_kernel(left, right, hidden, grads, out, sems):
    cols = left.shape[1]
    tail = DISP + HALO
    first, last = pl.ds(0, HALO), pl.ds(cols - HALO, HALO)
    low, high = pl.ds(0, LANES), pl.ds(LANES, LANES)
    every = pl.ds(0, 2 * LANES)
    moves = (
        (right, pl.ds(cols - tail, tail), pl.ds(0, tail), every),
        (left, last, pl.ds(tail, HALO), every),
        (left, first, pl.ds(tail + HALO, HALO), every),
        (right, first, pl.ds(tail + 2 * HALO, HALO), every),
        (hidden, last, pl.ds(tail + 3 * HALO, HALO), low),
        (hidden, first, pl.ds(tail + 3 * HALO, HALO), high),
        (grads, last, pl.ds(tail + 4 * HALO, HALO), low),
        (grads, first, pl.ds(tail + 4 * HALO, HALO), high),
    )
    copies = [
        pltpu.make_async_copy(source.at[:, start], out.at[:, stop, lanes], sems.at[number])
        for number, (source, start, stop, lanes) in enumerate(moves)
    ]
    for copy in copies:
        copy.start()
    for copy in copies:
        copy.wait()


def packed(left, right, hidden, grads):
    rows, cols, channels = left.shape
    count = DISP + 6 * HALO
    return pl.pallas_call(
        pack_kernel,
        out_shape=array((rows, count, channels), BF16),
        in_specs=[pl.BlockSpec(memory_space=pltpu.HBM)] * 4,
        out_specs=VMEM,
        scratch_shapes=[pltpu.SemaphoreType.DMA((8,))],
        compiler_params=pltpu.CompilerParams(vmem_limit_bytes=56 * 2**20),
        cost_estimate=pl.CostEstimate(flops=0, bytes_accessed=4 * rows * count * channels, transcendentals=0),
    )(left, right, hidden, grads)


def spread_half(core, half, scale, gate, cand, gate_part, cand_part, sems):
    depth = gate_part.shape[0]
    count = cand_part.shape[0]
    block = depth // 4
    lanes = pl.ds(pl.multiple_of(core * LANES, LANES), LANES)
    copies = []
    for number in range(4):
        here = pl.ds(number * block, block)
        gate_part[here] = half[here].astype(F32) * scale
        copies.append(pltpu.make_async_copy(gate_part.at[here], gate.at[here, lanes], sems.at[number]))
        copies[-1].start()
    cand_part[...] = half[depth : depth + count].astype(F32) * scale
    there = pl.ds(pl.multiple_of(core * count, LANES), count)
    copies.append(pltpu.make_async_copy(cand_part, cand.at[there], sems.at[4]))
    copies[-1].start()
    for copy in copies:
        copy.wait()


def own_half_kernel(scale, place, half, gate, cand, gate_part, cand_part, sems):
    spread_half(place[1] % 2, half, scale, gate, cand, gate_part, cand_part, sems)


def other_half_kernel(scale, place, half, other, gate_in, cand_in, motion, gate, cand, gate_part, cand_part, sems):
    core = place[1] % 2
    start = gate_part.shape[0] + cand_part.shape[0]
    rows = pl.ds(start, motion.shape[0])
    motion[...] = jnp.where(core == 0, half[rows], other[rows]).astype(F32) * scale
    spread_half(1 - core, other, scale, gate, cand, gate_part, cand_part, sems)


def half_call(body, place, arrays, outs, depth, aliases):
    anywhere = pl.BlockSpec(memory_space=pltpu.HBM)
    return pl.pallas_call(
        body,
        out_shape=outs,
        in_specs=[SMEM] + [VMEM] * (len(arrays) - len(aliases)) + [anywhere] * len(aliases),
        out_specs=[VMEM] * (len(outs) - 2) + [anywhere] * 2,
        scratch_shapes=[
            pltpu.VMEM((depth, LANES), F32), pltpu.VMEM((depth // 2, LANES), F32), pltpu.SemaphoreType.DMA((5,))
        ],
        input_output_aliases=aliases,
        compiler_params=pltpu.CompilerParams(vmem_limit_bytes=12 * 2**20),
        cost_estimate=pl.CostEstimate(flops=0, bytes_accessed=6 * depth * LANES, transcendentals=0),
    )(place, *arrays)


def motion_kernel(place, disparity, offsets, left, right, got_a, got_b, weight, hidden, grads,
                  motion, pre, feats, hidden_ext, grads_ext, ext, window, flipped):
    odd = place[1] % 2 == 1
    cols = left.shape[1]
    wide = cols + 2 * HALO
    block = wide // 2
    span = 512
    tail = DISP + HALO
    flat = (lax.broadcasted_iota(jnp.int32, (LANES, LANES), 0)
            + lax.broadcasted_iota(jnp.int32, (LANES, LANES), 1))
    mirror = jnp.where(flat == LANES - 1, 1.0, 0.0).astype(BF16)
    total = window.shape[0]
    position = lax.broadcasted_iota(jnp.int32, (span, LANES), 0) - (block - 1)
    valid = (position >= 0) & (position < DISP)
    for row in range(2):
        from_left, from_right = sides(odd, got_a[row], got_b[row])
        state, last = tail + 3 * HALO, HALO + cols
        hidden_ext[row, 0:HALO] = from_left[state : state + HALO, :LANES]
        hidden_ext[row, HALO:last] = hidden[row]
        hidden_ext[row, last:] = from_right[state : state + HALO, LANES:]
        grads_ext[row, 0:HALO] = from_left[state + HALO :, :LANES]
        grads_ext[row, HALO:last] = grads[row]
        grads_ext[row, last:] = from_right[state + HALO :, LANES:]
        motion[row, wide : wide + HALO] = from_left[state : state + HALO, :LANES]
        motion[row, wide + HALO :] = from_right[state : state + HALO, LANES:]
        ext[0:HALO] = from_left[tail : tail + HALO]
        ext[HALO : HALO + cols] = left[row]
        ext[HALO + cols : wide] = from_right[tail + HALO : tail + 2 * HALO]
        window[0:tail] = from_left[0:tail]
        window[tail : tail + cols] = right[row]
        window[tail + cols : tail + cols + HALO] = from_right[tail + 2 * HALO : tail + 3 * HALO]
        window[tail + cols + HALO :] = jnp.zeros((total - tail - cols - HALO, window.shape[1]), BF16)
        parts = total // LANES
        for part in range(parts):
            source = window[(parts - 1 - part) * LANES : (parts - part) * LANES]
            flipped[part * LANES : (part + 1) * LANES] = dot(mirror, source).astype(BF16)
        flipped[total:] = jnp.zeros((flipped.shape[0] - total, window.shape[1]), BF16)
        table = lookup_rows(position, valid, disparity, offsets, row)
        for part in range(2):
            start = part * block
            base = total - DISP - start - block
            scores = dot_nt(ext[start : start + block], flipped[base : base + span])
            scores = scores * (1.0 / math.sqrt(left.shape[2]))
            band = pltpu.roll(scores, 0, 1, stride=1, stride_axis=0)
            found = split_dot(band, table, dot).astype(BF16)
            value = dot(found, weight[...])
            feats[row, start : start + block] = found
            pre[row, start : start + block] = value
            motion[row, start : start + block] = (value * jax.nn.sigmoid(value)).astype(BF16)


def image_columns(place, wide, cols, cols_axis):
    column = lax.broadcasted_iota(jnp.int32, (wide, LANES), 0) - HALO + place[1] * cols
    return (column >= 0) & (column < cols * cols_axis)


def fill_rows(store, odd, own, first, second, wide):
    for row in range(2):
        above, below = sides(odd, first[row, :wide], second[row, :wide])
        store(row, above.astype(F32))
        store(4 + row, below.astype(F32))
        store(2 + row, own[row, :wide].astype(F32))


def gates(fields, resets, gate_w, update, reset, reset_hidden, wide):
    block = wide // SPLIT
    deep = gate_w.shape[0] // 3

    for step in range(4 * SPLIT):
        row, start = step // SPLIT, (step % SPLIT) * block
        here = pl.ds(start, block)
        total = sum(dot(fields[row + a, here], gate_w[a * deep : (a + 1) * deep]) for a in range(3))
        reset_part = jax.nn.sigmoid(total[:, LANES:])
        update[row, here] = jax.nn.sigmoid(total[:, :LANES])
        reset[row, here] = reset_part
        hidden = fields[row + 1, here, 2 * LANES : 3 * LANES].astype(F32)
        reset_hidden[row, here] = (reset_part * hidden).astype(BF16)
    for row in range(4):
        store_taps(resets, row, 0, 2 * LANES, reset_hidden[row].astype(F32), True)
        for tap in range(3):
            start = (2 * tap + 1) * LANES
            resets[row, :, start : start + LANES] = fields[row + 1, :, start : start + LANES]


def load_field(odd, fields, lane, own, first, second):
    wide = fields.shape[1]
    fill_rows(lambda r, v: store_taps(fields, r, lane, 2 * LANES, v, True), odd, own, first, second, wide)


def candidate_part(resets, cand_w, row, here):
    deep = cand_w.shape[0] // 3
    total = sum(dot(resets[row + a, here], cand_w[a * deep : (a + 1) * deep]) for a in range(3))
    return jnp.tanh(total)


def first_kernel(cols_axis, place, hidden, init_a, init_b, motion, motion_a, motion_b, gate_w, cand_w,
                 later, update, reset, reset_hidden, candidate, hiddens, fields, resets):
    odd = place[0] % 2 == 1
    wide = hidden.shape[1]
    block = wide // SPLIT
    load_field(odd, fields, LANES, motion, motion_a, motion_b)
    for row in range(2):
        got_a, got_b = (
            jnp.concatenate(
                [sent[row, wide : wide + HALO], inner[row], sent[row, wide + HALO :]], axis=0
            )
            for sent, inner in ((motion_a, init_a), (motion_b, init_b))
        )
        above, below = sides(odd, got_a, got_b)
        for there, value in ((row, above), (2 + row, hidden[row]), (4 + row, below)):
            store_taps(fields, there, 0, 2 * LANES, value.astype(F32), True)
            if 0 < there < 5:
                hiddens[there - 1] = value
    gates(fields, resets, gate_w, update, reset, reset_hidden, wide)
    inside = image_columns(place, wide, wide - 2 * HALO, cols_axis)
    for row in range(2):
        for start in range(0, wide, block):
            here = pl.ds(start, block)
            new = candidate_part(resets, cand_w, row, here)
            candidate[row, here] = new
            gate = update[row + 1, here]
            old = hidden[row, here].astype(F32)
            value = (1.0 - gate) * old + gate * new
            later[row, here] = jnp.where(inside[start : start + block], value, 0.0).astype(BF16)


def gradients_out(grad, gate, new, old, row, here, grad_cand, grad_update, send_a, send_b):
    cand_part = (grad * gate * (1.0 - new * new)).astype(BF16)
    grad_cand[row, here] = cand_part
    send_a[row, here] = cand_part
    send_b[row, here] = cand_part
    grad_update[row, here] = (grad * (new - old) * gate * (1.0 - gate)).astype(BF16)


def send_updates(odd, grad_update, send_a, send_b):
    send_a[2], send_b[2] = sides(odd, grad_update[0], grad_update[1])


def second_kernel(place, hidden, hidden_a, hidden_b, motion, motion_a, motion_b, gate_w, cand_w, grad_hidden,
                  update, reset, reset_hidden, grad_cand, grad_update, send_a, send_b, fields, resets):
    odd = place[0] % 2 == 1
    wide = hidden.shape[1]
    block = wide // SPLIT
    load_field(odd, fields, LANES, motion, motion_a, motion_b)
    load_field(odd, fields, 0, hidden, hidden_a, hidden_b)
    gates(fields, resets, gate_w, update, reset, reset_hidden, wide)
    for row in range(2):
        for start in range(0, wide, block):
            here = pl.ds(start, block)
            new = candidate_part(resets, cand_w, row, here)
            gradients_out(grad_hidden[row, here].astype(F32), update[row + 1, here], new,
                          hidden[row, here].astype(F32), row, here, grad_cand, grad_update, send_a, send_b)
    send_updates(odd, grad_update, send_a, send_b)


def back_step(place, grad_cand, grad_a, grad_b, grad_update, hiddens, reset, cand_wt, gate_wt,
              grad_reset, cand_taps, gate_taps, inner, grad_motion, finish):
    odd = place[0] % 2 == 1
    wide = grad_cand.shape[1]
    block = wide // SPLIT
    fill_rows(lambda r, v: store_taps(cand_taps, r, 0, LANES, v, False), odd, grad_cand, grad_a, grad_b, wide)
    deep = cand_wt.shape[0] // 3
    deeper = gate_wt.shape[0] // 3

    for step in range(4 * SPLIT):
        row, start = step // SPLIT, (step % SPLIT) * block
        here = pl.ds(start, block)
        total = sum(dot(cand_taps[row + 2 - a, here], cand_wt[a * deep : (a + 1) * deep]) for a in range(3))
        inner[row, here] = total[:, :LANES]
        if row in (1, 2):
            grad_motion[row - 1, here] = total[:, LANES:]
    above_u, below_u = sides(odd, grad_a[2], grad_b[2])
    updates = (above_u, grad_update[0], grad_update[1], below_u)
    for row in range(4):
        gate = reset[row]
        value = (inner[row] * hiddens[row].astype(F32) * gate * (1.0 - gate)).astype(BF16)
        store_taps(gate_taps, row, 0, 2 * LANES, updates[row].astype(F32), False)
        store_taps(gate_taps, row, LANES, 2 * LANES, value.astype(F32), False)
        if row in (1, 2):
            grad_reset[row - 1] = value
    for row in range(2):
        for start in range(0, wide, block):
            here = pl.ds(start, block)
            total = sum(
                dot(gate_taps[row + 2 - a, here], gate_wt[a * deeper : (a + 1) * deeper]) for a in range(3)
            )
            grad_motion[row, here] += total[:, LANES:]
            finish(row, start, here, inner[row + 1, here] * reset[row + 1, here] + total[:, :LANES])


def later_back_kernel(cols_axis, place, grad_cand, grad_a, grad_b, grad_update, hidden, hidden_a, hidden_b, reset,
                      cand_wt, gate_wt, update, grad_hidden, older_hiddens, older_update, older_candidate,
                      grad_reset, grad_state, grad_motion, older_cand, older_upd, send_a, send_b,
                      cand_taps, gate_taps, inner):
    odd = place[0] % 2 == 1
    wide = hidden.shape[1]
    block = wide // SPLIT
    inside = image_columns(place, wide, wide - 2 * HALO, cols_axis)

    def finish(row, start, here, terms):
        gate = update[row + 1, here]
        grad = grad_hidden[row, here].astype(F32) * (1.0 - gate) + terms
        grad = jnp.where(inside[start : start + block], grad, 0.0)
        grad_state[row, here] = grad
        gradients_out(grad, older_update[row + 1, here], older_candidate[row, here],
                      older_hiddens[row + 1, here].astype(F32), row, here, older_cand, older_upd, send_a, send_b)

    hiddens = hidden_rows(odd, hidden, hidden_a, hidden_b)
    back_step(place, grad_cand, grad_a, grad_b, grad_update, hiddens, reset, cand_wt, gate_wt,
              grad_reset, cand_taps, gate_taps, inner, grad_motion, finish)
    send_updates(odd, older_upd, send_a, send_b)


def first_back_kernel(place, grad_cand, grad_a, grad_b, grad_update, hiddens, reset,
                      cand_wt, gate_wt, update, grad_state, motion_so_far, pre, feats, weight,
                      grad_reset, grad_first, grad_feats, motion_w, cand_taps, gate_taps, inner, grad_motion):
    def finish(row, start, here, terms):
        gate = update[row + 1, here]
        grad = grad_state[row, here] * (1.0 - gate) + terms
        first, last = max(start, HALO), min(start + grad.shape[0], HALO + grad_first.shape[1])
        grad_first[row, first - HALO : last - HALO] = grad[first - start : last - start].astype(BF16)
        grad_motion[row, here] += motion_so_far[row, here]

    back_step(place, grad_cand, grad_a, grad_b, grad_update, hiddens, reset, cand_wt, gate_wt,
              grad_reset, cand_taps, gate_taps, inner, grad_motion, finish)
    inner_cols = slice(HALO, HALO + grad_feats.shape[1])
    total = jnp.zeros((LANES, LANES), F32)
    for row in range(2):
        value = pre[row, inner_cols]
        gate = jax.nn.sigmoid(value)
        slope = gate * (1.0 + value * (1.0 - gate))
        grad_pre = (grad_motion[row, inner_cols] * slope).astype(BF16)
        total = total + dot_tn(feats[row, inner_cols], grad_pre)
        grad_feats[row] = dot_nt(grad_pre, weight[...])
    motion_w[...] = total


def load_pixels(odd, pixels, hiddens, motion, motion_a, motion_b):
    wide = pixels.shape[0] // 4
    for row, value in enumerate(hidden_rows(odd, motion, motion_a, motion_b)):
        pixels[row * wide : (row + 1) * wide, LANES:] = value[:wide]
    for row, value in enumerate(hiddens):
        pixels[row * wide : (row + 1) * wide, :LANES] = value


def load_grads(taps, grads):
    wide = grads.shape[1]
    column = lax.broadcasted_iota(jnp.int32, (wide, LANES), 0)
    own = (column >= HALO) & (column < wide - HALO)
    depth = grads.shape[2]
    for row in range(2):
        for part in range(depth // LANES):
            value = jnp.where(own, grads[row, :, part * LANES : (part + 1) * LANES].astype(F32), 0.0)
            shifted = (pltpu.roll(value, wide - 1, 0), value, pltpu.roll(value, 1, 0))
            for tap in range(3):
                start = tap * depth + part * LANES
                taps[row * wide : (row + 1) * wide, start : start + LANES] = shifted[tap].astype(BF16)


def weight_products(pixels, taps, wide, depth, finish):
    for a in range(3):
        total = dot_tn(pixels[a * wide : (a + 2) * wide], taps[...])
        for b in range(3):
            finish((3 * a + b) * 2 * LANES, total[:, b * depth : (b + 1) * depth])


def hidden_rows(odd, hidden, hidden_a, hidden_b):
    above, below = sides(odd, hidden_a[1], hidden_b[1])[0], sides(odd, hidden_a[0], hidden_b[0])[1]
    return (above, hidden[0], hidden[1], below)


def load_hidden(pixels, rows, wide):
    for row, value in enumerate(rows):
        pixels[row * wide : (row + 1) * wide, :LANES] = value


def second_weights_kernel(place, resets, hidden, hidden_a, hidden_b, motion, motion_a, motion_b, cand_grads, update_grads,
                          cand_out, update_out, pixels, taps):
    odd = place[0] % 2 == 1
    wide = taps.shape[0] // 2
    load_pixels(odd, pixels, [resets[row] for row in range(4)], motion, motion_a, motion_b)
    load_grads(taps, cand_grads)

    def cand_finish(start, value):
        cand_out[pl.ds(start, 2 * LANES)] = value

    def update_finish(start, value):
        update_out[pl.ds(start, 2 * LANES)] = value

    weight_products(pixels, taps, wide, LANES, cand_finish)
    load_hidden(pixels, hidden_rows(odd, hidden, hidden_a, hidden_b), wide)
    load_grads(taps, update_grads)
    weight_products(pixels, taps, wide, LANES, update_finish)


def first_weights_kernel(place, resets, older, hidden, hidden_a, hidden_b, motion, motion_a, motion_b,
                         cand_grads, update_grads, reset_grads, cand_sum, update_sum,
                         cand_out, update_out, reset_out, pixels, taps):
    odd = place[0] % 2 == 1
    wide = taps.shape[0] // 2
    load_pixels(odd, pixels, [resets[row] for row in range(4)], motion, motion_a, motion_b)
    load_grads(taps, cand_grads)

    def cand_finish(start, value):
        here = pl.ds(start, 2 * LANES)
        cand_out[here] = cand_sum[here] + value

    def update_finish(start, value):
        here = pl.ds(start, 2 * LANES)
        update_out[here] = update_sum[here] + value

    def reset_finish(start, value):
        reset_out[pl.ds(start, 2 * LANES)] = value

    weight_products(pixels, taps, wide, LANES, cand_finish)
    load_hidden(pixels, [older[row] for row in range(4)], wide)
    load_grads(taps, update_grads)
    weight_products(pixels, taps, wide, LANES, update_finish)
    load_hidden(pixels, hidden_rows(odd, hidden, hidden_a, hidden_b), wide)
    load_grads(taps, reset_grads)
    weight_products(pixels, taps, wide, LANES, reset_finish)


def last_weights_kernel(place, hiddens, motion, motion_a, motion_b, reset_grads, reset_sum,
                        update_sum, cand_sum, motion_w, kept, given, pixels, taps, parts):
    odd = place[0] % 2 == 1
    load_pixels(odd, pixels, [hiddens[row] for row in range(4)], motion, motion_a, motion_b)
    load_grads(taps, reset_grads)
    rows = cand_sum.shape[0]
    split = rows // 2
    last = rows + split

    def finish(start, value):
        parts[1, start : start + 2 * LANES] = (value + reset_sum[pl.ds(start, 2 * LANES)]).astype(BF16)

    weight_products(pixels, taps, taps.shape[0] // 2, LANES, finish)
    parts[0, 0:rows] = update_sum[...].astype(BF16)
    for half in range(2):
        parts[half, rows:last] = cand_sum[half * split : (half + 1) * split].astype(BF16)
    parts[0, last:] = motion_w[...].astype(BF16)
    parts[1, last:] = jnp.zeros((parts.shape[1] - last, LANES), BF16)
    core = place[1] % 2
    kept[...] = parts[core]
    given[...] = parts[1 - core]


def right_kernel(place, own, back_a, back_b, grad_right):
    odd = place[1] % 2 == 1
    split = own.shape[1] - DISP
    for row in range(2):
        grad_right[row, :split] = own[row, :split].astype(BF16)
        returned = sides(odd, back_a[row], back_b[row])[1].astype(F32)
        grad_right[row, split:] = (own[row, split:] + returned).astype(BF16)


def band_back_kernel(place, disparity, offsets, left, right, got_a, got_b, grad_feats,
                     grad_left, back, own, window, grad_window):
    odd = place[1] % 2 == 1
    cols = left.shape[1]
    block = cols // 2
    span = 512
    scaling = 1.0 / math.sqrt(left.shape[2])
    position = DISP - lax.broadcasted_iota(jnp.int32, (span, LANES), 0)
    valid = (position >= 0) & (position < DISP)
    for row in range(2):
        from_left = sides(odd, got_a[row], got_b[row])[0]
        window[0:DISP] = from_left[HALO : HALO + DISP]
        window[DISP : DISP + cols] = right[row]
        window[DISP + cols :] = jnp.zeros((window.shape[0] - DISP - cols, window.shape[1]), BF16)
        grad_window[...] = jnp.zeros(grad_window.shape, F32)
        table = lookup_rows(position, valid, disparity, offsets, row)
        for part in range(2):
            here = slice(part * block, (part + 1) * block)
            there = slice(part * block, part * block + span)
            band = split_dot(grad_feats[row, here], table, dot_nt)
            scores = (pltpu.roll(band, 0, 1, stride=1, stride_axis=0) * scaling).astype(BF16)
            grad_left[row, here] = dot(scores, window[there]).astype(BF16)
            grad_window[there] += dot_tn(scores, left[row, here])
        back[row] = grad_window[0:DISP].astype(BF16)
        own[row] = grad_window[DISP : DISP + cols]


def pairings(count):
    first = [(2 * k, 2 * k + 1) for k in range(count // 2)]
    second = [(2 * k + 1, 2 * k + 2) for k in range(count // 2 - 1)]
    both = lambda pairs: pairs + [(b, a) for a, b in pairs]
    return both(first), both(second)


def exchanged(value, axis):
    first, second = pairings(lax.axis_size(axis))
    return lax.ppermute(value, axis, first), lax.ppermute(value, axis, second)


def exchanged_pair(value_a, value_b, axis):
    first, second = pairings(lax.axis_size(axis))
    return lax.ppermute(value_a, axis, first), lax.ppermute(value_b, axis, second)


def core_groups():
    devices = lax.axis_size("rows") * lax.axis_size("cols")
    return [[i for i in range(devices) if i % 2 == c] for c in range(2)]


def shared_out(kept, given, axes):
    got = swapped(given)
    half = (kept.astype(F32) + got.astype(F32)).astype(BF16)
    half = half.reshape(len(core_groups()[0]), -1, LANES)
    return lax.all_to_all(half, axes, 0, 0, tiled=True, axis_index_groups=core_groups())


def gathered(pieces, axes):
    piece = jnp.sum(pieces.astype(F32), axis=0).astype(BF16)
    spread = jnp.broadcast_to(piece[None], pieces.shape)
    half = lax.all_to_all(spread, axes, 0, 0, tiled=True, axis_index_groups=core_groups())
    return half.reshape(-1, LANES)


def swapped(value):
    return lax.ppermute(value, "cols", [(i, i ^ 1) for i in range(lax.axis_size("cols"))])


def on_device(
    fmap_left,
    fmap_right,
    hidden_init,
    disp_init,
    level_offset,
    motion_weight,
    gate_weight,
    cand_weight,
    grad_hidden,
):
    rows, cols, channels = fmap_left.shape
    wide = cols + 2 * HALO
    state = hidden_init.shape[2]
    feats_count = motion_weight.shape[0]
    rows_axis, cols_axis = lax.axis_size("rows"), lax.axis_size("cols")
    rows_index, cols_index = lax.axis_index("rows"), lax.axis_index("cols")
    place = jnp.stack([rows_index, cols_index]).astype(jnp.int32)

    halos = packed(fmap_left, fmap_right, hidden_init, grad_hidden)
    maps_a, maps_b = exchanged(halos, "cols")
    init_a, init_b = exchanged(hidden_init, "rows")
    motion_w = jnp.pad(motion_weight, ((0, LANES - feats_count), (0, 0)))
    gate_wt = jnp.transpose(gate_weight.reshape(3, 3, 2 * state, 2 * state), (0, 1, 3, 2)).reshape(-1, 2 * state)
    cand_wt = jnp.transpose(cand_weight.reshape(3, 3, 2 * state, state), (0, 1, 3, 2)).reshape(-1, 2 * state)
    motion_w, gate_wt, cand_wt = lax.optimization_barrier((motion_w, gate_wt, cand_wt))

    field = lambda count, dtype: array((count, wide, LANES), dtype)
    band_flops = 2 * rows * wide * 512 * channels
    motion, motion_pre, feats, hidden, grads = kernel_call(
        motion_kernel,
        [array((2, wide + 2 * HALO, LANES), BF16), field(2, F32), field(2, BF16), field(2, BF16), field(2, BF16)],
        [place, disp_init, level_offset, fmap_left, fmap_right, maps_a, maps_b, motion_w, hidden_init, grad_hidden],
        3,
        [pltpu.VMEM((wide, channels), BF16), pltpu.VMEM((768, channels), BF16), pltpu.VMEM((832, channels), BF16)],
        2 * band_flops,
    )
    motion, init_a, init_b = lax.optimization_barrier((motion, init_a, init_b))
    motions = (motion, *exchanged(motion, "rows"))
    unit = 2 * wide * 9 * 2 * state * state
    fields = [pltpu.VMEM((6, wide, 6 * LANES), BF16), pltpu.VMEM((4, wide, 6 * LANES), BF16)]

    hidden_1, update_0, reset_0, reset_hidden_0, candidate_0, hiddens_0 = kernel_call(
        lambda *refs: first_kernel(cols_axis, *refs),
        [field(2, BF16), field(4, F32), field(4, F32), field(4, BF16), field(2, F32), field(4, BF16)],
        [place, hidden, init_a, init_b, *motions, gate_weight, cand_weight],
        1,
        fields,
        10 * unit,
    )
    hidden_1a, hidden_1b = exchanged(hidden_1, "rows")
    update_1, reset_1, reset_hidden_1, grad_cand_1, grad_update_1, send_a, send_b = kernel_call(
        second_kernel,
        [field(4, F32), field(4, F32), field(4, BF16), field(2, BF16), field(2, BF16), field(3, BF16), field(3, BF16)],
        [place, hidden_1, hidden_1a, hidden_1b, *motions, gate_weight, cand_weight, grads],
        1,
        fields,
        10 * unit,
    )
    got_a, got_b = exchanged_pair(send_a, send_b, "rows")
    pixels = pltpu.VMEM((4 * wide, 2 * LANES), BF16)
    taps = pltpu.VMEM((2 * wide, 3 * LANES), BF16)
    weights = array(cand_weight.shape, F32)
    cand_sum, update_sum = kernel_call(
        second_weights_kernel,
        [weights, weights],
        [place, reset_hidden_1, hidden_1, hidden_1a, hidden_1b, *motions, grad_cand_1, grad_update_1],
        1,
        [pixels, taps],
        4 * unit,
    )
    got_a, got_b, cand_sum, update_sum = lax.optimization_barrier((got_a, got_b, cand_sum, update_sum))
    back_scratch = [
        pltpu.VMEM((6, wide, 3 * LANES), BF16),
        pltpu.VMEM((4, wide, 6 * LANES), BF16),
        pltpu.VMEM((4, wide, LANES), F32),
    ]
    grad_reset_1, grad_state, grad_motion_1, grad_cand_0, grad_update_0, send_a, send_b = kernel_call(
        lambda *refs: later_back_kernel(cols_axis, *refs),
        [field(2, BF16), field(2, F32), field(2, F32), field(2, BF16), field(2, BF16),
         field(3, BF16), field(3, BF16)],
        [place, grad_cand_1, got_a, got_b, grad_update_1, hidden_1, hidden_1a, hidden_1b, reset_1, cand_wt, gate_wt,
         update_1, grads, hiddens_0, update_0, candidate_0],
        1,
        back_scratch,
        8 * unit,
    )
    got_a, got_b = exchanged_pair(send_a, send_b, "rows")
    cand_sum, update_sum, reset_sum = kernel_call(
        first_weights_kernel,
        [weights, weights, weights],
        [place, reset_hidden_0, hiddens_0, hidden_1, hidden_1a, hidden_1b, *motions,
         grad_cand_0, grad_update_0, grad_reset_1, cand_sum, update_sum],
        1,
        [pixels, taps],
        6 * unit,
    )
    got_a, got_b, cand_sum, update_sum, reset_sum = lax.optimization_barrier(
        (got_a, got_b, cand_sum, update_sum, reset_sum)
    )
    grad_reset_0, grad_first, grad_feats, motion_sum = kernel_call(
        first_back_kernel,
        [field(2, BF16), array((2, cols, LANES), BF16), array((2, cols, LANES), F32), array((LANES, LANES), F32)],
        [place, grad_cand_0, got_a, got_b, grad_update_0, hiddens_0, reset_0, cand_wt, gate_wt,
         update_0, grad_state, grad_motion_1, motion_pre, feats, motion_w],
        1,
        back_scratch + [pltpu.VMEM((2, wide, LANES), F32)],
        8 * unit,
    )
    total = rows_axis * cols_axis * CHUNK_ROWS
    kept, given = kernel_call(
        last_weights_kernel,
        [array((total // 2, LANES), BF16), array((total // 2, LANES), BF16)],
        [place, hiddens_0, *motions, grad_reset_0, reset_sum, update_sum, cand_sum, motion_sum],
        1,
        [pixels, taps, pltpu.VMEM((2, total // 2, LANES), BF16)],
        2 * unit,
    )
    grad_left, back, own = kernel_call(
        band_back_kernel,
        [array((2, cols, channels), BF16), array((2, DISP, channels), BF16), array((2, cols, channels), F32)],
        [place, disp_init, level_offset, fmap_left, fmap_right, maps_a, maps_b, grad_feats],
        3,
        [pltpu.VMEM((768, channels), BF16), pltpu.VMEM((768, channels), F32)],
        3 * band_flops,
    )
    pieces = shared_out(kept, given, ("rows", "cols"))
    pieces, grad_left, back, own = lax.optimization_barrier((pieces, grad_left, back, own))
    back_a, back_b = exchanged(back, "cols")
    (grad_right,) = kernel_call(
        right_kernel, [array((2, cols, channels), BF16)], [place, own, back_a, back_b], 1, [], 0
    )
    half = gathered(pieces, ("rows", "cols"))
    half, grad_right = lax.optimization_barrier((half, grad_right))
    normaliser = 1.0 / math.sqrt(rows * rows_axis * cols * cols_axis)
    other = swapped(half)
    depth = cand_weight.shape[0]
    results = [array(gate_weight.shape, F32), array(cand_weight.shape, F32)]
    own_parts = half_call(
        lambda *refs: own_half_kernel(normaliser, *refs), place, [half], results, depth, {}
    )
    other, *own_parts = lax.optimization_barrier((other, *own_parts))
    grad_motion_w, grad_gate_w, grad_cand_w = half_call(
        lambda *refs: other_half_kernel(normaliser, *refs), place, [half, other, *own_parts],
        [array((feats_count, LANES), F32)] + results, depth, {3: 1, 4: 2},
    )
    return (grad_left, grad_right, grad_first, grad_motion_w, grad_gate_w, grad_cand_w)


def solution(mesh):
    in_specs = (
        P("rows", "cols", None),
        P("rows", "cols", None),
        P("rows", "cols", None),
        P("rows"),
        P("rows", None),
        P(),
        P(),
        P(),
        P("rows", "cols", None),
    )
    out_specs = (
        P("rows", "cols", None),
        P("rows", "cols", None),
        P("rows", "cols", None),
        P(),
        P(),
        P(),
    )
    return jax.shard_map(
        on_device, mesh=mesh, in_specs=in_specs, out_specs=out_specs, check_vma=False
    )
```

```python
import math

import jax
import jax.numpy as jnp
from jax import lax
from jax.experimental import pallas as pl
from jax.experimental.pallas import tpu as pltpu
from jax.sharding import PartitionSpec as P

LEVELS = 4
RADIUS = 4
DISP = 192
TAPS = 2 * RADIUS + 1
HALO = 16
LANES = 128
SPLIT = 2
CHUNK_ROWS = 56

BF16 = jnp.bfloat16
F32 = jnp.float32
VMEM = pl.BlockSpec(memory_space=pltpu.VMEM)
SMEM = pl.BlockSpec(memory_space=pltpu.SMEM)


def dot(a, b):
    return jnp.dot(a, b, preferred_element_type=F32)


def dot_nt(a, b):
    return lax.dot_general(a, b, (((1,), (1,)), ((), ())), preferred_element_type=F32)


def dot_tn(a, b):
    return lax.dot_general(a, b, (((0,), (0,)), ((), ())), preferred_element_type=F32)


def split_dot(a, table, contract):
    high = a.astype(BF16)
    low = (a - high.astype(F32)).astype(BF16)
    return contract(high, table) + contract(low, table)


def kernel_call(body, outs, ins, scalars, scratch, flops):
    bytes_moved = sum(math.prod(x.shape) * x.dtype.itemsize for x in (*ins, *outs))
    held = sum(math.prod(x.shape) * jnp.dtype(x.dtype).itemsize for x in scratch)
    return pl.pallas_call(
        body,
        out_shape=outs,
        in_specs=[SMEM] * scalars + [VMEM] * (len(ins) - scalars),
        out_specs=[VMEM] * len(outs),
        scratch_shapes=scratch,
        compiler_params=pltpu.CompilerParams(vmem_limit_bytes=bytes_moved + held + 4 * 2**20),
        cost_estimate=pl.CostEstimate(flops=flops, bytes_accessed=bytes_moved, transcendentals=0),
    )(*ins)


def array(shape, dtype):
    return jax.ShapeDtypeStruct(shape, dtype)


def lookup_rows(position, valid, disparity, offsets, row):
    count = position.shape[0]
    feature = lax.broadcasted_iota(jnp.int32, (count, LANES), 1)
    table = jnp.zeros((count, LANES), F32)
    for level in range(LEVELS):
        centre = (disparity[row] >> level) + offsets[row, level]
        tap = feature - level * TAPS
        matches = (position >> level) == tap + (centre - RADIUS)
        matches = matches & (tap >= 0) & (tap < TAPS) & valid
        table = jnp.where(matches, 1.0 / 2**level, table)
    return table.astype(BF16)


def sides(odd, first, second):
    return jnp.where(odd, first, second), jnp.where(odd, second, first)


def store_taps(ref, row, lane, step, value, forward):
    wide = value.shape[0]
    left = pltpu.roll(value, 1, 0).astype(BF16)
    right = pltpu.roll(value, wide - 1, 0).astype(BF16)
    taps = (left, value.astype(BF16), right) if forward else (right, value.astype(BF16), left)
    for tap in range(3):
        start = lane + tap * step
        ref[row, :, start : start + LANES] = taps[tap]


def pack_kernel(left, right, hidden, grads, out, sems):
    cols = left.shape[1]
    tail = DISP + HALO
    first, last = pl.ds(0, HALO), pl.ds(cols - HALO, HALO)
    low, high = pl.ds(0, LANES), pl.ds(LANES, LANES)
    every = pl.ds(0, 2 * LANES)
    moves = (
        (right, pl.ds(cols - tail, tail), pl.ds(0, tail), every),
        (left, last, pl.ds(tail, HALO), every),
        (left, first, pl.ds(tail + HALO, HALO), every),
        (right, first, pl.ds(tail + 2 * HALO, HALO), every),
        (hidden, last, pl.ds(tail + 3 * HALO, HALO), low),
        (hidden, first, pl.ds(tail + 3 * HALO, HALO), high),
        (grads, last, pl.ds(tail + 4 * HALO, HALO), low),
        (grads, first, pl.ds(tail + 4 * HALO, HALO), high),
    )
    copies = [
        pltpu.make_async_copy(source.at[:, start], out.at[:, stop, lanes], sems.at[number])
        for number, (source, start, stop, lanes) in enumerate(moves)
    ]
    for copy in copies:
        copy.start()
    for copy in copies:
        copy.wait()


def packed(left, right, hidden, grads):
    rows, cols, channels = left.shape
    count = DISP + 6 * HALO
    return pl.pallas_call(
        pack_kernel,
        out_shape=array((rows, count, channels), BF16),
        in_specs=[pl.BlockSpec(memory_space=pltpu.HBM)] * 4,
        out_specs=VMEM,
        scratch_shapes=[pltpu.SemaphoreType.DMA((8,))],
        compiler_params=pltpu.CompilerParams(vmem_limit_bytes=56 * 2**20),
        cost_estimate=pl.CostEstimate(flops=0, bytes_accessed=4 * rows * count * channels, transcendentals=0),
    )(left, right, hidden, grads)


def spread_half(core, half, scale, gate, cand, gate_part, cand_part, sems):
    depth = gate_part.shape[0]
    count = cand_part.shape[0]
    block = depth // 4
    lanes = pl.ds(pl.multiple_of(core * LANES, LANES), LANES)
    copies = []
    for number in range(4):
        here = pl.ds(number * block, block)
        gate_part[here] = half[here].astype(F32) * scale
        copies.append(pltpu.make_async_copy(gate_part.at[here], gate.at[here, lanes], sems.at[number]))
        copies[-1].start()
    cand_part[...] = half[depth : depth + count].astype(F32) * scale
    there = pl.ds(pl.multiple_of(core * count, LANES), count)
    copies.append(pltpu.make_async_copy(cand_part, cand.at[there], sems.at[4]))
    copies[-1].start()
    for copy in copies:
        copy.wait()


def own_half_kernel(scale, place, half, gate, cand, gate_part, cand_part, sems):
    spread_half(place[1] % 2, half, scale, gate, cand, gate_part, cand_part, sems)


def other_half_kernel(scale, place, half, other, gate_in, cand_in, motion, gate, cand, gate_part, cand_part, sems):
    core = place[1] % 2
    start = gate_part.shape[0] + cand_part.shape[0]
    rows = pl.ds(start, motion.shape[0])
    motion[...] = jnp.where(core == 0, half[rows], other[rows]).astype(F32) * scale
    spread_half(1 - core, other, scale, gate, cand, gate_part, cand_part, sems)


def half_call(body, place, arrays, outs, depth, aliases):
    anywhere = pl.BlockSpec(memory_space=pltpu.HBM)
    return pl.pallas_call(
        body,
        out_shape=outs,
        in_specs=[SMEM] + [VMEM] * (len(arrays) - len(aliases)) + [anywhere] * len(aliases),
        out_specs=[VMEM] * (len(outs) - 2) + [anywhere] * 2,
        scratch_shapes=[
            pltpu.VMEM((depth, LANES), F32), pltpu.VMEM((depth // 2, LANES), F32), pltpu.SemaphoreType.DMA((5,))
        ],
        input_output_aliases=aliases,
        compiler_params=pltpu.CompilerParams(vmem_limit_bytes=12 * 2**20),
        cost_estimate=pl.CostEstimate(flops=0, bytes_accessed=6 * depth * LANES, transcendentals=0),
    )(place, *arrays)


def motion_kernel(place, disparity, offsets, left, right, got_a, got_b, weight, hidden, grads,
                  motion, pre, feats, hidden_ext, grads_ext, ext, window, flipped):
    odd = place[1] % 2 == 1
    cols = left.shape[1]
    wide = cols + 2 * HALO
    block = wide // 2
    span = 512
    tail = DISP + HALO
    flat = (lax.broadcasted_iota(jnp.int32, (LANES, LANES), 0)
            + lax.broadcasted_iota(jnp.int32, (LANES, LANES), 1))
    mirror = jnp.where(flat == LANES - 1, 1.0, 0.0).astype(BF16)
    total = window.shape[0]
    position = lax.broadcasted_iota(jnp.int32, (span, LANES), 0) - (block - 1)
    valid = (position >= 0) & (position < DISP)
    for row in range(2):
        from_left, from_right = sides(odd, got_a[row], got_b[row])
        state, last = tail + 3 * HALO, HALO + cols
        hidden_ext[row, 0:HALO] = from_left[state : state + HALO, :LANES]
        hidden_ext[row, HALO:last] = hidden[row]
        hidden_ext[row, last:] = from_right[state : state + HALO, LANES:]
        grads_ext[row, 0:HALO] = from_left[state + HALO :, :LANES]
        grads_ext[row, HALO:last] = grads[row]
        grads_ext[row, last:] = from_right[state + HALO :, LANES:]
        motion[row, wide : wide + HALO] = from_left[state : state + HALO, :LANES]
        motion[row, wide + HALO :] = from_right[state : state + HALO, LANES:]
        ext[0:HALO] = from_left[tail : tail + HALO]
        ext[HALO : HALO + cols] = left[row]
        ext[HALO + cols : wide] = from_right[tail + HALO : tail + 2 * HALO]
        window[0:tail] = from_left[0:tail]
        window[tail : tail + cols] = right[row]
        window[tail + cols : tail + cols + HALO] = from_right[tail + 2 * HALO : tail + 3 * HALO]
        window[tail + cols + HALO :] = jnp.zeros((total - tail - cols - HALO, window.shape[1]), BF16)
        parts = total // LANES
        for part in range(parts):
            source = window[(parts - 1 - part) * LANES : (parts - part) * LANES]
            flipped[part * LANES : (part + 1) * LANES] = dot(mirror, source).astype(BF16)
        flipped[total:] = jnp.zeros((flipped.shape[0] - total, window.shape[1]), BF16)
        table = lookup_rows(position, valid, disparity, offsets, row)
        for part in range(2):
            start = part * block
            base = total - DISP - start - block
            scores = dot_nt(ext[start : start + block], flipped[base : base + span])
            scores = scores * (1.0 / math.sqrt(left.shape[2]))
            band = pltpu.roll(scores, 0, 1, stride=1, stride_axis=0)
            found = split_dot(band, table, dot).astype(BF16)
            value = dot(found, weight[...])
            feats[row, start : start + block] = found
            pre[row, start : start + block] = value
            motion[row, start : start + block] = (value * jax.nn.sigmoid(value)).astype(BF16)


def image_columns(place, wide, cols, cols_axis):
    column = lax.broadcasted_iota(jnp.int32, (wide, LANES), 0) - HALO + place[1] * cols
    return (column >= 0) & (column < cols * cols_axis)


def fill_neighbours(store, odd, first, second, wide):
    for row in range(2):
        above, below = sides(odd, first[row, :wide], second[row, :wide])
        store(row, above.astype(F32))
        store(4 + row, below.astype(F32))


def own_products(partial, taps, weights, source):
    deep = weights.shape[0] // 3
    block = partial.shape[1] // SPLIT
    for step in range(4 * SPLIT):
        row, start = step // SPLIT, (step % SPLIT) * block
        here = pl.ds(start, block)
        partial[row, here] = sum(
            dot(taps[source(row, a), here], weights[a * deep : (a + 1) * deep])
            for a in range(3)
            if source(row, a) in (0, 1)
        )


def own_gates_kernel(hidden, motion, gate_w, taps, partial):
    wide = hidden.shape[1]
    for row in range(2):
        store_taps(taps, row, 0, 2 * LANES, hidden[row].astype(F32), True)
        store_taps(taps, row, LANES, 2 * LANES, motion[row, :wide].astype(F32), True)
    own_products(partial, taps, gate_w, lambda row, a: row + a - 2)


def own_cand_kernel(grad_cand, cand_wt, partial, taps):
    for row in range(2):
        store_taps(taps, row, 0, LANES, grad_cand[row].astype(F32), False)
    own_products(partial, taps, cand_wt, lambda row, a: row - a)


def gates(fields, own, partial, resets, gate_w, update, reset, reset_hidden, wide):
    block = wide // SPLIT
    deep = gate_w.shape[0] // 3
    six = [fields.at[0], fields.at[1], own.at[0], own.at[1], fields.at[4], fields.at[5]]
    for step in range(4 * SPLIT):
        row, start = step // SPLIT, (step % SPLIT) * block
        here = pl.ds(start, block)
        total = partial[row, here] + sum(
            dot(six[row + a][here], gate_w[a * deep : (a + 1) * deep])
            for a in range(3)
            if row + a not in (2, 3)
        )
        reset_part = jax.nn.sigmoid(total[:, LANES:])
        update[row, here] = jax.nn.sigmoid(total[:, :LANES])
        reset[row, here] = reset_part
        hidden = six[row + 1][here, 2 * LANES : 3 * LANES].astype(F32)
        reset_hidden[row, here] = (reset_part * hidden).astype(BF16)
    for row in range(4):
        store_taps(resets, row, 0, 2 * LANES, reset_hidden[row].astype(F32), True)
        for tap in range(3):
            start = (2 * tap + 1) * LANES
            resets[row, :, start : start + LANES] = six[row + 1][:, start : start + LANES]


def load_field(odd, fields, lane, first, second):
    wide = fields.shape[1]
    fill_neighbours(lambda r, v: store_taps(fields, r, lane, 2 * LANES, v, True), odd, first, second, wide)


def candidate_part(resets, cand_w, row, here):
    deep = cand_w.shape[0] // 3
    total = sum(dot(resets[row + a, here], cand_w[a * deep : (a + 1) * deep]) for a in range(3))
    return jnp.tanh(total)


def first_kernel(cols_axis, place, hidden, init_a, init_b, motion_a, motion_b, gate_w, cand_w, own, partial,
                 later, update, reset, reset_hidden, candidate, hiddens, fields, resets):
    odd = place[0] % 2 == 1
    wide = hidden.shape[1]
    block = wide // SPLIT
    load_field(odd, fields, LANES, motion_a, motion_b)
    for row in range(2):
        got_a, got_b = (
            jnp.concatenate(
                [sent[row, wide : wide + HALO], inner[row], sent[row, wide + HALO :]], axis=0
            )
            for sent, inner in ((motion_a, init_a), (motion_b, init_b))
        )
        above, below = sides(odd, got_a, got_b)
        for there, value in ((row, above), (4 + row, below)):
            store_taps(fields, there, 0, 2 * LANES, value.astype(F32), True)
            if 0 < there < 5:
                hiddens[there - 1] = value
        hiddens[1 + row] = hidden[row]
    gates(fields, own, partial, resets, gate_w, update, reset, reset_hidden, wide)
    inside = image_columns(place, wide, wide - 2 * HALO, cols_axis)
    for row in range(2):
        for start in range(0, wide, block):
            here = pl.ds(start, block)
            new = candidate_part(resets, cand_w, row, here)
            candidate[row, here] = new
            gate = update[row + 1, here]
            old = hidden[row, here].astype(F32)
            value = (1.0 - gate) * old + gate * new
            later[row, here] = jnp.where(inside[start : start + block], value, 0.0).astype(BF16)


def gradients_out(grad, gate, new, old, row, here, grad_cand, grad_update, send_a, send_b):
    cand_part = (grad * gate * (1.0 - new * new)).astype(BF16)
    grad_cand[row, here] = cand_part
    send_a[row, here] = cand_part
    send_b[row, here] = cand_part
    grad_update[row, here] = (grad * (new - old) * gate * (1.0 - gate)).astype(BF16)


def send_updates(odd, grad_update, send_a, send_b):
    send_a[2], send_b[2] = sides(odd, grad_update[0], grad_update[1])


def second_kernel(place, hidden, hidden_a, hidden_b, motion_a, motion_b, gate_w, cand_w, own, partial, grad_hidden,
                  update, reset, reset_hidden, grad_cand, grad_update, send_a, send_b, fields, resets):
    odd = place[0] % 2 == 1
    wide = hidden.shape[1]
    block = wide // SPLIT
    load_field(odd, fields, LANES, motion_a, motion_b)
    load_field(odd, fields, 0, hidden_a, hidden_b)
    gates(fields, own, partial, resets, gate_w, update, reset, reset_hidden, wide)
    for row in range(2):
        for start in range(0, wide, block):
            here = pl.ds(start, block)
            new = candidate_part(resets, cand_w, row, here)
            gradients_out(grad_hidden[row, here].astype(F32), update[row + 1, here], new,
                          hidden[row, here].astype(F32), row, here, grad_cand, grad_update, send_a, send_b)
    send_updates(odd, grad_update, send_a, send_b)


def back_step(place, partial, grad_a, grad_b, grad_update, hiddens, reset, cand_wt, gate_wt,
              grad_reset, cand_taps, gate_taps, inner, grad_motion, finish):
    odd = place[0] % 2 == 1
    wide = partial.shape[1]
    block = wide // SPLIT
    fill_neighbours(lambda r, v: store_taps(cand_taps, r, 0, LANES, v, False), odd, grad_a, grad_b, wide)
    deep = cand_wt.shape[0] // 3
    deeper = gate_wt.shape[0] // 3

    for step in range(4 * SPLIT):
        row, start = step // SPLIT, (step % SPLIT) * block
        here = pl.ds(start, block)
        total = partial[row, here] + sum(
            dot(cand_taps[row + 2 - a, here], cand_wt[a * deep : (a + 1) * deep])
            for a in range(3)
            if row - a not in (0, 1)
        )
        inner[row, here] = total[:, :LANES]
        if row in (1, 2):
            grad_motion[row - 1, here] = total[:, LANES:]
    above_u, below_u = sides(odd, grad_a[2], grad_b[2])
    updates = (above_u, grad_update[0], grad_update[1], below_u)
    for row in range(4):
        gate = reset[row]
        value = (inner[row] * hiddens[row].astype(F32) * gate * (1.0 - gate)).astype(BF16)
        store_taps(gate_taps, row, 0, 2 * LANES, updates[row].astype(F32), False)
        store_taps(gate_taps, row, LANES, 2 * LANES, value.astype(F32), False)
        if row in (1, 2):
            grad_reset[row - 1] = value
    for row in range(2):
        for start in range(0, wide, block):
            here = pl.ds(start, block)
            total = sum(
                dot(gate_taps[row + 2 - a, here], gate_wt[a * deeper : (a + 1) * deeper]) for a in range(3)
            )
            grad_motion[row, here] += total[:, LANES:]
            finish(row, start, here, inner[row + 1, here] * reset[row + 1, here] + total[:, :LANES])


def later_back_kernel(cols_axis, place, partial, grad_a, grad_b, grad_update, hidden, hidden_a, hidden_b, reset,
                      cand_wt, gate_wt, update, grad_hidden, older_hiddens, older_update, older_candidate,
                      grad_reset, grad_state, grad_motion, older_cand, older_upd, send_a, send_b,
                      cand_taps, gate_taps, inner):
    odd = place[0] % 2 == 1
    wide = hidden.shape[1]
    block = wide // SPLIT
    inside = image_columns(place, wide, wide - 2 * HALO, cols_axis)

    def finish(row, start, here, terms):
        gate = update[row + 1, here]
        grad = grad_hidden[row, here].astype(F32) * (1.0 - gate) + terms
        grad = jnp.where(inside[start : start + block], grad, 0.0)
        grad_state[row, here] = grad
        gradients_out(grad, older_update[row + 1, here], older_candidate[row, here],
                      older_hiddens[row + 1, here].astype(F32), row, here, older_cand, older_upd, send_a, send_b)

    hiddens = hidden_rows(odd, hidden, hidden_a, hidden_b)
    back_step(place, partial, grad_a, grad_b, grad_update, hiddens, reset, cand_wt, gate_wt,
              grad_reset, cand_taps, gate_taps, inner, grad_motion, finish)
    send_updates(odd, older_upd, send_a, send_b)


def first_back_kernel(place, partial, grad_a, grad_b, grad_update, hiddens, reset,
                      cand_wt, gate_wt, update, grad_state, motion_so_far, pre, feats, weight,
                      grad_reset, grad_first, grad_feats, motion_w, cand_taps, gate_taps, inner, grad_motion):
    def finish(row, start, here, terms):
        gate = update[row + 1, here]
        grad = grad_state[row, here] * (1.0 - gate) + terms
        first, last = max(start, HALO), min(start + grad.shape[0], HALO + grad_first.shape[1])
        grad_first[row, first - HALO : last - HALO] = grad[first - start : last - start].astype(BF16)
        grad_motion[row, here] += motion_so_far[row, here]

    back_step(place, partial, grad_a, grad_b, grad_update, hiddens, reset, cand_wt, gate_wt,
              grad_reset, cand_taps, gate_taps, inner, grad_motion, finish)
    inner_cols = slice(HALO, HALO + grad_feats.shape[1])
    total = jnp.zeros((LANES, LANES), F32)
    for row in range(2):
        value = pre[row, inner_cols]
        gate = jax.nn.sigmoid(value)
        slope = gate * (1.0 + value * (1.0 - gate))
        grad_pre = (grad_motion[row, inner_cols] * slope).astype(BF16)
        total = total + dot_tn(feats[row, inner_cols], grad_pre)
        grad_feats[row] = dot_nt(grad_pre, weight[...])
    motion_w[...] = total


def load_pixels(odd, pixels, hiddens, motion, motion_a, motion_b):
    wide = pixels.shape[0] // 4
    for row, value in enumerate(hidden_rows(odd, motion, motion_a, motion_b)):
        pixels[row * wide : (row + 1) * wide, LANES:] = value[:wide]
    for row, value in enumerate(hiddens):
        pixels[row * wide : (row + 1) * wide, :LANES] = value


def load_grads(taps, grads):
    wide = grads.shape[1]
    column = lax.broadcasted_iota(jnp.int32, (wide, LANES), 0)
    own = (column >= HALO) & (column < wide - HALO)
    depth = grads.shape[2]
    for row in range(2):
        for part in range(depth // LANES):
            value = jnp.where(own, grads[row, :, part * LANES : (part + 1) * LANES].astype(F32), 0.0)
            shifted = (pltpu.roll(value, wide - 1, 0), value, pltpu.roll(value, 1, 0))
            for tap in range(3):
                start = tap * depth + part * LANES
                taps[row * wide : (row + 1) * wide, start : start + LANES] = shifted[tap].astype(BF16)


def weight_products(pixels, taps, wide, depth, finish):
    for a in range(3):
        total = dot_tn(pixels[a * wide : (a + 2) * wide], taps[...])
        for b in range(3):
            finish((3 * a + b) * 2 * LANES, total[:, b * depth : (b + 1) * depth])


def hidden_rows(odd, hidden, hidden_a, hidden_b):
    above, below = sides(odd, hidden_a[1], hidden_b[1])[0], sides(odd, hidden_a[0], hidden_b[0])[1]
    return (above, hidden[0], hidden[1], below)


def load_hidden(pixels, rows, wide):
    for row, value in enumerate(rows):
        pixels[row * wide : (row + 1) * wide, :LANES] = value


def second_weights_kernel(place, resets, hidden, hidden_a, hidden_b, motion, motion_a, motion_b, cand_grads, update_grads,
                          cand_out, update_out, pixels, taps):
    odd = place[0] % 2 == 1
    wide = taps.shape[0] // 2
    load_pixels(odd, pixels, [resets[row] for row in range(4)], motion, motion_a, motion_b)
    load_grads(taps, cand_grads)

    def cand_finish(start, value):
        cand_out[pl.ds(start, 2 * LANES)] = value

    def update_finish(start, value):
        update_out[pl.ds(start, 2 * LANES)] = value

    weight_products(pixels, taps, wide, LANES, cand_finish)
    load_hidden(pixels, hidden_rows(odd, hidden, hidden_a, hidden_b), wide)
    load_grads(taps, update_grads)
    weight_products(pixels, taps, wide, LANES, update_finish)


def first_weights_kernel(place, resets, older, hidden, hidden_a, hidden_b, motion, motion_a, motion_b,
                         cand_grads, update_grads, reset_grads, cand_sum, update_sum,
                         cand_out, update_out, reset_out, pixels, taps):
    odd = place[0] % 2 == 1
    wide = taps.shape[0] // 2
    load_pixels(odd, pixels, [resets[row] for row in range(4)], motion, motion_a, motion_b)
    load_grads(taps, cand_grads)

    def cand_finish(start, value):
        here = pl.ds(start, 2 * LANES)
        cand_out[here] = cand_sum[here] + value

    def update_finish(start, value):
        here = pl.ds(start, 2 * LANES)
        update_out[here] = update_sum[here] + value

    def reset_finish(start, value):
        reset_out[pl.ds(start, 2 * LANES)] = value

    weight_products(pixels, taps, wide, LANES, cand_finish)
    load_hidden(pixels, [older[row] for row in range(4)], wide)
    load_grads(taps, update_grads)
    weight_products(pixels, taps, wide, LANES, update_finish)
    load_hidden(pixels, hidden_rows(odd, hidden, hidden_a, hidden_b), wide)
    load_grads(taps, reset_grads)
    weight_products(pixels, taps, wide, LANES, reset_finish)


def last_weights_kernel(place, hiddens, motion, motion_a, motion_b, reset_grads, reset_sum,
                        update_sum, cand_sum, motion_w, kept, given, pixels, taps, parts):
    odd = place[0] % 2 == 1
    load_pixels(odd, pixels, [hiddens[row] for row in range(4)], motion, motion_a, motion_b)
    load_grads(taps, reset_grads)
    rows = cand_sum.shape[0]
    split = rows // 2
    last = rows + split

    def finish(start, value):
        parts[1, start : start + 2 * LANES] = (value + reset_sum[pl.ds(start, 2 * LANES)]).astype(BF16)

    weight_products(pixels, taps, taps.shape[0] // 2, LANES, finish)
    parts[0, 0:rows] = update_sum[...].astype(BF16)
    for half in range(2):
        parts[half, rows:last] = cand_sum[half * split : (half + 1) * split].astype(BF16)
    parts[0, last:] = motion_w[...].astype(BF16)
    parts[1, last:] = jnp.zeros((parts.shape[1] - last, LANES), BF16)
    core = place[1] % 2
    kept[...] = parts[core]
    given[...] = parts[1 - core]


def right_kernel(place, own, back_a, back_b, grad_right):
    odd = place[1] % 2 == 1
    split = own.shape[1] - DISP
    for row in range(2):
        grad_right[row, :split] = own[row, :split].astype(BF16)
        returned = sides(odd, back_a[row], back_b[row])[1].astype(F32)
        grad_right[row, split:] = (own[row, split:] + returned).astype(BF16)


def band_back_kernel(place, disparity, offsets, left, right, got_a, got_b, grad_feats,
                     grad_left, back, own, window, grad_window):
    odd = place[1] % 2 == 1
    cols = left.shape[1]
    block = cols // 2
    span = 512
    scaling = 1.0 / math.sqrt(left.shape[2])
    position = DISP - lax.broadcasted_iota(jnp.int32, (span, LANES), 0)
    valid = (position >= 0) & (position < DISP)
    for row in range(2):
        from_left = sides(odd, got_a[row], got_b[row])[0]
        window[0:DISP] = from_left[HALO : HALO + DISP]
        window[DISP : DISP + cols] = right[row]
        window[DISP + cols :] = jnp.zeros((window.shape[0] - DISP - cols, window.shape[1]), BF16)
        grad_window[...] = jnp.zeros(grad_window.shape, F32)
        table = lookup_rows(position, valid, disparity, offsets, row)
        for part in range(2):
            here = slice(part * block, (part + 1) * block)
            there = slice(part * block, part * block + span)
            band = split_dot(grad_feats[row, here], table, dot_nt)
            scores = (pltpu.roll(band, 0, 1, stride=1, stride_axis=0) * scaling).astype(BF16)
            grad_left[row, here] = dot(scores, window[there]).astype(BF16)
            grad_window[there] += dot_tn(scores, left[row, here])
        back[row] = grad_window[0:DISP].astype(BF16)
        own[row] = grad_window[DISP : DISP + cols]


def pairings(count):
    first = [(2 * k, 2 * k + 1) for k in range(count // 2)]
    second = [(2 * k + 1, 2 * k + 2) for k in range(count // 2 - 1)]
    both = lambda pairs: pairs + [(b, a) for a, b in pairs]
    return both(first), both(second)


def exchanged(value, axis):
    first, second = pairings(lax.axis_size(axis))
    return lax.ppermute(value, axis, first), lax.ppermute(value, axis, second)


def exchanged_pair(value_a, value_b, axis):
    first, second = pairings(lax.axis_size(axis))
    return lax.ppermute(value_a, axis, first), lax.ppermute(value_b, axis, second)


def core_groups():
    devices = lax.axis_size("rows") * lax.axis_size("cols")
    return [[i for i in range(devices) if i % 2 == c] for c in range(2)]


def shared_out(kept, given, axes):
    got = swapped(given)
    half = (kept.astype(F32) + got.astype(F32)).astype(BF16)
    half = half.reshape(len(core_groups()[0]), -1, LANES)
    return lax.all_to_all(half, axes, 0, 0, tiled=True, axis_index_groups=core_groups())


def spread_kernel(pieces, out):
    out[...] = jnp.broadcast_to(jnp.sum(pieces[...].astype(F32), axis=0).astype(BF16)[None], out.shape)


def gathered(pieces, axes):
    (spread,) = kernel_call(spread_kernel, [array(pieces.shape, BF16)], [pieces], 0, [], 0)
    half = lax.all_to_all(spread, axes, 0, 0, tiled=True, axis_index_groups=core_groups())
    return half.reshape(-1, LANES)


def swapped(value):
    return lax.ppermute(value, "cols", [(i, i ^ 1) for i in range(lax.axis_size("cols"))])


def on_device(
    fmap_left,
    fmap_right,
    hidden_init,
    disp_init,
    level_offset,
    motion_weight,
    gate_weight,
    cand_weight,
    grad_hidden,
):
    rows, cols, channels = fmap_left.shape
    wide = cols + 2 * HALO
    state = hidden_init.shape[2]
    feats_count = motion_weight.shape[0]
    rows_axis, cols_axis = lax.axis_size("rows"), lax.axis_size("cols")
    rows_index, cols_index = lax.axis_index("rows"), lax.axis_index("cols")
    place = jnp.stack([rows_index, cols_index]).astype(jnp.int32)

    halos = packed(fmap_left, fmap_right, hidden_init, grad_hidden)
    maps_a, maps_b = exchanged(halos, "cols")
    init_a, init_b = exchanged(hidden_init, "rows")
    motion_w = jnp.pad(motion_weight, ((0, LANES - feats_count), (0, 0)))
    gate_wt = jnp.transpose(gate_weight.reshape(3, 3, 2 * state, 2 * state), (0, 1, 3, 2)).reshape(-1, 2 * state)
    cand_wt = jnp.transpose(cand_weight.reshape(3, 3, 2 * state, state), (0, 1, 3, 2)).reshape(-1, 2 * state)
    motion_w, gate_wt, cand_wt = lax.optimization_barrier((motion_w, gate_wt, cand_wt))

    field = lambda count, dtype: array((count, wide, LANES), dtype)
    band_flops = 2 * rows * wide * 512 * channels
    motion, motion_pre, feats, hidden, grads = kernel_call(
        motion_kernel,
        [array((2, wide + 2 * HALO, LANES), BF16), field(2, F32), field(2, BF16), field(2, BF16), field(2, BF16)],
        [place, disp_init, level_offset, fmap_left, fmap_right, maps_a, maps_b, motion_w, hidden_init, grad_hidden],
        3,
        [pltpu.VMEM((wide, channels), BF16), pltpu.VMEM((768, channels), BF16), pltpu.VMEM((832, channels), BF16)],
        2 * band_flops,
    )
    motion, init_a, init_b = lax.optimization_barrier((motion, init_a, init_b))
    motions = (motion, *exchanged(motion, "rows"))
    unit = 2 * wide * 9 * 2 * state * state
    fields = [pltpu.VMEM((6, wide, 6 * LANES), BF16), pltpu.VMEM((4, wide, 6 * LANES), BF16)]

    field_taps = array((2, wide, 6 * LANES), BF16)
    partials = array((4, wide, 2 * LANES), F32)
    own_taps, partial = kernel_call(
        own_gates_kernel, [field_taps, partials], [hidden, motion, gate_weight], 0, [], 4 * unit
    )
    hidden_1, update_0, reset_0, reset_hidden_0, candidate_0, hiddens_0 = kernel_call(
        lambda *refs: first_kernel(cols_axis, *refs),
        [field(2, BF16), field(4, F32), field(4, F32), field(4, BF16), field(2, F32), field(4, BF16)],
        [place, hidden, init_a, init_b, *motions[1:], gate_weight, cand_weight, own_taps, partial],
        1,
        fields,
        10 * unit,
    )
    hidden_1a, hidden_1b = exchanged(hidden_1, "rows")
    own_taps, partial = kernel_call(
        own_gates_kernel, [field_taps, partials], [hidden_1, motion, gate_weight], 0, [], 4 * unit
    )
    update_1, reset_1, reset_hidden_1, grad_cand_1, grad_update_1, send_a, send_b = kernel_call(
        second_kernel,
        [field(4, F32), field(4, F32), field(4, BF16), field(2, BF16), field(2, BF16), field(3, BF16), field(3, BF16)],
        [place, hidden_1, hidden_1a, hidden_1b, *motions[1:], gate_weight, cand_weight, own_taps, partial, grads],
        1,
        fields,
        10 * unit,
    )
    got_a, got_b = exchanged_pair(send_a, send_b, "rows")
    pixels = pltpu.VMEM((4 * wide, 2 * LANES), BF16)
    taps = pltpu.VMEM((2 * wide, 3 * LANES), BF16)
    weights = array(cand_weight.shape, F32)
    cand_sum, update_sum = kernel_call(
        second_weights_kernel,
        [weights, weights],
        [place, reset_hidden_1, hidden_1, hidden_1a, hidden_1b, *motions, grad_cand_1, grad_update_1],
        1,
        [pixels, taps],
        4 * unit,
    )
    (partial,) = kernel_call(
        own_cand_kernel, [partials], [grad_cand_1, cand_wt], 0, [pltpu.VMEM((2, wide, 3 * LANES), BF16)], 2 * unit
    )
    got_a, got_b, cand_sum, update_sum = lax.optimization_barrier((got_a, got_b, cand_sum, update_sum))
    back_scratch = [
        pltpu.VMEM((6, wide, 3 * LANES), BF16),
        pltpu.VMEM((4, wide, 6 * LANES), BF16),
        pltpu.VMEM((4, wide, LANES), F32),
    ]
    grad_reset_1, grad_state, grad_motion_1, grad_cand_0, grad_update_0, send_a, send_b = kernel_call(
        lambda *refs: later_back_kernel(cols_axis, *refs),
        [field(2, BF16), field(2, F32), field(2, F32), field(2, BF16), field(2, BF16),
         field(3, BF16), field(3, BF16)],
        [place, partial, got_a, got_b, grad_update_1, hidden_1, hidden_1a, hidden_1b, reset_1, cand_wt, gate_wt,
         update_1, grads, hiddens_0, update_0, candidate_0],
        1,
        back_scratch,
        8 * unit,
    )
    got_a, got_b = exchanged_pair(send_a, send_b, "rows")
    cand_sum, update_sum, reset_sum = kernel_call(
        first_weights_kernel,
        [weights, weights, weights],
        [place, reset_hidden_0, hiddens_0, hidden_1, hidden_1a, hidden_1b, *motions,
         grad_cand_0, grad_update_0, grad_reset_1, cand_sum, update_sum],
        1,
        [pixels, taps],
        6 * unit,
    )
    (partial,) = kernel_call(
        own_cand_kernel, [partials], [grad_cand_0, cand_wt], 0, [pltpu.VMEM((2, wide, 3 * LANES), BF16)], 2 * unit
    )
    got_a, got_b, cand_sum, update_sum, reset_sum = lax.optimization_barrier(
        (got_a, got_b, cand_sum, update_sum, reset_sum)
    )
    grad_reset_0, grad_first, grad_feats, motion_sum = kernel_call(
        first_back_kernel,
        [field(2, BF16), array((2, cols, LANES), BF16), array((2, cols, LANES), F32), array((LANES, LANES), F32)],
        [place, partial, got_a, got_b, grad_update_0, hiddens_0, reset_0, cand_wt, gate_wt,
         update_0, grad_state, grad_motion_1, motion_pre, feats, motion_w],
        1,
        back_scratch + [pltpu.VMEM((2, wide, LANES), F32)],
        8 * unit,
    )
    total = rows_axis * cols_axis * CHUNK_ROWS
    kept, given = kernel_call(
        last_weights_kernel,
        [array((total // 2, LANES), BF16), array((total // 2, LANES), BF16)],
        [place, hiddens_0, *motions, grad_reset_0, reset_sum, update_sum, cand_sum, motion_sum],
        1,
        [pixels, taps, pltpu.VMEM((2, total // 2, LANES), BF16)],
        2 * unit,
    )
    grad_left, back, own = kernel_call(
        band_back_kernel,
        [array((2, cols, channels), BF16), array((2, DISP, channels), BF16), array((2, cols, channels), F32)],
        [place, disp_init, level_offset, fmap_left, fmap_right, maps_a, maps_b, grad_feats],
        3,
        [pltpu.VMEM((768, channels), BF16), pltpu.VMEM((768, channels), F32)],
        3 * band_flops,
    )
    pieces = shared_out(kept, given, ("rows", "cols"))
    pieces, grad_left, back, own = lax.optimization_barrier((pieces, grad_left, back, own))
    back_a, back_b = exchanged(back, "cols")
    (grad_right,) = kernel_call(
        right_kernel, [array((2, cols, channels), BF16)], [place, own, back_a, back_b], 1, [], 0
    )
    half = gathered(pieces, ("rows", "cols"))
    half, grad_right = lax.optimization_barrier((half, grad_right))
    normaliser = 1.0 / math.sqrt(rows * rows_axis * cols * cols_axis)
    other = swapped(half)
    depth = cand_weight.shape[0]
    results = [array(gate_weight.shape, F32), array(cand_weight.shape, F32)]
    own_parts = half_call(
        lambda *refs: own_half_kernel(normaliser, *refs), place, [half], results, depth, {}
    )
    other, *own_parts = lax.optimization_barrier((other, *own_parts))
    grad_motion_w, grad_gate_w, grad_cand_w = half_call(
        lambda *refs: other_half_kernel(normaliser, *refs), place, [half, other, *own_parts],
        [array((feats_count, LANES), F32)] + results, depth, {3: 1, 4: 2},
    )
    return (grad_left, grad_right, grad_first, grad_motion_w, grad_gate_w, grad_cand_w)


def solution(mesh):
    in_specs = (
        P("rows", "cols", None),
        P("rows", "cols", None),
        P("rows", "cols", None),
        P("rows"),
        P("rows", None),
        P(),
        P(),
        P(),
        P("rows", "cols", None),
    )
    out_specs = (
        P("rows", "cols", None),
        P("rows", "cols", None),
        P("rows", "cols", None),
        P(),
        P(),
        P(),
    )
    return jax.shard_map(
        on_device, mesh=mesh, in_specs=in_specs, out_specs=out_specs, check_vma=False
    )
```

```python
import math

import jax
import jax.numpy as jnp
from jax import lax
from jax.experimental import pallas as pl
from jax.experimental.pallas import tpu as pltpu
from jax.sharding import PartitionSpec as P

LEVELS = 4
RADIUS = 4
DISP = 192
TAPS = 2 * RADIUS + 1
HALO = 16
LANES = 128
SPLIT = 2
CHUNK_ROWS = 56

BF16 = jnp.bfloat16
F32 = jnp.float32
VMEM = pl.BlockSpec(memory_space=pltpu.VMEM)
SMEM = pl.BlockSpec(memory_space=pltpu.SMEM)


def dot(a, b):
    return jnp.dot(a, b, preferred_element_type=F32)


def dot_nt(a, b):
    return lax.dot_general(a, b, (((1,), (1,)), ((), ())), preferred_element_type=F32)


def dot_tn(a, b):
    return lax.dot_general(a, b, (((0,), (0,)), ((), ())), preferred_element_type=F32)


def split_dot(a, table, contract):
    high = a.astype(BF16)
    low = (a - high.astype(F32)).astype(BF16)
    return contract(high, table) + contract(low, table)


def kernel_call(body, outs, ins, scalars, scratch, flops):
    bytes_moved = sum(math.prod(x.shape) * x.dtype.itemsize for x in (*ins, *outs))
    held = sum(math.prod(x.shape) * jnp.dtype(x.dtype).itemsize for x in scratch)
    return pl.pallas_call(
        body,
        out_shape=outs,
        in_specs=[SMEM] * scalars + [VMEM] * (len(ins) - scalars),
        out_specs=[VMEM] * len(outs),
        scratch_shapes=scratch,
        compiler_params=pltpu.CompilerParams(vmem_limit_bytes=bytes_moved + held + 4 * 2**20),
        cost_estimate=pl.CostEstimate(flops=flops, bytes_accessed=bytes_moved, transcendentals=0),
    )(*ins)


def array(shape, dtype):
    return jax.ShapeDtypeStruct(shape, dtype)


def lookup_rows(position, valid, disparity, offsets, row):
    count = position.shape[0]
    feature = lax.broadcasted_iota(jnp.int32, (count, LANES), 1)
    table = jnp.zeros((count, LANES), F32)
    for level in range(LEVELS):
        centre = (disparity[row] >> level) + offsets[row, level]
        tap = feature - level * TAPS
        matches = (position >> level) == tap + (centre - RADIUS)
        matches = matches & (tap >= 0) & (tap < TAPS) & valid
        table = jnp.where(matches, 1.0 / 2**level, table)
    return table.astype(BF16)


def sides(odd, first, second):
    return jnp.where(odd, first, second), jnp.where(odd, second, first)


def store_taps(ref, row, lane, step, value, forward):
    wide = value.shape[0]
    left = pltpu.roll(value, 1, 0).astype(BF16)
    right = pltpu.roll(value, wide - 1, 0).astype(BF16)
    taps = (left, value.astype(BF16), right) if forward else (right, value.astype(BF16), left)
    for tap in range(3):
        start = lane + tap * step
        ref[row, :, start : start + LANES] = taps[tap]


def pack_kernel(left, right, hidden, grads, out, sems):
    cols = left.shape[1]
    tail = DISP + HALO
    first, last = pl.ds(0, HALO), pl.ds(cols - HALO, HALO)
    low, high = pl.ds(0, LANES), pl.ds(LANES, LANES)
    every = pl.ds(0, 2 * LANES)
    moves = (
        (right, pl.ds(cols - tail, tail), pl.ds(0, tail), every),
        (left, last, pl.ds(tail, HALO), every),
        (left, first, pl.ds(tail + HALO, HALO), every),
        (right, first, pl.ds(tail + 2 * HALO, HALO), every),
        (hidden, last, pl.ds(tail + 3 * HALO, HALO), low),
        (hidden, first, pl.ds(tail + 3 * HALO, HALO), high),
        (grads, last, pl.ds(tail + 4 * HALO, HALO), low),
        (grads, first, pl.ds(tail + 4 * HALO, HALO), high),
    )
    copies = [
        pltpu.make_async_copy(source.at[:, start], out.at[:, stop, lanes], sems.at[number])
        for number, (source, start, stop, lanes) in enumerate(moves)
    ]
    for copy in copies:
        copy.start()
    for copy in copies:
        copy.wait()


def packed(left, right, hidden, grads):
    rows, cols, channels = left.shape
    count = DISP + 6 * HALO
    return pl.pallas_call(
        pack_kernel,
        out_shape=array((rows, count, channels), BF16),
        in_specs=[pl.BlockSpec(memory_space=pltpu.HBM)] * 4,
        out_specs=VMEM,
        scratch_shapes=[pltpu.SemaphoreType.DMA((8,))],
        compiler_params=pltpu.CompilerParams(vmem_limit_bytes=56 * 2**20),
        cost_estimate=pl.CostEstimate(flops=0, bytes_accessed=4 * rows * count * channels, transcendentals=0),
    )(left, right, hidden, grads)


def turn_kernel(gate_w, cand_w, gate_wt, cand_wt):
    for tap in range(9):
        here = slice(tap * 2 * LANES, (tap + 1) * 2 * LANES)
        gate_wt[here] = gate_w[here].T
        cand_wt[tap * LANES : (tap + 1) * LANES] = cand_w[here].T


def spread_half(core, half, scale, gate, cand, parts, sems):
    count = parts.shape[1]
    there = pl.ds(pl.multiple_of(core * count, LANES), count)
    targets = (gate.at[there, pl.ds(0, LANES)], cand.at[there], gate.at[there, pl.ds(LANES, LANES)])
    copies = []
    for number, target in enumerate(targets):
        parts[number] = half[number * count : (number + 1) * count].astype(F32) * scale
        copies.append(pltpu.make_async_copy(parts.at[number], target, sems.at[number]))
        copies[-1].start()
    for copy in copies:
        copy.wait()


def own_half_kernel(scale, place, half, gate, cand, parts, sems):
    spread_half(place[1] % 2, half, scale, gate, cand, parts, sems)


def other_half_kernel(scale, place, half, other, gate_in, cand_in, motion, gate, cand, parts, sems):
    core = place[1] % 2
    start = 3 * parts.shape[1]
    count = motion.shape[0]
    rows = slice(start, start + LANES)
    motion[...] = jnp.where(core == 0, half[rows], other[rows]).astype(F32)[:count] * scale
    spread_half(1 - core, other, scale, gate, cand, parts, sems)


def half_call(body, place, arrays, outs, depth, aliases):
    anywhere = pl.BlockSpec(memory_space=pltpu.HBM)
    return pl.pallas_call(
        body,
        out_shape=outs,
        in_specs=[SMEM] + [VMEM] * (len(arrays) - len(aliases)) + [anywhere] * len(aliases),
        out_specs=[VMEM] * (len(outs) - 2) + [anywhere] * 2,
        scratch_shapes=[
            pltpu.VMEM((3, depth // 2, LANES), F32), pltpu.SemaphoreType.DMA((3,))
        ],
        input_output_aliases=aliases,
        compiler_params=pltpu.CompilerParams(vmem_limit_bytes=12 * 2**20),
        cost_estimate=pl.CostEstimate(flops=0, bytes_accessed=6 * depth * LANES, transcendentals=0),
    )(place, *arrays)


def motion_kernel(place, disparity, offsets, left, right, got_a, got_b, weight, hidden, grads,
                  motion, pre, feats, hidden_ext, grads_ext, ext, window, flipped):
    odd = place[1] % 2 == 1
    cols = left.shape[1]
    wide = cols + 2 * HALO
    block = wide // 2
    span = 512
    tail = DISP + HALO
    flat = (lax.broadcasted_iota(jnp.int32, (LANES, LANES), 0)
            + lax.broadcasted_iota(jnp.int32, (LANES, LANES), 1))
    mirror = jnp.where(flat == LANES - 1, 1.0, 0.0).astype(BF16)
    total = window.shape[0]
    position = lax.broadcasted_iota(jnp.int32, (span, LANES), 0) - (block - 1)
    valid = (position >= 0) & (position < DISP)
    for row in range(2):
        from_left, from_right = sides(odd, got_a[row], got_b[row])
        state, last = tail + 3 * HALO, HALO + cols
        hidden_ext[row, 0:HALO] = from_left[state : state + HALO, :LANES]
        hidden_ext[row, HALO:last] = hidden[row]
        hidden_ext[row, last:] = from_right[state : state + HALO, LANES:]
        grads_ext[row, 0:HALO] = from_left[state + HALO :, :LANES]
        grads_ext[row, HALO:last] = grads[row]
        grads_ext[row, last:] = from_right[state + HALO :, LANES:]
        motion[row, wide : wide + HALO] = from_left[state : state + HALO, :LANES]
        motion[row, wide + HALO :] = from_right[state : state + HALO, LANES:]
        ext[0:HALO] = from_left[tail : tail + HALO]
        ext[HALO : HALO + cols] = left[row]
        ext[HALO + cols : wide] = from_right[tail + HALO : tail + 2 * HALO]
        window[0:tail] = from_left[0:tail]
        window[tail : tail + cols] = right[row]
        window[tail + cols : tail + cols + HALO] = from_right[tail + 2 * HALO : tail + 3 * HALO]
        window[tail + cols + HALO :] = jnp.zeros((total - tail - cols - HALO, window.shape[1]), BF16)
        parts = total // LANES
        for part in range(parts):
            source = window[(parts - 1 - part) * LANES : (parts - part) * LANES]
            flipped[part * LANES : (part + 1) * LANES] = dot(mirror, source).astype(BF16)
        flipped[total:] = jnp.zeros((flipped.shape[0] - total, window.shape[1]), BF16)
        table = lookup_rows(position, valid, disparity, offsets, row)
        for part in range(2):
            start = part * block
            base = total - DISP - start - block
            scores = dot_nt(ext[start : start + block], flipped[base : base + span])
            scores = scores * (1.0 / math.sqrt(left.shape[2]))
            band = pltpu.roll(scores, 0, 1, stride=1, stride_axis=0)
            found = split_dot(band, table, dot).astype(BF16)
            value = dot(found, weight[...])
            feats[row, start : start + block] = found
            pre[row, start : start + block] = value
            motion[row, start : start + block] = (value * jax.nn.sigmoid(value)).astype(BF16)


def image_columns(place, wide, cols, cols_axis):
    column = lax.broadcasted_iota(jnp.int32, (wide, LANES), 0) - HALO + place[1] * cols
    return (column >= 0) & (column < cols * cols_axis)


def fill_neighbours(store, odd, first, second, wide):
    for row in range(2):
        above, below = sides(odd, first[row, :wide], second[row, :wide])
        store(row, above.astype(F32))
        store(4 + row, below.astype(F32))


def own_products(partial, taps, weights, source):
    deep = weights.shape[0] // 3
    block = partial.shape[1] // SPLIT
    for step in range(4 * SPLIT):
        row, start = step // SPLIT, (step % SPLIT) * block
        here = pl.ds(start, block)
        partial[row, here] = sum(
            dot(taps[source(row, a), here], weights[a * deep : (a + 1) * deep])
            for a in range(3)
            if source(row, a) in (0, 1)
        )


def own_gates_kernel(hidden, motion, gate_w, taps, partial):
    wide = hidden.shape[1]
    for row in range(2):
        store_taps(taps, row, 0, 2 * LANES, hidden[row].astype(F32), True)
        store_taps(taps, row, LANES, 2 * LANES, motion[row, :wide].astype(F32), True)
    own_products(partial, taps, gate_w, lambda row, a: row + a - 2)


def own_cand_kernel(grad_cand, cand_wt, partial, taps):
    for row in range(2):
        store_taps(taps, row, 0, LANES, grad_cand[row].astype(F32), False)
    own_products(partial, taps, cand_wt, lambda row, a: row - a)


def gates(fields, own, partial, resets, gate_w, update, reset, reset_hidden, wide):
    block = wide // SPLIT
    deep = gate_w.shape[0] // 3
    six = [fields.at[0], fields.at[1], own.at[0], own.at[1], fields.at[4], fields.at[5]]
    for step in range(4 * SPLIT):
        row, start = step // SPLIT, (step % SPLIT) * block
        here = pl.ds(start, block)
        total = partial[row, here] + sum(
            dot(six[row + a][here], gate_w[a * deep : (a + 1) * deep])
            for a in range(3)
            if row + a not in (2, 3)
        )
        reset_part = jax.nn.sigmoid(total[:, LANES:])
        update[row, here] = jax.nn.sigmoid(total[:, :LANES])
        reset[row, here] = reset_part
        hidden = six[row + 1][here, 2 * LANES : 3 * LANES].astype(F32)
        reset_hidden[row, here] = (reset_part * hidden).astype(BF16)
    for row in range(4):
        store_taps(resets, row, 0, 2 * LANES, reset_hidden[row].astype(F32), True)
        for tap in range(3):
            start = (2 * tap + 1) * LANES
            resets[row, :, start : start + LANES] = six[row + 1][:, start : start + LANES]


def load_field(odd, fields, lane, first, second):
    wide = fields.shape[1]
    fill_neighbours(lambda r, v: store_taps(fields, r, lane, 2 * LANES, v, True), odd, first, second, wide)


def candidate_part(resets, cand_w, row, here):
    deep = cand_w.shape[0] // 3
    total = sum(dot(resets[row + a, here], cand_w[a * deep : (a + 1) * deep]) for a in range(3))
    return jnp.tanh(total)


def first_kernel(cols_axis, place, hidden, init_a, init_b, motion_a, motion_b, gate_w, cand_w, own, partial,
                 later, update, reset, reset_hidden, candidate, hiddens, fields, resets):
    odd = place[0] % 2 == 1
    wide = hidden.shape[1]
    block = wide // SPLIT
    load_field(odd, fields, LANES, motion_a, motion_b)
    for row in range(2):
        got_a, got_b = (
            jnp.concatenate(
                [sent[row, wide : wide + HALO], inner[row], sent[row, wide + HALO :]], axis=0
            )
            for sent, inner in ((motion_a, init_a), (motion_b, init_b))
        )
        above, below = sides(odd, got_a, got_b)
        for there, value in ((row, above), (4 + row, below)):
            store_taps(fields, there, 0, 2 * LANES, value.astype(F32), True)
            if 0 < there < 5:
                hiddens[there - 1] = value
        hiddens[1 + row] = hidden[row]
    gates(fields, own, partial, resets, gate_w, update, reset, reset_hidden, wide)
    inside = image_columns(place, wide, wide - 2 * HALO, cols_axis)
    for row in range(2):
        for start in range(0, wide, block):
            here = pl.ds(start, block)
            new = candidate_part(resets, cand_w, row, here)
            candidate[row, here] = new
            gate = update[row + 1, here]
            old = hidden[row, here].astype(F32)
            value = (1.0 - gate) * old + gate * new
            later[row, here] = jnp.where(inside[start : start + block], value, 0.0).astype(BF16)


def gradients_out(grad, gate, new, old, row, here, grad_cand, grad_update, send_a, send_b):
    cand_part = (grad * gate * (1.0 - new * new)).astype(BF16)
    grad_cand[row, here] = cand_part
    send_a[row, here] = cand_part
    send_b[row, here] = cand_part
    grad_update[row, here] = (grad * (new - old) * gate * (1.0 - gate)).astype(BF16)


def send_updates(odd, grad_update, send_a, send_b):
    send_a[2], send_b[2] = sides(odd, grad_update[0], grad_update[1])


def second_kernel(place, hidden, hidden_a, hidden_b, motion_a, motion_b, gate_w, cand_w, own, partial, grad_hidden,
                  update, reset, reset_hidden, grad_cand, grad_update, send_a, send_b, fields, resets):
    odd = place[0] % 2 == 1
    wide = hidden.shape[1]
    block = wide // SPLIT
    load_field(odd, fields, LANES, motion_a, motion_b)
    load_field(odd, fields, 0, hidden_a, hidden_b)
    gates(fields, own, partial, resets, gate_w, update, reset, reset_hidden, wide)
    for row in range(2):
        for start in range(0, wide, block):
            here = pl.ds(start, block)
            new = candidate_part(resets, cand_w, row, here)
            gradients_out(grad_hidden[row, here].astype(F32), update[row + 1, here], new,
                          hidden[row, here].astype(F32), row, here, grad_cand, grad_update, send_a, send_b)
    send_updates(odd, grad_update, send_a, send_b)


def back_step(place, partial, grad_a, grad_b, grad_update, hiddens, reset, cand_wt, gate_wt,
              grad_reset, cand_taps, gate_taps, inner, grad_motion, finish):
    odd = place[0] % 2 == 1
    wide = partial.shape[1]
    block = wide // SPLIT
    fill_neighbours(lambda r, v: store_taps(cand_taps, r, 0, LANES, v, False), odd, grad_a, grad_b, wide)
    deep = cand_wt.shape[0] // 3
    deeper = gate_wt.shape[0] // 3

    for step in range(4 * SPLIT):
        row, start = step // SPLIT, (step % SPLIT) * block
        here = pl.ds(start, block)
        total = partial[row, here] + sum(
            dot(cand_taps[row + 2 - a, here], cand_wt[a * deep : (a + 1) * deep])
            for a in range(3)
            if row - a not in (0, 1)
        )
        inner[row, here] = total[:, :LANES]
        if row in (1, 2):
            grad_motion[row - 1, here] = total[:, LANES:]
    above_u, below_u = sides(odd, grad_a[2], grad_b[2])
    updates = (above_u, grad_update[0], grad_update[1], below_u)
    for row in range(4):
        gate = reset[row]
        value = (inner[row] * hiddens[row].astype(F32) * gate * (1.0 - gate)).astype(BF16)
        store_taps(gate_taps, row, 0, 2 * LANES, updates[row].astype(F32), False)
        store_taps(gate_taps, row, LANES, 2 * LANES, value.astype(F32), False)
        if row in (1, 2):
            grad_reset[row - 1] = value
    for row in range(2):
        for start in range(0, wide, block):
            here = pl.ds(start, block)
            total = sum(
                dot(gate_taps[row + 2 - a, here], gate_wt[a * deeper : (a + 1) * deeper]) for a in range(3)
            )
            grad_motion[row, here] += total[:, LANES:]
            finish(row, start, here, inner[row + 1, here] * reset[row + 1, here] + total[:, :LANES])


def later_back_kernel(cols_axis, place, partial, grad_a, grad_b, grad_update, hidden, hidden_a, hidden_b, reset,
                      cand_wt, gate_wt, update, grad_hidden, older_hiddens, older_update, older_candidate,
                      grad_reset, grad_state, grad_motion, older_cand, older_upd, send_a, send_b,
                      cand_taps, gate_taps, inner):
    odd = place[0] % 2 == 1
    wide = hidden.shape[1]
    block = wide // SPLIT
    inside = image_columns(place, wide, wide - 2 * HALO, cols_axis)

    def finish(row, start, here, terms):
        gate = update[row + 1, here]
        grad = grad_hidden[row, here].astype(F32) * (1.0 - gate) + terms
        grad = jnp.where(inside[start : start + block], grad, 0.0)
        grad_state[row, here] = grad
        gradients_out(grad, older_update[row + 1, here], older_candidate[row, here],
                      older_hiddens[row + 1, here].astype(F32), row, here, older_cand, older_upd, send_a, send_b)

    hiddens = hidden_rows(odd, hidden, hidden_a, hidden_b)
    back_step(place, partial, grad_a, grad_b, grad_update, hiddens, reset, cand_wt, gate_wt,
              grad_reset, cand_taps, gate_taps, inner, grad_motion, finish)
    send_updates(odd, older_upd, send_a, send_b)


def first_back_kernel(place, partial, grad_a, grad_b, grad_update, hiddens, reset,
                      cand_wt, gate_wt, update, grad_state, motion_so_far, pre, feats, weight,
                      grad_reset, grad_first, grad_feats, motion_w, cand_taps, gate_taps, inner, grad_motion):
    def finish(row, start, here, terms):
        gate = update[row + 1, here]
        grad = grad_state[row, here] * (1.0 - gate) + terms
        first, last = max(start, HALO), min(start + grad.shape[0], HALO + grad_first.shape[1])
        grad_first[row, first - HALO : last - HALO] = grad[first - start : last - start].astype(BF16)
        grad_motion[row, here] += motion_so_far[row, here]

    back_step(place, partial, grad_a, grad_b, grad_update, hiddens, reset, cand_wt, gate_wt,
              grad_reset, cand_taps, gate_taps, inner, grad_motion, finish)
    inner_cols = slice(HALO, HALO + grad_feats.shape[1])
    total = jnp.zeros((LANES, LANES), F32)
    for row in range(2):
        value = pre[row, inner_cols]
        gate = jax.nn.sigmoid(value)
        slope = gate * (1.0 + value * (1.0 - gate))
        grad_pre = (grad_motion[row, inner_cols] * slope).astype(BF16)
        total = total + dot_tn(feats[row, inner_cols], grad_pre)
        grad_feats[row] = dot_nt(grad_pre, weight[...])
    motion_w[...] = total


def load_pixels(odd, pixels, hiddens, motion, motion_a, motion_b):
    wide = pixels.shape[0] // 4
    for row, value in enumerate(hidden_rows(odd, motion, motion_a, motion_b)):
        pixels[row * wide : (row + 1) * wide, LANES:] = value[:wide]
    for row, value in enumerate(hiddens):
        pixels[row * wide : (row + 1) * wide, :LANES] = value


def load_grads(taps, grads):
    wide = grads.shape[1]
    column = lax.broadcasted_iota(jnp.int32, (wide, LANES), 0)
    own = (column >= HALO) & (column < wide - HALO)
    depth = grads.shape[2]
    for row in range(2):
        for part in range(depth // LANES):
            value = jnp.where(own, grads[row, :, part * LANES : (part + 1) * LANES].astype(F32), 0.0)
            shifted = (pltpu.roll(value, wide - 1, 0), value, pltpu.roll(value, 1, 0))
            for tap in range(3):
                start = tap * depth + part * LANES
                taps[row * wide : (row + 1) * wide, start : start + LANES] = shifted[tap].astype(BF16)


def weight_products(pixels, taps, wide, depth, finish):
    for a in range(3):
        total = dot_tn(pixels[a * wide : (a + 2) * wide], taps[...])
        for b in range(3):
            finish((3 * a + b) * 2 * LANES, total[:, b * depth : (b + 1) * depth])


def hidden_rows(odd, hidden, hidden_a, hidden_b):
    above, below = sides(odd, hidden_a[1], hidden_b[1])[0], sides(odd, hidden_a[0], hidden_b[0])[1]
    return (above, hidden[0], hidden[1], below)


def load_hidden(pixels, rows, wide):
    for row, value in enumerate(rows):
        pixels[row * wide : (row + 1) * wide, :LANES] = value


def second_weights_kernel(place, resets, hidden, hidden_a, hidden_b, motion, motion_a, motion_b, cand_grads, update_grads,
                          cand_out, update_out, pixels, taps):
    odd = place[0] % 2 == 1
    wide = taps.shape[0] // 2
    load_pixels(odd, pixels, [resets[row] for row in range(4)], motion, motion_a, motion_b)
    load_grads(taps, cand_grads)

    def cand_finish(start, value):
        cand_out[pl.ds(start, 2 * LANES)] = value

    def update_finish(start, value):
        update_out[pl.ds(start, 2 * LANES)] = value

    weight_products(pixels, taps, wide, LANES, cand_finish)
    load_hidden(pixels, hidden_rows(odd, hidden, hidden_a, hidden_b), wide)
    load_grads(taps, update_grads)
    weight_products(pixels, taps, wide, LANES, update_finish)


def store_halves(parts, offset, rows, start, value):
    for piece in range(0, 2 * LANES, LANES):
        half, row = divmod(start + piece, rows // 2)
        there = offset + row
        parts[half, there : there + LANES] = value[piece : piece + LANES].astype(BF16)


def share_cores(place, parts, kept, given):
    core = place[1] % 2
    kept[...] = parts[core]
    given[...] = parts[1 - core]


def first_weights_kernel(place, resets, older, hidden, hidden_a, hidden_b, motion, motion_a, motion_b,
                         cand_grads, update_grads, reset_grads, cand_sum, update_sum,
                         kept, given, reset_out, pixels, taps, parts):
    odd = place[0] % 2 == 1
    wide = taps.shape[0] // 2
    rows = cand_sum.shape[0]
    load_pixels(odd, pixels, [resets[row] for row in range(4)], motion, motion_a, motion_b)
    load_grads(taps, cand_grads)

    def cand_finish(start, value):
        store_halves(parts, rows // 2, rows, start, cand_sum[pl.ds(start, 2 * LANES)] + value)

    def update_finish(start, value):
        store_halves(parts, 0, rows, start, update_sum[pl.ds(start, 2 * LANES)] + value)

    def reset_finish(start, value):
        reset_out[pl.ds(start, 2 * LANES)] = value

    weight_products(pixels, taps, wide, LANES, cand_finish)
    load_hidden(pixels, [older[row] for row in range(4)], wide)
    load_grads(taps, update_grads)
    weight_products(pixels, taps, wide, LANES, update_finish)
    share_cores(place, parts, kept, given)
    load_hidden(pixels, hidden_rows(odd, hidden, hidden_a, hidden_b), wide)
    load_grads(taps, reset_grads)
    weight_products(pixels, taps, wide, LANES, reset_finish)


def last_weights_kernel(place, hiddens, motion, motion_a, motion_b, reset_grads, reset_sum, motion_w,
                        kept, given, pixels, taps, parts):
    odd = place[0] % 2 == 1
    load_pixels(odd, pixels, [hiddens[row] for row in range(4)], motion, motion_a, motion_b)
    load_grads(taps, reset_grads)
    rows = reset_sum.shape[0]

    def finish(start, value):
        store_halves(parts, 0, rows, start, reset_sum[pl.ds(start, 2 * LANES)] + value)

    weight_products(pixels, taps, taps.shape[0] // 2, LANES, finish)
    parts[0, rows // 2 :] = motion_w[...].astype(BF16)
    parts[1, rows // 2 :] = jnp.zeros((parts.shape[1] - rows // 2, LANES), BF16)
    share_cores(place, parts, kept, given)


def join_kernel(kept, got, last_kept, last_got, half):
    split = kept.shape[0]
    half[:split] = (kept[...].astype(F32) + got[...].astype(F32)).astype(BF16)
    half[split:] = (last_kept[...].astype(F32) + last_got[...].astype(F32)).astype(BF16)


def right_kernel(place, own, back_a, back_b, grad_right):
    odd = place[1] % 2 == 1
    split = own.shape[1] - DISP
    for row in range(2):
        grad_right[row, :split] = own[row, :split].astype(BF16)
        returned = sides(odd, back_a[row], back_b[row])[1].astype(F32)
        grad_right[row, split:] = (own[row, split:] + returned).astype(BF16)


def band_back_kernel(place, disparity, offsets, left, right, got_a, got_b, grad_feats,
                     grad_left, back, own, window, grad_window):
    odd = place[1] % 2 == 1
    cols = left.shape[1]
    block = cols // 2
    span = 512
    scaling = 1.0 / math.sqrt(left.shape[2])
    position = DISP - lax.broadcasted_iota(jnp.int32, (span, LANES), 0)
    valid = (position >= 0) & (position < DISP)
    for row in range(2):
        from_left = sides(odd, got_a[row], got_b[row])[0]
        window[0:DISP] = from_left[HALO : HALO + DISP]
        window[DISP : DISP + cols] = right[row]
        window[DISP + cols :] = jnp.zeros((window.shape[0] - DISP - cols, window.shape[1]), BF16)
        grad_window[...] = jnp.zeros(grad_window.shape, F32)
        table = lookup_rows(position, valid, disparity, offsets, row)
        for part in range(2):
            here = slice(part * block, (part + 1) * block)
            there = slice(part * block, part * block + span)
            band = split_dot(grad_feats[row, here], table, dot_nt)
            scores = (pltpu.roll(band, 0, 1, stride=1, stride_axis=0) * scaling).astype(BF16)
            grad_left[row, here] = dot(scores, window[there]).astype(BF16)
            grad_window[there] += dot_tn(scores, left[row, here])
        back[row] = grad_window[0:DISP].astype(BF16)
        own[row] = grad_window[DISP : DISP + cols]


def pairings(count):
    first = [(2 * k, 2 * k + 1) for k in range(count // 2)]
    second = [(2 * k + 1, 2 * k + 2) for k in range(count // 2 - 1)]
    both = lambda pairs: pairs + [(b, a) for a, b in pairs]
    return both(first), both(second)


def exchanged(value, axis):
    first, second = pairings(lax.axis_size(axis))
    return lax.ppermute(value, axis, first), lax.ppermute(value, axis, second)


def exchanged_pair(value_a, value_b, axis):
    first, second = pairings(lax.axis_size(axis))
    other = lax.ppermute(value_b, axis, second)
    return lax.ppermute(value_a, axis, first), other


def core_groups():
    devices = lax.axis_size("rows") * lax.axis_size("cols")
    return [[i for i in range(devices) if i % 2 == c] for c in range(2)]


def shared_out(kept, got, last_kept, last_given, axes):
    total = kept.shape[0] + last_kept.shape[0]
    (half,) = kernel_call(
        join_kernel, [array((total, LANES), BF16)], [kept, got, last_kept, swapped(last_given)], 0, [], 0
    )
    half = half.reshape(len(core_groups()[0]), -1, LANES)
    return lax.all_to_all(half, axes, 0, 0, tiled=True, axis_index_groups=core_groups())


def spread_kernel(pieces, out):
    out[...] = jnp.broadcast_to(jnp.sum(pieces[...].astype(F32), axis=0).astype(BF16)[None], out.shape)


def gathered(pieces, axes):
    (spread,) = kernel_call(spread_kernel, [array(pieces.shape, BF16)], [pieces], 0, [], 0)
    half = lax.all_to_all(spread, axes, 0, 0, tiled=True, axis_index_groups=core_groups())
    return half.reshape(-1, LANES)


def swapped(value):
    return lax.ppermute(value, "cols", [(i, i ^ 1) for i in range(lax.axis_size("cols"))])


def on_device(
    fmap_left,
    fmap_right,
    hidden_init,
    disp_init,
    level_offset,
    motion_weight,
    gate_weight,
    cand_weight,
    grad_hidden,
):
    rows, cols, channels = fmap_left.shape
    wide = cols + 2 * HALO
    state = hidden_init.shape[2]
    feats_count = motion_weight.shape[0]
    rows_axis, cols_axis = lax.axis_size("rows"), lax.axis_size("cols")
    rows_index, cols_index = lax.axis_index("rows"), lax.axis_index("cols")
    place = jnp.stack([rows_index, cols_index]).astype(jnp.int32)

    maps_a, maps_b = exchanged(packed(fmap_left, fmap_right, hidden_init, grad_hidden), "cols")
    init_a, init_b = exchanged(hidden_init, "rows")
    motion_w = jnp.pad(motion_weight, ((0, LANES - feats_count), (0, 0)))
    field = lambda count, dtype: array((count, wide, LANES), dtype)
    band_flops = 2 * rows * wide * 512 * channels
    motion, motion_pre, feats, hidden, grads = kernel_call(
        motion_kernel,
        [array((2, wide + 2 * HALO, LANES), BF16), field(2, F32), field(2, BF16), field(2, BF16), field(2, BF16)],
        [place, disp_init, level_offset, fmap_left, fmap_right, maps_a, maps_b, motion_w, hidden_init, grad_hidden],
        3,
        [pltpu.VMEM((wide, channels), BF16), pltpu.VMEM((768, channels), BF16), pltpu.VMEM((832, channels), BF16)],
        2 * band_flops,
    )
    motion, init_a, init_b = lax.optimization_barrier((motion, init_a, init_b))
    motion_a, motion_b = exchanged(motion, "rows")
    gate_wt, cand_wt = kernel_call(
        turn_kernel,
        [array(gate_weight.shape, BF16), array((9 * state, 2 * state), BF16)],
        [gate_weight, cand_weight],
        0,
        [],
        0,
    )
    motion_a, motion_b, gate_wt, cand_wt = lax.optimization_barrier((motion_a, motion_b, gate_wt, cand_wt))
    motions = (motion, motion_a, motion_b)
    unit = 2 * wide * 9 * 2 * state * state
    fields = [pltpu.VMEM((6, wide, 6 * LANES), BF16), pltpu.VMEM((4, wide, 6 * LANES), BF16)]

    field_taps = array((2, wide, 6 * LANES), BF16)
    partials = array((4, wide, 2 * LANES), F32)
    own_taps, partial = kernel_call(
        own_gates_kernel, [field_taps, partials], [hidden, motion, gate_weight], 0, [], 4 * unit
    )
    hidden_1, update_0, reset_0, reset_hidden_0, candidate_0, hiddens_0 = kernel_call(
        lambda *refs: first_kernel(cols_axis, *refs),
        [field(2, BF16), field(4, F32), field(4, F32), field(4, BF16), field(2, F32), field(4, BF16)],
        [place, hidden, init_a, init_b, *motions[1:], gate_weight, cand_weight, own_taps, partial],
        1,
        fields,
        10 * unit,
    )
    hidden_1a, hidden_1b = exchanged(hidden_1, "rows")
    own_taps, partial = kernel_call(
        own_gates_kernel, [field_taps, partials], [hidden_1, motion, gate_weight], 0, [], 4 * unit
    )
    update_1, reset_1, reset_hidden_1, grad_cand_1, grad_update_1, send_a, send_b = kernel_call(
        second_kernel,
        [field(4, F32), field(4, F32), field(4, BF16), field(2, BF16), field(2, BF16), field(3, BF16), field(3, BF16)],
        [place, hidden_1, hidden_1a, hidden_1b, *motions[1:], gate_weight, cand_weight, own_taps, partial, grads],
        1,
        fields,
        10 * unit,
    )
    got_a, got_b = exchanged_pair(send_a, send_b, "rows")
    pixels = pltpu.VMEM((4 * wide, 2 * LANES), BF16)
    taps = pltpu.VMEM((2 * wide, 3 * LANES), BF16)
    weights = array(cand_weight.shape, F32)
    cand_sum, update_sum = kernel_call(
        second_weights_kernel,
        [weights, weights],
        [place, reset_hidden_1, hidden_1, hidden_1a, hidden_1b, *motions, grad_cand_1, grad_update_1],
        1,
        [pixels, taps],
        4 * unit,
    )
    (partial,) = kernel_call(
        own_cand_kernel, [partials], [grad_cand_1, cand_wt], 0, [pltpu.VMEM((2, wide, 3 * LANES), BF16)], 2 * unit
    )
    got_a, got_b, cand_sum, update_sum = lax.optimization_barrier((got_a, got_b, cand_sum, update_sum))
    back_scratch = [
        pltpu.VMEM((6, wide, 3 * LANES), BF16),
        pltpu.VMEM((4, wide, 6 * LANES), BF16),
        pltpu.VMEM((4, wide, LANES), F32),
    ]
    grad_reset_1, grad_state, grad_motion_1, grad_cand_0, grad_update_0, send_a, send_b = kernel_call(
        lambda *refs: later_back_kernel(cols_axis, *refs),
        [field(2, BF16), field(2, F32), field(2, F32), field(2, BF16), field(2, BF16),
         field(3, BF16), field(3, BF16)],
        [place, partial, got_a, got_b, grad_update_1, hidden_1, hidden_1a, hidden_1b, reset_1, cand_wt, gate_wt,
         update_1, grads, hiddens_0, update_0, candidate_0],
        1,
        back_scratch,
        8 * unit,
    )
    got_a, got_b = exchanged_pair(send_a, send_b, "rows")
    depth = cand_weight.shape[0]
    total = rows_axis * cols_axis * CHUNK_ROWS // 2
    late = total - depth
    kept, given, reset_sum = kernel_call(
        first_weights_kernel,
        [array((depth, LANES), BF16), array((depth, LANES), BF16), weights],
        [place, reset_hidden_0, hiddens_0, hidden_1, hidden_1a, hidden_1b, *motions,
         grad_cand_0, grad_update_0, grad_reset_1, cand_sum, update_sum],
        1,
        [pixels, taps, pltpu.VMEM((2, depth, LANES), BF16)],
        6 * unit,
    )
    (partial,) = kernel_call(
        own_cand_kernel, [partials], [grad_cand_0, cand_wt], 0, [pltpu.VMEM((2, wide, 3 * LANES), BF16)], 2 * unit
    )
    got_a, got_b, kept, given, reset_sum, partial = lax.optimization_barrier(
        (got_a, got_b, kept, given, reset_sum, partial)
    )
    got = swapped(given)
    grad_reset_0, grad_first, grad_feats, motion_sum = kernel_call(
        first_back_kernel,
        [field(2, BF16), array((2, cols, LANES), BF16), array((2, cols, LANES), F32), array((LANES, LANES), F32)],
        [place, partial, got_a, got_b, grad_update_0, hiddens_0, reset_0, cand_wt, gate_wt,
         update_0, grad_state, grad_motion_1, motion_pre, feats, motion_w],
        1,
        back_scratch + [pltpu.VMEM((2, wide, LANES), F32)],
        8 * unit,
    )
    reset_sum, got = lax.optimization_barrier((reset_sum, got))
    last_kept, last_given = kernel_call(
        last_weights_kernel,
        [array((late, LANES), BF16), array((late, LANES), BF16)],
        [place, hiddens_0, *motions, grad_reset_0, reset_sum, motion_sum],
        1,
        [pixels, taps, pltpu.VMEM((2, late, LANES), BF16)],
        2 * unit,
    )
    grad_left, back, own = kernel_call(
        band_back_kernel,
        [array((2, cols, channels), BF16), array((2, DISP, channels), BF16), array((2, cols, channels), F32)],
        [place, disp_init, level_offset, fmap_left, fmap_right, maps_a, maps_b, grad_feats],
        3,
        [pltpu.VMEM((768, channels), BF16), pltpu.VMEM((768, channels), F32)],
        3 * band_flops,
    )
    pieces = shared_out(kept, got, last_kept, last_given, ("rows", "cols"))
    pieces, grad_left, back, own = lax.optimization_barrier((pieces, grad_left, back, own))
    back_a, back_b = exchanged(back, "cols")
    (grad_right,) = kernel_call(
        right_kernel, [array((2, cols, channels), BF16)], [place, own, back_a, back_b], 1, [], 0
    )
    half = gathered(pieces, ("rows", "cols"))
    half, grad_right = lax.optimization_barrier((half, grad_right))
    normaliser = 1.0 / math.sqrt(rows * rows_axis * cols * cols_axis)
    other = swapped(half)
    results = [array(gate_weight.shape, F32), array(cand_weight.shape, F32)]
    own_parts = half_call(
        lambda *refs: own_half_kernel(normaliser, *refs), place, [half], results, depth, {}
    )
    other, *own_parts = lax.optimization_barrier((other, *own_parts))
    grad_motion_w, grad_gate_w, grad_cand_w = half_call(
        lambda *refs: other_half_kernel(normaliser, *refs), place, [half, other, *own_parts],
        [array((feats_count, LANES), F32)] + results, depth, {3: 1, 4: 2},
    )
    return (grad_left, grad_right, grad_first, grad_motion_w, grad_gate_w, grad_cand_w)


def solution(mesh):
    in_specs = (
        P("rows", "cols", None),
        P("rows", "cols", None),
        P("rows", "cols", None),
        P("rows"),
        P("rows", None),
        P(),
        P(),
        P(),
        P("rows", "cols", None),
    )
    out_specs = (
        P("rows", "cols", None),
        P("rows", "cols", None),
        P("rows", "cols", None),
        P(),
        P(),
        P(),
    )
    return jax.shard_map(
        on_device, mesh=mesh, in_specs=in_specs, out_specs=out_specs, check_vma=False
    )
```

```python
import math

import jax
import jax.numpy as jnp
from jax import lax
from jax.experimental import pallas as pl
from jax.experimental.pallas import tpu as pltpu
from jax.sharding import PartitionSpec as P

LEVELS = 4
RADIUS = 4
DISP = 192
TAPS = 2 * RADIUS + 1
HALO = 16
LANES = 128
SPLIT = 2
CHUNK_ROWS = 56

BF16 = jnp.bfloat16
F32 = jnp.float32
VMEM = pl.BlockSpec(memory_space=pltpu.VMEM)
SMEM = pl.BlockSpec(memory_space=pltpu.SMEM)


def dot(a, b):
    return jnp.dot(a, b, preferred_element_type=F32)


def dot_nt(a, b):
    return lax.dot_general(a, b, (((1,), (1,)), ((), ())), preferred_element_type=F32)


def dot_tn(a, b):
    return lax.dot_general(a, b, (((0,), (0,)), ((), ())), preferred_element_type=F32)


def split_dot(a, table, contract):
    high = a.astype(BF16)
    low = (a - high.astype(F32)).astype(BF16)
    return contract(high, table) + contract(low, table)


def kernel_call(body, outs, ins, scalars, scratch, flops):
    bytes_moved = sum(math.prod(x.shape) * x.dtype.itemsize for x in (*ins, *outs))
    held = sum(math.prod(x.shape) * jnp.dtype(x.dtype).itemsize for x in scratch)
    return pl.pallas_call(
        body,
        out_shape=outs,
        in_specs=[SMEM] * scalars + [VMEM] * (len(ins) - scalars),
        out_specs=[VMEM] * len(outs),
        scratch_shapes=scratch,
        compiler_params=pltpu.CompilerParams(vmem_limit_bytes=bytes_moved + held + 4 * 2**20),
        cost_estimate=pl.CostEstimate(flops=flops, bytes_accessed=bytes_moved, transcendentals=0),
    )(*ins)


def array(shape, dtype):
    return jax.ShapeDtypeStruct(shape, dtype)


def lookup_rows(position, valid, disparity, offsets, row):
    count = position.shape[0]
    feature = lax.broadcasted_iota(jnp.int32, (count, LANES), 1)
    table = jnp.zeros((count, LANES), F32)
    for level in range(LEVELS):
        centre = (disparity[row] >> level) + offsets[row, level]
        tap = feature - level * TAPS
        matches = (position >> level) == tap + (centre - RADIUS)
        matches = matches & (tap >= 0) & (tap < TAPS) & valid
        table = jnp.where(matches, 1.0 / 2**level, table)
    return table.astype(BF16)


def sides(odd, first, second):
    return jnp.where(odd, first, second), jnp.where(odd, second, first)


def store_taps(ref, row, lane, step, value, forward):
    wide = value.shape[0]
    left = pltpu.roll(value, 1, 0).astype(BF16)
    right = pltpu.roll(value, wide - 1, 0).astype(BF16)
    taps = (left, value.astype(BF16), right) if forward else (right, value.astype(BF16), left)
    for tap in range(3):
        start = lane + tap * step
        ref[row, :, start : start + LANES] = taps[tap]


def pack_kernel(left, right, hidden, grads, out, sems):
    cols = left.shape[1]
    tail = DISP + HALO
    first, last = pl.ds(0, HALO), pl.ds(cols - HALO, HALO)
    low, high = pl.ds(0, LANES), pl.ds(LANES, LANES)
    every = pl.ds(0, 2 * LANES)
    moves = (
        (right, pl.ds(cols - tail, tail), pl.ds(0, tail), every),
        (left, last, pl.ds(tail, HALO), every),
        (left, first, pl.ds(tail + HALO, HALO), every),
        (right, first, pl.ds(tail + 2 * HALO, HALO), every),
        (hidden, last, pl.ds(tail + 3 * HALO, HALO), low),
        (hidden, first, pl.ds(tail + 3 * HALO, HALO), high),
        (grads, last, pl.ds(tail + 4 * HALO, HALO), low),
        (grads, first, pl.ds(tail + 4 * HALO, HALO), high),
    )
    copies = [
        pltpu.make_async_copy(source.at[:, start], out.at[:, stop, lanes], sems.at[number])
        for number, (source, start, stop, lanes) in enumerate(moves)
    ]
    for copy in copies:
        copy.start()
    for copy in copies:
        copy.wait()


def packed(left, right, hidden, grads):
    rows, cols, channels = left.shape
    count = DISP + 6 * HALO
    return pl.pallas_call(
        pack_kernel,
        out_shape=array((rows, count, channels), BF16),
        in_specs=[pl.BlockSpec(memory_space=pltpu.HBM)] * 4,
        out_specs=VMEM,
        scratch_shapes=[pltpu.SemaphoreType.DMA((8,))],
        compiler_params=pltpu.CompilerParams(vmem_limit_bytes=56 * 2**20),
        cost_estimate=pl.CostEstimate(flops=0, bytes_accessed=4 * rows * count * channels, transcendentals=0),
    )(left, right, hidden, grads)


def turn_kernel(gate_w, cand_w, gate_wt, cand_wt, cand_pair):
    deep = cand_w.shape[0] // 3
    nothing = jnp.zeros((deep, LANES), BF16)
    for row in range(4):
        here = slice(row * deep, (row + 1) * deep)
        cand_pair[here, :LANES] = cand_w[here] if row < 3 else nothing
        cand_pair[here, LANES:] = cand_w[(row - 1) * deep : row * deep] if row > 0 else nothing
    for tap in range(9):
        here = slice(tap * 2 * LANES, (tap + 1) * 2 * LANES)
        gate_wt[here] = gate_w[here].T
        cand_wt[tap * LANES : (tap + 1) * LANES] = cand_w[here].T


def spread_half(core, half, scale, gate, cand, parts, sems):
    count = parts.shape[1]
    there = pl.ds(pl.multiple_of(core * count, LANES), count)
    targets = (gate.at[there, pl.ds(0, LANES)], cand.at[there], gate.at[there, pl.ds(LANES, LANES)])
    copies = []
    for number, target in enumerate(targets):
        parts[number] = half[number * count : (number + 1) * count].astype(F32) * scale
        copies.append(pltpu.make_async_copy(parts.at[number], target, sems.at[number]))
        copies[-1].start()
    for copy in copies:
        copy.wait()


def own_half_kernel(scale, place, half, gate, cand, parts, sems):
    spread_half(place[1] % 2, half, scale, gate, cand, parts, sems)


def other_half_kernel(scale, place, half, other, gate_in, cand_in, motion, gate, cand, parts, sems):
    core = place[1] % 2
    start = 3 * parts.shape[1]
    count = motion.shape[0]
    rows = slice(start, start + LANES)
    motion[...] = jnp.where(core == 0, half[rows], other[rows]).astype(F32)[:count] * scale
    spread_half(1 - core, other, scale, gate, cand, parts, sems)


def half_call(body, place, arrays, outs, depth, aliases):
    anywhere = pl.BlockSpec(memory_space=pltpu.HBM)
    return pl.pallas_call(
        body,
        out_shape=outs,
        in_specs=[SMEM] + [VMEM] * (len(arrays) - len(aliases)) + [anywhere] * len(aliases),
        out_specs=[VMEM] * (len(outs) - 2) + [anywhere] * 2,
        scratch_shapes=[
            pltpu.VMEM((3, depth // 2, LANES), F32), pltpu.SemaphoreType.DMA((3,))
        ],
        input_output_aliases=aliases,
        compiler_params=pltpu.CompilerParams(vmem_limit_bytes=12 * 2**20),
        cost_estimate=pl.CostEstimate(flops=0, bytes_accessed=6 * depth * LANES, transcendentals=0),
    )(place, *arrays)


def motion_kernel(place, disparity, offsets, left, right, got_a, got_b, weight, hidden, grads,
                  motion, pre, feats, hidden_ext, grads_ext, ext, window, flipped):
    odd = place[1] % 2 == 1
    cols = left.shape[1]
    wide = cols + 2 * HALO
    block = wide // 2
    span = 512
    tail = DISP + HALO
    flat = (lax.broadcasted_iota(jnp.int32, (LANES, LANES), 0)
            + lax.broadcasted_iota(jnp.int32, (LANES, LANES), 1))
    mirror = jnp.where(flat == LANES - 1, 1.0, 0.0).astype(BF16)
    total = window.shape[0]
    position = lax.broadcasted_iota(jnp.int32, (span, LANES), 0) - (block - 1)
    valid = (position >= 0) & (position < DISP)
    for row in range(2):
        from_left, from_right = sides(odd, got_a[row], got_b[row])
        state, last = tail + 3 * HALO, HALO + cols
        hidden_ext[row, 0:HALO] = from_left[state : state + HALO, :LANES]
        hidden_ext[row, HALO:last] = hidden[row]
        hidden_ext[row, last:] = from_right[state : state + HALO, LANES:]
        grads_ext[row, 0:HALO] = from_left[state + HALO :, :LANES]
        grads_ext[row, HALO:last] = grads[row]
        grads_ext[row, last:] = from_right[state + HALO :, LANES:]
        motion[row, wide : wide + HALO] = from_left[state : state + HALO, :LANES]
        motion[row, wide + HALO :] = from_right[state : state + HALO, LANES:]
        ext[0:HALO] = from_left[tail : tail + HALO]
        ext[HALO : HALO + cols] = left[row]
        ext[HALO + cols : wide] = from_right[tail + HALO : tail + 2 * HALO]
        window[0:tail] = from_left[0:tail]
        window[tail : tail + cols] = right[row]
        window[tail + cols : tail + cols + HALO] = from_right[tail + 2 * HALO : tail + 3 * HALO]
        window[tail + cols + HALO :] = jnp.zeros((total - tail - cols - HALO, window.shape[1]), BF16)
        parts = total // LANES
        for part in range(parts):
            source = window[(parts - 1 - part) * LANES : (parts - part) * LANES]
            flipped[part * LANES : (part + 1) * LANES] = dot(mirror, source).astype(BF16)
        flipped[total:] = jnp.zeros((flipped.shape[0] - total, window.shape[1]), BF16)
        table = lookup_rows(position, valid, disparity, offsets, row)
        for part in range(2):
            start = part * block
            base = total - DISP - start - block
            scores = dot_nt(ext[start : start + block], flipped[base : base + span])
            scores = scores * (1.0 / math.sqrt(left.shape[2]))
            band = pltpu.roll(scores, 0, 1, stride=1, stride_axis=0)
            found = split_dot(band, table, dot).astype(BF16)
            value = dot(found, weight[...])
            feats[row, start : start + block] = found
            pre[row, start : start + block] = value
            motion[row, start : start + block] = (value * jax.nn.sigmoid(value)).astype(BF16)


def image_columns(place, wide, cols, cols_axis):
    column = lax.broadcasted_iota(jnp.int32, (wide, LANES), 0) - HALO + place[1] * cols
    return (column >= 0) & (column < cols * cols_axis)


def fill_neighbours(store, odd, first, second, wide):
    for row in range(2):
        above, below = sides(odd, first[row, :wide], second[row, :wide])
        store(row, above.astype(F32))
        store(4 + row, below.astype(F32))


def own_products(partial, taps, weights, source):
    deep = weights.shape[0] // 3
    block = partial.shape[1] // SPLIT
    for step in range(4 * SPLIT):
        row, start = step // SPLIT, (step % SPLIT) * block
        here = pl.ds(start, block)
        partial[row, here] = sum(
            dot(taps[source(row, a), here], weights[a * deep : (a + 1) * deep])
            for a in range(3)
            if source(row, a) in (0, 1)
        )


def own_gates_kernel(hidden, motion, gate_w, taps, partial):
    wide = hidden.shape[1]
    for row in range(2):
        store_taps(taps, row, 0, 2 * LANES, hidden[row].astype(F32), True)
        store_taps(taps, row, LANES, 2 * LANES, motion[row, :wide].astype(F32), True)
    own_products(partial, taps, gate_w, lambda row, a: row + a - 2)


def own_cand_kernel(grad_cand, cand_wt, partial, taps):
    for row in range(2):
        store_taps(taps, row, 0, LANES, grad_cand[row].astype(F32), False)
    own_products(partial, taps, cand_wt, lambda row, a: row - a)


def gates(fields, own, partial, resets, gate_w, update, reset, reset_hidden, wide):
    block = wide // SPLIT
    deep = gate_w.shape[0] // 3
    six = [fields.at[0], fields.at[1], own.at[0], own.at[1], fields.at[4], fields.at[5]]
    for step in range(4 * SPLIT):
        row, start = step // SPLIT, (step % SPLIT) * block
        here = pl.ds(start, block)
        total = partial[row, here] + sum(
            dot(six[row + a][here], gate_w[a * deep : (a + 1) * deep])
            for a in range(3)
            if row + a not in (2, 3)
        )
        reset_part = jax.nn.sigmoid(total[:, LANES:])
        update[row, here] = jax.nn.sigmoid(total[:, :LANES])
        reset[row, here] = reset_part
        hidden = six[row + 1][here, 2 * LANES : 3 * LANES].astype(F32)
        reset_hidden[row, here] = (reset_part * hidden).astype(BF16)
    for row in range(4):
        store_taps(resets, row, 0, 2 * LANES, reset_hidden[row].astype(F32), True)
        for tap in range(3):
            start = (2 * tap + 1) * LANES
            resets[row, :, start : start + LANES] = six[row + 1][:, start : start + LANES]


def load_field(odd, fields, lane, first, second):
    wide = fields.shape[1]
    fill_neighbours(lambda r, v: store_taps(fields, r, lane, 2 * LANES, v, True), odd, first, second, wide)


def candidates(resets, cand_pair, here):
    deep = cand_pair.shape[0] // 4
    total = sum(dot(resets[row, here], cand_pair[row * deep : (row + 1) * deep]) for row in range(4))
    return jnp.tanh(total[:, :LANES]), jnp.tanh(total[:, LANES:])


def first_kernel(cols_axis, place, hidden, init_a, init_b, motion_a, motion_b, gate_w, cand_w, own, partial,
                 later, update, reset, reset_hidden, candidate, hiddens, fields, resets):
    odd = place[0] % 2 == 1
    wide = hidden.shape[1]
    block = wide // SPLIT
    load_field(odd, fields, LANES, motion_a, motion_b)
    for row in range(2):
        got_a, got_b = (
            jnp.concatenate(
                [sent[row, wide : wide + HALO], inner[row], sent[row, wide + HALO :]], axis=0
            )
            for sent, inner in ((motion_a, init_a), (motion_b, init_b))
        )
        above, below = sides(odd, got_a, got_b)
        for there, value in ((row, above), (4 + row, below)):
            store_taps(fields, there, 0, 2 * LANES, value.astype(F32), True)
            if 0 < there < 5:
                hiddens[there - 1] = value
        hiddens[1 + row] = hidden[row]
    gates(fields, own, partial, resets, gate_w, update, reset, reset_hidden, wide)
    inside = image_columns(place, wide, wide - 2 * HALO, cols_axis)
    for start in range(0, wide, block):
        here = pl.ds(start, block)
        for row, new in enumerate(candidates(resets, cand_w, here)):
            candidate[row, here] = new
            gate = update[row + 1, here]
            old = hidden[row, here].astype(F32)
            value = (1.0 - gate) * old + gate * new
            later[row, here] = jnp.where(inside[start : start + block], value, 0.0).astype(BF16)


def gradients_out(grad, gate, new, old, row, here, grad_cand, grad_update, send_a, send_b):
    cand_part = (grad * gate * (1.0 - new * new)).astype(BF16)
    grad_cand[row, here] = cand_part
    send_a[row, here] = cand_part
    send_b[row, here] = cand_part
    grad_update[row, here] = (grad * (new - old) * gate * (1.0 - gate)).astype(BF16)


def send_updates(odd, grad_update, send_a, send_b):
    send_a[2], send_b[2] = sides(odd, grad_update[0], grad_update[1])


def second_kernel(place, hidden, hidden_a, hidden_b, motion_a, motion_b, gate_w, cand_w, own, partial, grad_hidden,
                  update, reset, reset_hidden, grad_cand, grad_update, send_a, send_b, fields, resets):
    odd = place[0] % 2 == 1
    wide = hidden.shape[1]
    block = wide // SPLIT
    load_field(odd, fields, LANES, motion_a, motion_b)
    load_field(odd, fields, 0, hidden_a, hidden_b)
    gates(fields, own, partial, resets, gate_w, update, reset, reset_hidden, wide)
    for start in range(0, wide, block):
        here = pl.ds(start, block)
        for row, new in enumerate(candidates(resets, cand_w, here)):
            gradients_out(grad_hidden[row, here].astype(F32), update[row + 1, here], new,
                          hidden[row, here].astype(F32), row, here, grad_cand, grad_update, send_a, send_b)
    send_updates(odd, grad_update, send_a, send_b)


def back_step(place, partial, grad_a, grad_b, grad_update, hiddens, reset, cand_wt, gate_wt,
              grad_reset, cand_taps, gate_taps, inner, grad_motion, finish):
    odd = place[0] % 2 == 1
    wide = partial.shape[1]
    block = wide // SPLIT
    fill_neighbours(lambda r, v: store_taps(cand_taps, r, 0, LANES, v, False), odd, grad_a, grad_b, wide)
    deep = cand_wt.shape[0] // 3
    deeper = gate_wt.shape[0] // 3

    for step in range(4 * SPLIT):
        row, start = step // SPLIT, (step % SPLIT) * block
        here = pl.ds(start, block)
        total = partial[row, here] + sum(
            dot(cand_taps[row + 2 - a, here], cand_wt[a * deep : (a + 1) * deep])
            for a in range(3)
            if row - a not in (0, 1)
        )
        inner[row, here] = total[:, :LANES]
        if row in (1, 2):
            grad_motion[row - 1, here] = total[:, LANES:]
    above_u, below_u = sides(odd, grad_a[2], grad_b[2])
    updates = (above_u, grad_update[0], grad_update[1], below_u)
    for row in range(4):
        gate = reset[row]
        value = (inner[row] * hiddens[row].astype(F32) * gate * (1.0 - gate)).astype(BF16)
        store_taps(gate_taps, row, 0, 2 * LANES, updates[row].astype(F32), False)
        store_taps(gate_taps, row, LANES, 2 * LANES, value.astype(F32), False)
        if row in (1, 2):
            grad_reset[row - 1] = value
    for row in range(2):
        for start in range(0, wide, block):
            here = pl.ds(start, block)
            total = sum(
                dot(gate_taps[row + 2 - a, here], gate_wt[a * deeper : (a + 1) * deeper]) for a in range(3)
            )
            grad_motion[row, here] += total[:, LANES:]
            finish(row, start, here, inner[row + 1, here] * reset[row + 1, here] + total[:, :LANES])


def later_back_kernel(cols_axis, place, partial, grad_a, grad_b, grad_update, hidden, hidden_a, hidden_b, reset,
                      cand_wt, gate_wt, update, grad_hidden, older_hiddens, older_update, older_candidate,
                      grad_reset, grad_state, grad_motion, older_cand, older_upd, send_a, send_b,
                      cand_taps, gate_taps, inner):
    odd = place[0] % 2 == 1
    wide = hidden.shape[1]
    block = wide // SPLIT
    inside = image_columns(place, wide, wide - 2 * HALO, cols_axis)

    def finish(row, start, here, terms):
        gate = update[row + 1, here]
        grad = grad_hidden[row, here].astype(F32) * (1.0 - gate) + terms
        grad = jnp.where(inside[start : start + block], grad, 0.0)
        grad_state[row, here] = grad
        gradients_out(grad, older_update[row + 1, here], older_candidate[row, here],
                      older_hiddens[row + 1, here].astype(F32), row, here, older_cand, older_upd, send_a, send_b)

    hiddens = hidden_rows(odd, hidden, hidden_a, hidden_b)
    back_step(place, partial, grad_a, grad_b, grad_update, hiddens, reset, cand_wt, gate_wt,
              grad_reset, cand_taps, gate_taps, inner, grad_motion, finish)
    send_updates(odd, older_upd, send_a, send_b)


def first_back_kernel(place, partial, grad_a, grad_b, grad_update, hiddens, reset,
                      cand_wt, gate_wt, update, grad_state, motion_so_far, pre, feats, weight,
                      motion, motion_a, motion_b, reset_sum, grad_first, grad_feats, kept, given,
                      cand_taps, gate_taps, inner, grad_motion, grad_reset, pixels, taps, parts):
    def finish(row, start, here, terms):
        gate = update[row + 1, here]
        grad = grad_state[row, here] * (1.0 - gate) + terms
        first, last = max(start, HALO), min(start + grad.shape[0], HALO + grad_first.shape[1])
        grad_first[row, first - HALO : last - HALO] = grad[first - start : last - start].astype(BF16)
        grad_motion[row, here] += motion_so_far[row, here]

    back_step(place, partial, grad_a, grad_b, grad_update, hiddens, reset, cand_wt, gate_wt,
              grad_reset, cand_taps, gate_taps, inner, grad_motion, finish)
    inner_cols = slice(HALO, HALO + grad_feats.shape[1])
    total = jnp.zeros((LANES, LANES), F32)
    for row in range(2):
        value = pre[row, inner_cols]
        gate = jax.nn.sigmoid(value)
        slope = gate * (1.0 + value * (1.0 - gate))
        grad_pre = (grad_motion[row, inner_cols] * slope).astype(BF16)
        total = total + dot_tn(feats[row, inner_cols], grad_pre)
        grad_feats[row] = dot_nt(grad_pre, weight[...])
    last_weights(place, hiddens, motion, motion_a, motion_b, grad_reset, reset_sum, total, kept, given, pixels, taps, parts)


def load_pixels(odd, pixels, hiddens, motion, motion_a, motion_b):
    wide = pixels.shape[0] // 4
    for row, value in enumerate(hidden_rows(odd, motion, motion_a, motion_b)):
        pixels[row * wide : (row + 1) * wide, LANES:] = value[:wide]
    for row, value in enumerate(hiddens):
        pixels[row * wide : (row + 1) * wide, :LANES] = value


def load_grads(taps, grads):
    wide = grads.shape[1]
    column = lax.broadcasted_iota(jnp.int32, (wide, LANES), 0)
    own = (column >= HALO) & (column < wide - HALO)
    depth = grads.shape[2]
    for row in range(2):
        for part in range(depth // LANES):
            value = jnp.where(own, grads[row, :, part * LANES : (part + 1) * LANES].astype(F32), 0.0)
            shifted = (pltpu.roll(value, wide - 1, 0), value, pltpu.roll(value, 1, 0))
            for tap in range(3):
                start = tap * depth + part * LANES
                taps[row * wide : (row + 1) * wide, start : start + LANES] = shifted[tap].astype(BF16)


def weight_products(pixels, taps, wide, depth, finish):
    for a in range(3):
        total = dot_tn(pixels[a * wide : (a + 2) * wide], taps[...])
        for b in range(3):
            finish((3 * a + b) * 2 * LANES, total[:, b * depth : (b + 1) * depth])


def hidden_rows(odd, hidden, hidden_a, hidden_b):
    above, below = sides(odd, hidden_a[1], hidden_b[1])[0], sides(odd, hidden_a[0], hidden_b[0])[1]
    return (above, hidden[0], hidden[1], below)


def load_hidden(pixels, rows, wide):
    for row, value in enumerate(rows):
        pixels[row * wide : (row + 1) * wide, :LANES] = value


def second_weights_kernel(place, resets, hidden, hidden_a, hidden_b, motion, motion_a, motion_b, cand_grads, update_grads,
                          cand_out, update_out, pixels, taps):
    odd = place[0] % 2 == 1
    wide = taps.shape[0] // 2
    load_pixels(odd, pixels, [resets[row] for row in range(4)], motion, motion_a, motion_b)
    load_grads(taps, cand_grads)

    def cand_finish(start, value):
        cand_out[pl.ds(start, 2 * LANES)] = value

    def update_finish(start, value):
        update_out[pl.ds(start, 2 * LANES)] = value

    weight_products(pixels, taps, wide, LANES, cand_finish)
    load_hidden(pixels, hidden_rows(odd, hidden, hidden_a, hidden_b), wide)
    load_grads(taps, update_grads)
    weight_products(pixels, taps, wide, LANES, update_finish)


def store_halves(parts, offset, rows, start, value):
    for piece in range(0, 2 * LANES, LANES):
        half, row = divmod(start + piece, rows // 2)
        there = offset + row
        parts[half, there : there + LANES] = value[piece : piece + LANES].astype(BF16)


def share_cores(place, parts, kept, given):
    core = place[1] % 2
    kept[...] = parts[core]
    given[...] = parts[1 - core]


def first_weights_kernel(place, resets, older, hidden, hidden_a, hidden_b, motion, motion_a, motion_b,
                         cand_grads, update_grads, reset_grads, cand_sum, update_sum,
                         kept, given, reset_out, pixels, taps, parts):
    odd = place[0] % 2 == 1
    wide = taps.shape[0] // 2
    rows = cand_sum.shape[0]
    load_pixels(odd, pixels, [resets[row] for row in range(4)], motion, motion_a, motion_b)
    load_grads(taps, cand_grads)

    def cand_finish(start, value):
        store_halves(parts, rows // 2, rows, start, cand_sum[pl.ds(start, 2 * LANES)] + value)

    def update_finish(start, value):
        store_halves(parts, 0, rows, start, update_sum[pl.ds(start, 2 * LANES)] + value)

    def reset_finish(start, value):
        reset_out[pl.ds(start, 2 * LANES)] = value

    weight_products(pixels, taps, wide, LANES, cand_finish)
    load_hidden(pixels, [older[row] for row in range(4)], wide)
    load_grads(taps, update_grads)
    weight_products(pixels, taps, wide, LANES, update_finish)
    share_cores(place, parts, kept, given)
    load_hidden(pixels, hidden_rows(odd, hidden, hidden_a, hidden_b), wide)
    load_grads(taps, reset_grads)
    weight_products(pixels, taps, wide, LANES, reset_finish)


def last_weights(place, hiddens, motion, motion_a, motion_b, reset_grads, reset_sum, motion_w,
                 kept, given, pixels, taps, parts):
    odd = place[0] % 2 == 1
    load_pixels(odd, pixels, [hiddens[row] for row in range(4)], motion, motion_a, motion_b)
    load_grads(taps, reset_grads)
    rows = reset_sum.shape[0]

    def finish(start, value):
        store_halves(parts, 0, rows, start, reset_sum[pl.ds(start, 2 * LANES)] + value)

    weight_products(pixels, taps, taps.shape[0] // 2, LANES, finish)
    parts[0, rows // 2 :] = motion_w.astype(BF16)
    parts[1, rows // 2 :] = jnp.zeros((parts.shape[1] - rows // 2, LANES), BF16)
    share_cores(place, parts, kept, given)


def join_kernel(kept, got, last_kept, last_got, half):
    split = kept.shape[0]
    half[:split] = (kept[...].astype(F32) + got[...].astype(F32)).astype(BF16)
    half[split:] = (last_kept[...].astype(F32) + last_got[...].astype(F32)).astype(BF16)


def right_kernel(place, own, back_a, back_b, grad_right):
    odd = place[1] % 2 == 1
    split = own.shape[1] - DISP
    for row in range(2):
        grad_right[row, :split] = own[row, :split].astype(BF16)
        returned = sides(odd, back_a[row], back_b[row])[1].astype(F32)
        grad_right[row, split:] = (own[row, split:] + returned).astype(BF16)


def band_back_kernel(place, disparity, offsets, left, right, got_a, got_b, grad_feats,
                     grad_left, back, own, window, grad_window):
    odd = place[1] % 2 == 1
    cols = left.shape[1]
    block = cols // 2
    span = 512
    scaling = 1.0 / math.sqrt(left.shape[2])
    position = DISP - lax.broadcasted_iota(jnp.int32, (span, LANES), 0)
    valid = (position >= 0) & (position < DISP)
    for row in range(2):
        from_left = sides(odd, got_a[row], got_b[row])[0]
        window[0:DISP] = from_left[HALO : HALO + DISP]
        window[DISP : DISP + cols] = right[row]
        window[DISP + cols :] = jnp.zeros((window.shape[0] - DISP - cols, window.shape[1]), BF16)
        grad_window[...] = jnp.zeros(grad_window.shape, F32)
        table = lookup_rows(position, valid, disparity, offsets, row)
        for part in range(2):
            here = slice(part * block, (part + 1) * block)
            there = slice(part * block, part * block + span)
            band = split_dot(grad_feats[row, here], table, dot_nt)
            scores = (pltpu.roll(band, 0, 1, stride=1, stride_axis=0) * scaling).astype(BF16)
            grad_left[row, here] = dot(scores, window[there]).astype(BF16)
            grad_window[there] += dot_tn(scores, left[row, here])
        back[row] = grad_window[0:DISP].astype(BF16)
        own[row] = grad_window[DISP : DISP + cols]


def pairings(count):
    first = [(2 * k, 2 * k + 1) for k in range(count // 2)]
    second = [(2 * k + 1, 2 * k + 2) for k in range(count // 2 - 1)]
    both = lambda pairs: pairs + [(b, a) for a, b in pairs]
    return both(first), both(second)


def exchanged(value, axis):
    first, second = pairings(lax.axis_size(axis))
    return lax.ppermute(value, axis, first), lax.ppermute(value, axis, second)


def exchanged_pair(value_a, value_b, axis):
    first, second = pairings(lax.axis_size(axis))
    other = lax.ppermute(value_b, axis, second)
    return lax.ppermute(value_a, axis, first), other


def core_groups():
    devices = lax.axis_size("rows") * lax.axis_size("cols")
    return [[i for i in range(devices) if i % 2 == c] for c in range(2)]


def shared_out(kept, got, last_kept, last_given, axes):
    total = kept.shape[0] + last_kept.shape[0]
    (half,) = kernel_call(
        join_kernel, [array((total, LANES), BF16)], [kept, got, last_kept, swapped(last_given)], 0, [], 0
    )
    half = half.reshape(len(core_groups()[0]), -1, LANES)
    return lax.all_to_all(half, axes, 0, 0, tiled=True, axis_index_groups=core_groups())


def spread_kernel(pieces, out):
    out[...] = jnp.broadcast_to(jnp.sum(pieces[...].astype(F32), axis=0).astype(BF16)[None], out.shape)


def gathered(pieces, axes):
    (spread,) = kernel_call(spread_kernel, [array(pieces.shape, BF16)], [pieces], 0, [], 0)
    half = lax.all_to_all(spread, axes, 0, 0, tiled=True, axis_index_groups=core_groups())
    return half.reshape(-1, LANES)


def swapped(value):
    return lax.ppermute(value, "cols", [(i, i ^ 1) for i in range(lax.axis_size("cols"))])


def on_device(
    fmap_left,
    fmap_right,
    hidden_init,
    disp_init,
    level_offset,
    motion_weight,
    gate_weight,
    cand_weight,
    grad_hidden,
):
    rows, cols, channels = fmap_left.shape
    wide = cols + 2 * HALO
    state = hidden_init.shape[2]
    feats_count = motion_weight.shape[0]
    rows_axis, cols_axis = lax.axis_size("rows"), lax.axis_size("cols")
    rows_index, cols_index = lax.axis_index("rows"), lax.axis_index("cols")
    place = jnp.stack([rows_index, cols_index]).astype(jnp.int32)

    maps_a, maps_b = exchanged(packed(fmap_left, fmap_right, hidden_init, grad_hidden), "cols")
    init_a, init_b = exchanged(hidden_init, "rows")
    motion_w = jnp.pad(motion_weight, ((0, LANES - feats_count), (0, 0)))
    field = lambda count, dtype: array((count, wide, LANES), dtype)
    band_flops = 2 * rows * wide * 512 * channels
    motion, motion_pre, feats, hidden, grads = kernel_call(
        motion_kernel,
        [array((2, wide + 2 * HALO, LANES), BF16), field(2, F32), field(2, BF16), field(2, BF16), field(2, BF16)],
        [place, disp_init, level_offset, fmap_left, fmap_right, maps_a, maps_b, motion_w, hidden_init, grad_hidden],
        3,
        [pltpu.VMEM((wide, channels), BF16), pltpu.VMEM((768, channels), BF16), pltpu.VMEM((832, channels), BF16)],
        2 * band_flops,
    )
    motion, init_a, init_b = lax.optimization_barrier((motion, init_a, init_b))
    motion_a, motion_b = exchanged(motion, "rows")
    gate_wt, cand_wt, cand_pair = kernel_call(
        turn_kernel,
        [array(gate_weight.shape, BF16), array((9 * state, 2 * state), BF16), array((24 * state, 2 * state), BF16)],
        [gate_weight, cand_weight],
        0,
        [],
        0,
    )
    motion_a, motion_b, gate_wt, cand_wt, cand_pair = lax.optimization_barrier(
        (motion_a, motion_b, gate_wt, cand_wt, cand_pair)
    )
    motions = (motion, motion_a, motion_b)
    unit = 2 * wide * 9 * 2 * state * state
    fields = [pltpu.VMEM((6, wide, 6 * LANES), BF16), pltpu.VMEM((4, wide, 6 * LANES), BF16)]

    field_taps = array((2, wide, 6 * LANES), BF16)
    partials = array((4, wide, 2 * LANES), F32)
    own_taps, partial = kernel_call(
        own_gates_kernel, [field_taps, partials], [hidden, motion, gate_weight], 0, [], 4 * unit
    )
    hidden_1, update_0, reset_0, reset_hidden_0, candidate_0, hiddens_0 = kernel_call(
        lambda *refs: first_kernel(cols_axis, *refs),
        [field(2, BF16), field(4, F32), field(4, F32), field(4, BF16), field(2, F32), field(4, BF16)],
        [place, hidden, init_a, init_b, *motions[1:], gate_weight, cand_pair, own_taps, partial],
        1,
        fields,
        10 * unit,
    )
    hidden_1a, hidden_1b = exchanged(hidden_1, "rows")
    own_taps, partial = kernel_call(
        own_gates_kernel, [field_taps, partials], [hidden_1, motion, gate_weight], 0, [], 4 * unit
    )
    update_1, reset_1, reset_hidden_1, grad_cand_1, grad_update_1, send_a, send_b = kernel_call(
        second_kernel,
        [field(4, F32), field(4, F32), field(4, BF16), field(2, BF16), field(2, BF16), field(3, BF16), field(3, BF16)],
        [place, hidden_1, hidden_1a, hidden_1b, *motions[1:], gate_weight, cand_pair, own_taps, partial, grads],
        1,
        fields,
        10 * unit,
    )
    got_a, got_b = exchanged_pair(send_a, send_b, "rows")
    pixels = pltpu.VMEM((4 * wide, 2 * LANES), BF16)
    taps = pltpu.VMEM((2 * wide, 3 * LANES), BF16)
    weights = array(cand_weight.shape, F32)
    cand_sum, update_sum = kernel_call(
        second_weights_kernel,
        [weights, weights],
        [place, reset_hidden_1, hidden_1, hidden_1a, hidden_1b, *motions, grad_cand_1, grad_update_1],
        1,
        [pixels, taps],
        4 * unit,
    )
    (partial,) = kernel_call(
        own_cand_kernel, [partials], [grad_cand_1, cand_wt], 0, [pltpu.VMEM((2, wide, 3 * LANES), BF16)], 2 * unit
    )
    got_a, got_b, cand_sum, update_sum = lax.optimization_barrier((got_a, got_b, cand_sum, update_sum))
    back_scratch = [
        pltpu.VMEM((6, wide, 3 * LANES), BF16),
        pltpu.VMEM((4, wide, 6 * LANES), BF16),
        pltpu.VMEM((4, wide, LANES), F32),
    ]
    grad_reset_1, grad_state, grad_motion_1, grad_cand_0, grad_update_0, send_a, send_b = kernel_call(
        lambda *refs: later_back_kernel(cols_axis, *refs),
        [field(2, BF16), field(2, F32), field(2, F32), field(2, BF16), field(2, BF16),
         field(3, BF16), field(3, BF16)],
        [place, partial, got_a, got_b, grad_update_1, hidden_1, hidden_1a, hidden_1b, reset_1, cand_wt, gate_wt,
         update_1, grads, hiddens_0, update_0, candidate_0],
        1,
        back_scratch,
        8 * unit,
    )
    got_a, got_b = exchanged_pair(send_a, send_b, "rows")
    depth = cand_weight.shape[0]
    total = rows_axis * cols_axis * CHUNK_ROWS // 2
    late = total - depth
    kept, given, reset_sum = kernel_call(
        first_weights_kernel,
        [array((depth, LANES), BF16), array((depth, LANES), BF16), weights],
        [place, reset_hidden_0, hiddens_0, hidden_1, hidden_1a, hidden_1b, *motions,
         grad_cand_0, grad_update_0, grad_reset_1, cand_sum, update_sum],
        1,
        [pixels, taps, pltpu.VMEM((2, depth, LANES), BF16)],
        6 * unit,
    )
    (partial,) = kernel_call(
        own_cand_kernel, [partials], [grad_cand_0, cand_wt], 0, [pltpu.VMEM((2, wide, 3 * LANES), BF16)], 2 * unit
    )
    got_a, got_b, kept, given, reset_sum, partial = lax.optimization_barrier(
        (got_a, got_b, kept, given, reset_sum, partial)
    )
    got = swapped(given)
    grad_first, grad_feats, last_kept, last_given = kernel_call(
        first_back_kernel,
        [array((2, cols, LANES), BF16), array((2, cols, LANES), F32), array((late, LANES), BF16), array((late, LANES), BF16)],
        [place, partial, got_a, got_b, grad_update_0, hiddens_0, reset_0, cand_wt, gate_wt,
         update_0, grad_state, grad_motion_1, motion_pre, feats, motion_w, *motions, reset_sum],
        1,
        back_scratch + [pltpu.VMEM((2, wide, LANES), F32), pltpu.VMEM((2, wide, LANES), BF16), pixels, taps,
                        pltpu.VMEM((2, late, LANES), BF16)],
        10 * unit,
    )
    last_kept, last_given, got = lax.optimization_barrier((last_kept, last_given, got))
    grad_left, back, own = kernel_call(
        band_back_kernel,
        [array((2, cols, channels), BF16), array((2, DISP, channels), BF16), array((2, cols, channels), F32)],
        [place, disp_init, level_offset, fmap_left, fmap_right, maps_a, maps_b, grad_feats],
        3,
        [pltpu.VMEM((768, channels), BF16), pltpu.VMEM((768, channels), F32)],
        3 * band_flops,
    )
    pieces = shared_out(kept, got, last_kept, last_given, ("rows", "cols"))
    pieces, grad_left, back, own = lax.optimization_barrier((pieces, grad_left, back, own))
    back_a, back_b = exchanged(back, "cols")
    (grad_right,) = kernel_call(
        right_kernel, [array((2, cols, channels), BF16)], [place, own, back_a, back_b], 1, [], 0
    )
    half = gathered(pieces, ("rows", "cols"))
    half, grad_right = lax.optimization_barrier((half, grad_right))
    normaliser = 1.0 / math.sqrt(rows * rows_axis * cols * cols_axis)
    other = swapped(half)
    results = [array(gate_weight.shape, F32), array(cand_weight.shape, F32)]
    own_parts = half_call(
        lambda *refs: own_half_kernel(normaliser, *refs), place, [half], results, depth, {}
    )
    other, *own_parts = lax.optimization_barrier((other, *own_parts))
    grad_motion_w, grad_gate_w, grad_cand_w = half_call(
        lambda *refs: other_half_kernel(normaliser, *refs), place, [half, other, *own_parts],
        [array((feats_count, LANES), F32)] + results, depth, {3: 1, 4: 2},
    )
    return (grad_left, grad_right, grad_first, grad_motion_w, grad_gate_w, grad_cand_w)


def solution(mesh):
    in_specs = (
        P("rows", "cols", None),
        P("rows", "cols", None),
        P("rows", "cols", None),
        P("rows"),
        P("rows", None),
        P(),
        P(),
        P(),
        P("rows", "cols", None),
    )
    out_specs = (
        P("rows", "cols", None),
        P("rows", "cols", None),
        P("rows", "cols", None),
        P(),
        P(),
        P(),
    )
    return jax.shard_map(
        on_device, mesh=mesh, in_specs=in_specs, out_specs=out_specs, check_vma=False
    )
```

```python
import math

import jax
import jax.numpy as jnp
from jax import lax
from jax.experimental import pallas as pl
from jax.experimental.pallas import tpu as pltpu
from jax.sharding import PartitionSpec as P

LEVELS = 4
RADIUS = 4
DISP = 192
TAPS = 2 * RADIUS + 1
HALO = 16
LANES = 128
SPLIT = 2
CHUNK_ROWS = 56

BF16 = jnp.bfloat16
F32 = jnp.float32
VMEM = pl.BlockSpec(memory_space=pltpu.VMEM)
SMEM = pl.BlockSpec(memory_space=pltpu.SMEM)


def dot(a, b):
    return jnp.dot(a, b, preferred_element_type=F32)


def dot_nt(a, b):
    return lax.dot_general(a, b, (((1,), (1,)), ((), ())), preferred_element_type=F32)


def dot_tn(a, b):
    return lax.dot_general(a, b, (((0,), (0,)), ((), ())), preferred_element_type=F32)


def split_dot(a, table, contract):
    high = a.astype(BF16)
    low = (a - high.astype(F32)).astype(BF16)
    return contract(high, table) + contract(low, table)


def kernel_call(body, outs, ins, scalars, scratch, flops):
    bytes_moved = sum(math.prod(x.shape) * x.dtype.itemsize for x in (*ins, *outs))
    held = sum(math.prod(x.shape) * jnp.dtype(x.dtype).itemsize for x in scratch)
    return pl.pallas_call(
        body,
        out_shape=outs,
        in_specs=[SMEM] * scalars + [VMEM] * (len(ins) - scalars),
        out_specs=[VMEM] * len(outs),
        scratch_shapes=scratch,
        compiler_params=pltpu.CompilerParams(vmem_limit_bytes=bytes_moved + held + 4 * 2**20),
        cost_estimate=pl.CostEstimate(flops=flops, bytes_accessed=bytes_moved, transcendentals=0),
    )(*ins)


def array(shape, dtype):
    return jax.ShapeDtypeStruct(shape, dtype)


def lookup_rows(position, valid, disparity, offsets, row):
    count = position.shape[0]
    feature = lax.broadcasted_iota(jnp.int32, (count, LANES), 1)
    table = jnp.zeros((count, LANES), F32)
    for level in range(LEVELS):
        centre = (disparity[row] >> level) + offsets[row, level]
        tap = feature - level * TAPS
        matches = (position >> level) == tap + (centre - RADIUS)
        matches = matches & (tap >= 0) & (tap < TAPS) & valid
        table = jnp.where(matches, 1.0 / 2**level, table)
    return table.astype(BF16)


def sides(odd, first, second):
    return jnp.where(odd, first, second), jnp.where(odd, second, first)


def store_taps(ref, row, lane, step, value, forward):
    wide = value.shape[0]
    left = pltpu.roll(value, 1, 0).astype(BF16)
    right = pltpu.roll(value, wide - 1, 0).astype(BF16)
    taps = (left, value.astype(BF16), right) if forward else (right, value.astype(BF16), left)
    for tap in range(3):
        start = lane + tap * step
        ref[row, :, start : start + LANES] = taps[tap]


def pack_kernel(left, right, hidden, grads, out, sems):
    cols = left.shape[1]
    tail = DISP + HALO
    first, last = pl.ds(0, HALO), pl.ds(cols - HALO, HALO)
    low, high = pl.ds(0, LANES), pl.ds(LANES, LANES)
    every = pl.ds(0, 2 * LANES)
    moves = (
        (right, pl.ds(cols - tail, tail), pl.ds(0, tail), every),
        (left, last, pl.ds(tail, HALO), every),
        (left, first, pl.ds(tail + HALO, HALO), every),
        (right, first, pl.ds(tail + 2 * HALO, HALO), every),
        (hidden, last, pl.ds(tail + 3 * HALO, HALO), low),
        (hidden, first, pl.ds(tail + 3 * HALO, HALO), high),
        (grads, last, pl.ds(tail + 4 * HALO, HALO), low),
        (grads, first, pl.ds(tail + 4 * HALO, HALO), high),
    )
    copies = [
        pltpu.make_async_copy(source.at[:, start], out.at[:, stop, lanes], sems.at[number])
        for number, (source, start, stop, lanes) in enumerate(moves)
    ]
    for copy in copies:
        copy.start()
    for copy in copies:
        copy.wait()


def packed(left, right, hidden, grads):
    rows, cols, channels = left.shape
    count = DISP + 6 * HALO
    return pl.pallas_call(
        pack_kernel,
        out_shape=array((rows, count, channels), BF16),
        in_specs=[pl.BlockSpec(memory_space=pltpu.HBM)] * 4,
        out_specs=VMEM,
        scratch_shapes=[pltpu.SemaphoreType.DMA((8,))],
        compiler_params=pltpu.CompilerParams(vmem_limit_bytes=56 * 2**20),
        cost_estimate=pl.CostEstimate(flops=0, bytes_accessed=4 * rows * count * channels, transcendentals=0),
    )(left, right, hidden, grads)


def turn_kernel(gate_w, cand_w, gate_wt, cand_wt, cand_pair):
    deep = cand_w.shape[0] // 3
    nothing = jnp.zeros((deep, LANES), BF16)
    for row in range(4):
        here = slice(row * deep, (row + 1) * deep)
        cand_pair[here, :LANES] = cand_w[here] if row < 3 else nothing
        cand_pair[here, LANES:] = cand_w[(row - 1) * deep : row * deep] if row > 0 else nothing
    for tap in range(9):
        here = slice(tap * 2 * LANES, (tap + 1) * 2 * LANES)
        gate_wt[here] = gate_w[here].T
        cand_wt[tap * LANES : (tap + 1) * LANES] = cand_w[here].T


def spread_half(core, half, scale, gate, cand, parts, sems):
    count = parts.shape[1]
    there = pl.ds(pl.multiple_of(core * count, LANES), count)
    targets = (gate.at[there, pl.ds(0, LANES)], cand.at[there], gate.at[there, pl.ds(LANES, LANES)])
    copies = []
    for number, target in enumerate(targets):
        parts[number] = half[number * count : (number + 1) * count].astype(F32) * scale
        copies.append(pltpu.make_async_copy(parts.at[number], target, sems.at[number]))
        copies[-1].start()
    for copy in copies:
        copy.wait()


def own_half_kernel(scale, place, half, gate, cand, parts, sems):
    spread_half(place[1] % 2, half, scale, gate, cand, parts, sems)


def other_half_kernel(scale, place, half, other, gate_in, cand_in, motion, gate, cand, parts, sems):
    core = place[1] % 2
    start = 3 * parts.shape[1]
    count = motion.shape[0]
    rows = slice(start, start + LANES)
    motion[...] = jnp.where(core == 0, half[rows], other[rows]).astype(F32)[:count] * scale
    spread_half(1 - core, other, scale, gate, cand, parts, sems)


def half_call(body, place, arrays, outs, depth, aliases):
    anywhere = pl.BlockSpec(memory_space=pltpu.HBM)
    return pl.pallas_call(
        body,
        out_shape=outs,
        in_specs=[SMEM] + [VMEM] * (len(arrays) - len(aliases)) + [anywhere] * len(aliases),
        out_specs=[VMEM] * (len(outs) - 2) + [anywhere] * 2,
        scratch_shapes=[
            pltpu.VMEM((3, depth // 2, LANES), F32), pltpu.SemaphoreType.DMA((3,))
        ],
        input_output_aliases=aliases,
        compiler_params=pltpu.CompilerParams(vmem_limit_bytes=12 * 2**20),
        cost_estimate=pl.CostEstimate(flops=0, bytes_accessed=6 * depth * LANES, transcendentals=0),
    )(place, *arrays)


def motion_kernel(place, disparity, offsets, left, right, got_a, got_b, weight, hidden, grads,
                  motion, pre, feats, hidden_ext, grads_ext, ext, window, flipped):
    odd = place[1] % 2 == 1
    cols = left.shape[1]
    wide = cols + 2 * HALO
    block = wide // 2
    span = 512
    tail = DISP + HALO
    flat = (lax.broadcasted_iota(jnp.int32, (LANES, LANES), 0)
            + lax.broadcasted_iota(jnp.int32, (LANES, LANES), 1))
    mirror = jnp.where(flat == LANES - 1, 1.0, 0.0).astype(BF16)
    total = window.shape[0]
    position = lax.broadcasted_iota(jnp.int32, (span, LANES), 0) - (block - 1)
    valid = (position >= 0) & (position < DISP)
    for row in range(2):
        from_left, from_right = sides(odd, got_a[row], got_b[row])
        state, last = tail + 3 * HALO, HALO + cols
        hidden_ext[row, 0:HALO] = from_left[state : state + HALO, :LANES]
        hidden_ext[row, HALO:last] = hidden[row]
        hidden_ext[row, last:] = from_right[state : state + HALO, LANES:]
        grads_ext[row, 0:HALO] = from_left[state + HALO :, :LANES]
        grads_ext[row, HALO:last] = grads[row]
        grads_ext[row, last:] = from_right[state + HALO :, LANES:]
        motion[row, wide : wide + HALO] = from_left[state : state + HALO, :LANES]
        motion[row, wide + HALO :] = from_right[state : state + HALO, LANES:]
        ext[0:HALO] = from_left[tail : tail + HALO]
        ext[HALO : HALO + cols] = left[row]
        ext[HALO + cols : wide] = from_right[tail + HALO : tail + 2 * HALO]
        window[0:tail] = from_left[0:tail]
        window[tail : tail + cols] = right[row]
        window[tail + cols : tail + cols + HALO] = from_right[tail + 2 * HALO : tail + 3 * HALO]
        window[tail + cols + HALO :] = jnp.zeros((total - tail - cols - HALO, window.shape[1]), BF16)
        parts = total // LANES
        for part in range(parts):
            source = window[(parts - 1 - part) * LANES : (parts - part) * LANES]
            flipped[part * LANES : (part + 1) * LANES] = dot(mirror, source).astype(BF16)
        flipped[total:] = jnp.zeros((flipped.shape[0] - total, window.shape[1]), BF16)
        table = lookup_rows(position, valid, disparity, offsets, row)
        for part in range(2):
            start = part * block
            base = total - DISP - start - block
            scores = dot_nt(ext[start : start + block], flipped[base : base + span])
            scores = scores * (1.0 / math.sqrt(left.shape[2]))
            band = pltpu.roll(scores, 0, 1, stride=1, stride_axis=0)
            found = split_dot(band, table, dot).astype(BF16)
            value = dot(found, weight[...])
            feats[row, start : start + block] = found
            pre[row, start : start + block] = value
            motion[row, start : start + block] = (value * jax.nn.sigmoid(value)).astype(BF16)


def image_columns(place, wide, cols, cols_axis):
    column = lax.broadcasted_iota(jnp.int32, (wide, LANES), 0) - HALO + place[1] * cols
    return (column >= 0) & (column < cols * cols_axis)


def fill_neighbours(store, odd, first, second, wide):
    for row in range(2):
        above, below = sides(odd, first[row, :wide], second[row, :wide])
        store(row, above.astype(F32))
        store(4 + row, below.astype(F32))


def own_products(partial, taps, weights, source):
    deep = weights.shape[0] // 3
    block = partial.shape[1] // SPLIT
    for step in range(4 * SPLIT):
        row, start = step // SPLIT, (step % SPLIT) * block
        here = pl.ds(start, block)
        partial[row, here] = sum(
            dot(taps[source(row, a), here], weights[a * deep : (a + 1) * deep])
            for a in range(3)
            if source(row, a) in (0, 1)
        )


def own_gates_kernel(hidden, motion, gate_w, taps, partial):
    wide = hidden.shape[1]
    for row in range(2):
        store_taps(taps, row, 0, 2 * LANES, hidden[row].astype(F32), True)
        store_taps(taps, row, LANES, 2 * LANES, motion[row, :wide].astype(F32), True)
    own_products(partial, taps, gate_w, lambda row, a: row + a - 2)


def own_cand_kernel(grad_cand, cand_wt, partial, taps):
    for row in range(2):
        store_taps(taps, row, 0, LANES, grad_cand[row].astype(F32), False)
    own_products(partial, taps, cand_wt, lambda row, a: row - a)


def gates(fields, own, partial, resets, gate_w, update, reset, reset_hidden, wide):
    block = wide // SPLIT
    deep = gate_w.shape[0] // 3
    six = [fields.at[0], fields.at[1], own.at[0], own.at[1], fields.at[4], fields.at[5]]
    for step in range(4 * SPLIT):
        row, start = step // SPLIT, (step % SPLIT) * block
        here = pl.ds(start, block)
        total = partial[row, here] + sum(
            dot(six[row + a][here], gate_w[a * deep : (a + 1) * deep])
            for a in range(3)
            if row + a not in (2, 3)
        )
        reset_part = jax.nn.sigmoid(total[:, LANES:])
        update[row, here] = jax.nn.sigmoid(total[:, :LANES])
        reset[row, here] = reset_part
        hidden = six[row + 1][here, 2 * LANES : 3 * LANES].astype(F32)
        reset_hidden[row, here] = (reset_part * hidden).astype(BF16)
    for row in range(4):
        store_taps(resets, row, 0, 2 * LANES, reset_hidden[row].astype(F32), True)
        for tap in range(3):
            start = (2 * tap + 1) * LANES
            resets[row, :, start : start + LANES] = six[row + 1][:, start : start + LANES]


def load_field(odd, fields, lane, first, second):
    wide = fields.shape[1]
    fill_neighbours(lambda r, v: store_taps(fields, r, lane, 2 * LANES, v, True), odd, first, second, wide)


def candidates(resets, cand_pair, here):
    deep = cand_pair.shape[0] // 4
    total = sum(dot(resets[row, here], cand_pair[row * deep : (row + 1) * deep]) for row in range(4))
    return jnp.tanh(total[:, :LANES]), jnp.tanh(total[:, LANES:])


def first_kernel(cols_axis, place, hidden, init_a, init_b, motion_a, motion_b, gate_w, cand_w, own, partial,
                 later, update, reset, reset_hidden, candidate, hiddens, fields, resets):
    odd = place[0] % 2 == 1
    wide = hidden.shape[1]
    block = wide // SPLIT
    load_field(odd, fields, LANES, motion_a, motion_b)
    for row in range(2):
        got_a, got_b = (
            jnp.concatenate(
                [sent[row, wide : wide + HALO], inner[row], sent[row, wide + HALO :]], axis=0
            )
            for sent, inner in ((motion_a, init_a), (motion_b, init_b))
        )
        above, below = sides(odd, got_a, got_b)
        for there, value in ((row, above), (4 + row, below)):
            store_taps(fields, there, 0, 2 * LANES, value.astype(F32), True)
            if 0 < there < 5:
                hiddens[there - 1] = value
        hiddens[1 + row] = hidden[row]
    gates(fields, own, partial, resets, gate_w, update, reset, reset_hidden, wide)
    inside = image_columns(place, wide, wide - 2 * HALO, cols_axis)
    for start in range(0, wide, block):
        here = pl.ds(start, block)
        for row, new in enumerate(candidates(resets, cand_w, here)):
            candidate[row, here] = new
            gate = update[row + 1, here]
            old = hidden[row, here].astype(F32)
            value = (1.0 - gate) * old + gate * new
            later[row, here] = jnp.where(inside[start : start + block], value, 0.0).astype(BF16)


def gradients_out(grad, gate, new, old, row, here, grad_cand, grad_update, send_a, send_b):
    cand_part = (grad * gate * (1.0 - new * new)).astype(BF16)
    grad_cand[row, here] = cand_part
    send_a[row, here] = cand_part
    send_b[row, here] = cand_part
    grad_update[row, here] = (grad * (new - old) * gate * (1.0 - gate)).astype(BF16)


def send_updates(odd, grad_update, send_a, send_b):
    send_a[2], send_b[2] = sides(odd, grad_update[0], grad_update[1])


def second_kernel(place, hidden, hidden_a, hidden_b, motion_a, motion_b, gate_w, cand_w, own, partial, grad_hidden,
                  update, reset, reset_hidden, grad_cand, grad_update, send_a, send_b, fields, resets):
    odd = place[0] % 2 == 1
    wide = hidden.shape[1]
    block = wide // SPLIT
    load_field(odd, fields, LANES, motion_a, motion_b)
    load_field(odd, fields, 0, hidden_a, hidden_b)
    gates(fields, own, partial, resets, gate_w, update, reset, reset_hidden, wide)
    for start in range(0, wide, block):
        here = pl.ds(start, block)
        for row, new in enumerate(candidates(resets, cand_w, here)):
            gradients_out(grad_hidden[row, here].astype(F32), update[row + 1, here], new,
                          hidden[row, here].astype(F32), row, here, grad_cand, grad_update, send_a, send_b)
    send_updates(odd, grad_update, send_a, send_b)


def back_step(place, partial, grad_a, grad_b, grad_update, hiddens, reset, cand_wt, gate_wt,
              grad_reset, cand_taps, gate_taps, inner, grad_motion, finish):
    odd = place[0] % 2 == 1
    wide = partial.shape[1]
    block = wide // SPLIT
    fill_neighbours(lambda r, v: store_taps(cand_taps, r, 0, LANES, v, False), odd, grad_a, grad_b, wide)
    deep = cand_wt.shape[0] // 3
    deeper = gate_wt.shape[0] // 3

    for step in range(4 * SPLIT):
        row, start = step // SPLIT, (step % SPLIT) * block
        here = pl.ds(start, block)
        total = partial[row, here] + sum(
            dot(cand_taps[row + 2 - a, here], cand_wt[a * deep : (a + 1) * deep])
            for a in range(3)
            if row - a not in (0, 1)
        )
        inner[row, here] = total[:, :LANES]
        if row in (1, 2):
            grad_motion[row - 1, here] = total[:, LANES:]
    above_u, below_u = sides(odd, grad_a[2], grad_b[2])
    updates = (above_u, grad_update[0], grad_update[1], below_u)
    for row in range(4):
        gate = reset[row]
        value = (inner[row] * hiddens[row].astype(F32) * gate * (1.0 - gate)).astype(BF16)
        store_taps(gate_taps, row, 0, 2 * LANES, updates[row].astype(F32), False)
        store_taps(gate_taps, row, LANES, 2 * LANES, value.astype(F32), False)
        if row in (1, 2):
            grad_reset[row - 1] = value
    for row in range(2):
        for start in range(0, wide, block):
            here = pl.ds(start, block)
            total = sum(
                dot(gate_taps[row + 2 - a, here], gate_wt[a * deeper : (a + 1) * deeper]) for a in range(3)
            )
            grad_motion[row, here] += total[:, LANES:]
            finish(row, start, here, inner[row + 1, here] * reset[row + 1, here] + total[:, :LANES])


def later_back_kernel(cols_axis, place, partial, grad_a, grad_b, grad_update, hidden, hidden_a, hidden_b, reset,
                      cand_wt, gate_wt, update, grad_hidden, older_hiddens, older_update, older_candidate,
                      grad_reset, grad_state, grad_motion, older_cand, older_upd, send_a, send_b,
                      cand_taps, gate_taps, inner):
    odd = place[0] % 2 == 1
    wide = hidden.shape[1]
    block = wide // SPLIT
    inside = image_columns(place, wide, wide - 2 * HALO, cols_axis)

    def finish(row, start, here, terms):
        gate = update[row + 1, here]
        grad = grad_hidden[row, here].astype(F32) * (1.0 - gate) + terms
        grad = jnp.where(inside[start : start + block], grad, 0.0)
        grad_state[row, here] = grad
        gradients_out(grad, older_update[row + 1, here], older_candidate[row, here],
                      older_hiddens[row + 1, here].astype(F32), row, here, older_cand, older_upd, send_a, send_b)

    hiddens = hidden_rows(odd, hidden, hidden_a, hidden_b)
    back_step(place, partial, grad_a, grad_b, grad_update, hiddens, reset, cand_wt, gate_wt,
              grad_reset, cand_taps, gate_taps, inner, grad_motion, finish)
    send_updates(odd, older_upd, send_a, send_b)


def first_back_kernel(place, partial, grad_a, grad_b, grad_update, hiddens, reset,
                      cand_wt, gate_wt, update, grad_state, motion_so_far, pre, feats, weight,
                      motion, motion_a, motion_b, reset_sum, grad_first, grad_feats, kept, given,
                      cand_taps, gate_taps, inner, grad_motion, grad_reset, pixels, taps, parts):
    def finish(row, start, here, terms):
        gate = update[row + 1, here]
        grad = grad_state[row, here] * (1.0 - gate) + terms
        first, last = max(start, HALO), min(start + grad.shape[0], HALO + grad_first.shape[1])
        grad_first[row, first - HALO : last - HALO] = grad[first - start : last - start].astype(BF16)
        grad_motion[row, here] += motion_so_far[row, here]

    back_step(place, partial, grad_a, grad_b, grad_update, hiddens, reset, cand_wt, gate_wt,
              grad_reset, cand_taps, gate_taps, inner, grad_motion, finish)
    inner_cols = slice(HALO, HALO + grad_feats.shape[1])
    total = jnp.zeros((LANES, LANES), F32)
    for row in range(2):
        value = pre[row, inner_cols]
        gate = jax.nn.sigmoid(value)
        slope = gate * (1.0 + value * (1.0 - gate))
        grad_pre = (grad_motion[row, inner_cols] * slope).astype(BF16)
        total = total + dot_tn(feats[row, inner_cols], grad_pre)
        grad_feats[row] = dot_nt(grad_pre, weight[...])
    last_weights(place, hiddens, motion, motion_a, motion_b, grad_reset, reset_sum, total, kept, given, pixels, taps, parts)


def load_pixels(odd, pixels, hiddens, motion, motion_a, motion_b):
    wide = pixels.shape[0] // 4
    for row, value in enumerate(hidden_rows(odd, motion, motion_a, motion_b)):
        pixels[row * wide : (row + 1) * wide, LANES:] = value[:wide]
    for row, value in enumerate(hiddens):
        pixels[row * wide : (row + 1) * wide, :LANES] = value


def load_grads(taps, grads):
    wide = grads.shape[1]
    column = lax.broadcasted_iota(jnp.int32, (wide, LANES), 0)
    own = (column >= HALO) & (column < wide - HALO)
    depth = grads.shape[2]
    for row in range(2):
        for part in range(depth // LANES):
            value = jnp.where(own, grads[row, :, part * LANES : (part + 1) * LANES].astype(F32), 0.0)
            shifted = (pltpu.roll(value, wide - 1, 0), value, pltpu.roll(value, 1, 0))
            for tap in range(3):
                start = tap * depth + part * LANES
                taps[row * wide : (row + 1) * wide, start : start + LANES] = shifted[tap].astype(BF16)


def weight_products(pixels, taps, wide, depth, finish):
    for a in range(3):
        total = dot_tn(pixels[a * wide : (a + 2) * wide], taps[...])
        for b in range(3):
            finish((3 * a + b) * 2 * LANES, total[:, b * depth : (b + 1) * depth])


def hidden_rows(odd, hidden, hidden_a, hidden_b):
    above, below = sides(odd, hidden_a[1], hidden_b[1])[0], sides(odd, hidden_a[0], hidden_b[0])[1]
    return (above, hidden[0], hidden[1], below)


def load_hidden(pixels, rows, wide):
    for row, value in enumerate(rows):
        pixels[row * wide : (row + 1) * wide, :LANES] = value


def second_weights_kernel(place, resets, hidden, hidden_a, hidden_b, motion, motion_a, motion_b, cand_grads, update_grads,
                          cand_out, update_out, pixels, taps):
    odd = place[0] % 2 == 1
    wide = taps.shape[0] // 2
    load_pixels(odd, pixels, [resets[row] for row in range(4)], motion, motion_a, motion_b)
    load_grads(taps, cand_grads)

    def cand_finish(start, value):
        cand_out[pl.ds(start, 2 * LANES)] = value

    def update_finish(start, value):
        update_out[pl.ds(start, 2 * LANES)] = value

    weight_products(pixels, taps, wide, LANES, cand_finish)
    load_hidden(pixels, hidden_rows(odd, hidden, hidden_a, hidden_b), wide)
    load_grads(taps, update_grads)
    weight_products(pixels, taps, wide, LANES, update_finish)


def store_halves(parts, offset, rows, start, value):
    for piece in range(0, 2 * LANES, LANES):
        half, row = divmod(start + piece, rows // 2)
        there = offset + row
        parts[half, there : there + LANES] = value[piece : piece + LANES].astype(BF16)


def share_cores(place, parts, kept, given):
    core = place[1] % 2
    kept[...] = parts[core]
    given[...] = parts[1 - core]


def first_weights_kernel(place, resets, older, hidden, hidden_a, hidden_b, motion, motion_a, motion_b,
                         cand_grads, update_grads, reset_grads, cand_sum, update_sum,
                         kept, given, reset_out, pixels, taps, parts):
    odd = place[0] % 2 == 1
    wide = taps.shape[0] // 2
    rows = cand_sum.shape[0]
    load_pixels(odd, pixels, [resets[row] for row in range(4)], motion, motion_a, motion_b)
    load_grads(taps, cand_grads)

    def cand_finish(start, value):
        store_halves(parts, rows // 2, rows, start, cand_sum[pl.ds(start, 2 * LANES)] + value)

    def update_finish(start, value):
        store_halves(parts, 0, rows, start, update_sum[pl.ds(start, 2 * LANES)] + value)

    def reset_finish(start, value):
        reset_out[pl.ds(start, 2 * LANES)] = value

    weight_products(pixels, taps, wide, LANES, cand_finish)
    load_hidden(pixels, [older[row] for row in range(4)], wide)
    load_grads(taps, update_grads)
    weight_products(pixels, taps, wide, LANES, update_finish)
    share_cores(place, parts, kept, given)
    load_hidden(pixels, hidden_rows(odd, hidden, hidden_a, hidden_b), wide)
    load_grads(taps, reset_grads)
    weight_products(pixels, taps, wide, LANES, reset_finish)


def last_weights(place, hiddens, motion, motion_a, motion_b, reset_grads, reset_sum, motion_w,
                 kept, given, pixels, taps, parts):
    odd = place[0] % 2 == 1
    load_pixels(odd, pixels, [hiddens[row] for row in range(4)], motion, motion_a, motion_b)
    load_grads(taps, reset_grads)
    rows = reset_sum.shape[0]

    def finish(start, value):
        store_halves(parts, 0, rows, start, reset_sum[pl.ds(start, 2 * LANES)] + value)

    weight_products(pixels, taps, taps.shape[0] // 2, LANES, finish)
    parts[0, rows // 2 :] = motion_w.astype(BF16)
    parts[1, rows // 2 :] = jnp.zeros((parts.shape[1] - rows // 2, LANES), BF16)
    share_cores(place, parts, kept, given)


def add_kernel(kept, got, out):
    out[...] = (kept[...].astype(F32) + got[...].astype(F32)).astype(BF16)


def join_kernel(early, last_kept, last_got, half):
    split = early.shape[0]
    half[:split] = early[...]
    half[split:] = (last_kept[...].astype(F32) + last_got[...].astype(F32)).astype(BF16)


def right_kernel(place, own, back_a, back_b, grad_right):
    odd = place[1] % 2 == 1
    split = own.shape[1] - DISP
    for row in range(2):
        grad_right[row, :split] = own[row, :split].astype(BF16)
        returned = sides(odd, back_a[row], back_b[row])[1].astype(F32)
        grad_right[row, split:] = (own[row, split:] + returned).astype(BF16)


def band_back_kernel(place, disparity, offsets, left, right, got_a, got_b, grad_feats,
                     grad_left, back, own, window, grad_window):
    odd = place[1] % 2 == 1
    cols = left.shape[1]
    block = cols // 2
    span = 512
    scaling = 1.0 / math.sqrt(left.shape[2])
    position = DISP - lax.broadcasted_iota(jnp.int32, (span, LANES), 0)
    valid = (position >= 0) & (position < DISP)
    for row in range(2):
        from_left = sides(odd, got_a[row], got_b[row])[0]
        window[0:DISP] = from_left[HALO : HALO + DISP]
        window[DISP : DISP + cols] = right[row]
        window[DISP + cols :] = jnp.zeros((window.shape[0] - DISP - cols, window.shape[1]), BF16)
        grad_window[...] = jnp.zeros(grad_window.shape, F32)
        table = lookup_rows(position, valid, disparity, offsets, row)
        for part in range(2):
            here = slice(part * block, (part + 1) * block)
            there = slice(part * block, part * block + span)
            band = split_dot(grad_feats[row, here], table, dot_nt)
            scores = (pltpu.roll(band, 0, 1, stride=1, stride_axis=0) * scaling).astype(BF16)
            grad_left[row, here] = dot(scores, window[there]).astype(BF16)
            grad_window[there] += dot_tn(scores, left[row, here])
        back[row] = grad_window[0:DISP].astype(BF16)
        own[row] = grad_window[DISP : DISP + cols]


def pairings(count):
    first = [(2 * k, 2 * k + 1) for k in range(count // 2)]
    second = [(2 * k + 1, 2 * k + 2) for k in range(count // 2 - 1)]
    both = lambda pairs: pairs + [(b, a) for a, b in pairs]
    return both(first), both(second)


def exchanged(value, axis):
    first, second = pairings(lax.axis_size(axis))
    return lax.ppermute(value, axis, first), lax.ppermute(value, axis, second)


def exchanged_pair(value_a, value_b, axis):
    first, second = pairings(lax.axis_size(axis))
    other = lax.ppermute(value_b, axis, second)
    return lax.ppermute(value_a, axis, first), other


def core_groups():
    devices = lax.axis_size("rows") * lax.axis_size("cols")
    return [[i for i in range(devices) if i % 2 == c] for c in range(2)]


def shared_out(kept, got, last_kept, last_given, axes):
    total = kept.shape[0] + last_kept.shape[0]
    (early,) = kernel_call(add_kernel, [array(kept.shape, BF16)], [kept, got], 0, [], 0)
    last_got = swapped(last_given)
    early, last_got = lax.optimization_barrier((early, last_got))
    (half,) = kernel_call(join_kernel, [array((total, LANES), BF16)], [early, last_kept, last_got], 0, [], 0)
    half = half.reshape(len(core_groups()[0]), -1, LANES)
    return lax.all_to_all(half, axes, 0, 0, tiled=True, axis_index_groups=core_groups())


def spread_kernel(pieces, out):
    out[...] = jnp.broadcast_to(jnp.sum(pieces[...].astype(F32), axis=0).astype(BF16)[None], out.shape)


def gathered(pieces, axes):
    (spread,) = kernel_call(spread_kernel, [array(pieces.shape, BF16)], [pieces], 0, [], 0)
    half = lax.all_to_all(spread, axes, 0, 0, tiled=True, axis_index_groups=core_groups())
    return half.reshape(-1, LANES)


def swapped(value):
    return lax.ppermute(value, "cols", [(i, i ^ 1) for i in range(lax.axis_size("cols"))])


def on_device(
    fmap_left,
    fmap_right,
    hidden_init,
    disp_init,
    level_offset,
    motion_weight,
    gate_weight,
    cand_weight,
    grad_hidden,
):
    rows, cols, channels = fmap_left.shape
    wide = cols + 2 * HALO
    state = hidden_init.shape[2]
    feats_count = motion_weight.shape[0]
    rows_axis, cols_axis = lax.axis_size("rows"), lax.axis_size("cols")
    rows_index, cols_index = lax.axis_index("rows"), lax.axis_index("cols")
    place = jnp.stack([rows_index, cols_index]).astype(jnp.int32)

    maps_a, maps_b = exchanged(packed(fmap_left, fmap_right, hidden_init, grad_hidden), "cols")
    init_a, init_b = exchanged(hidden_init, "rows")
    motion_w = jnp.pad(motion_weight, ((0, LANES - feats_count), (0, 0)))
    field = lambda count, dtype: array((count, wide, LANES), dtype)
    band_flops = 2 * rows * wide * 512 * channels
    motion, motion_pre, feats, hidden, grads = kernel_call(
        motion_kernel,
        [array((2, wide + 2 * HALO, LANES), BF16), field(2, F32), field(2, BF16), field(2, BF16), field(2, BF16)],
        [place, disp_init, level_offset, fmap_left, fmap_right, maps_a, maps_b, motion_w, hidden_init, grad_hidden],
        3,
        [pltpu.VMEM((wide, channels), BF16), pltpu.VMEM((768, channels), BF16), pltpu.VMEM((832, channels), BF16)],
        2 * band_flops,
    )
    motion, init_a, init_b = lax.optimization_barrier((motion, init_a, init_b))
    motion_a, motion_b = exchanged(motion, "rows")
    gate_wt, cand_wt, cand_pair = kernel_call(
        turn_kernel,
        [array(gate_weight.shape, BF16), array((9 * state, 2 * state), BF16), array((24 * state, 2 * state), BF16)],
        [gate_weight, cand_weight],
        0,
        [],
        0,
    )
    motion_a, motion_b, gate_wt, cand_wt, cand_pair = lax.optimization_barrier(
        (motion_a, motion_b, gate_wt, cand_wt, cand_pair)
    )
    motions = (motion, motion_a, motion_b)
    unit = 2 * wide * 9 * 2 * state * state
    fields = [pltpu.VMEM((6, wide, 6 * LANES), BF16), pltpu.VMEM((4, wide, 6 * LANES), BF16)]

    field_taps = array((2, wide, 6 * LANES), BF16)
    partials = array((4, wide, 2 * LANES), F32)
    own_taps, partial = kernel_call(
        own_gates_kernel, [field_taps, partials], [hidden, motion, gate_weight], 0, [], 4 * unit
    )
    hidden_1, update_0, reset_0, reset_hidden_0, candidate_0, hiddens_0 = kernel_call(
        lambda *refs: first_kernel(cols_axis, *refs),
        [field(2, BF16), field(4, F32), field(4, F32), field(4, BF16), field(2, F32), field(4, BF16)],
        [place, hidden, init_a, init_b, *motions[1:], gate_weight, cand_pair, own_taps, partial],
        1,
        fields,
        10 * unit,
    )
    hidden_1a, hidden_1b = exchanged(hidden_1, "rows")
    own_taps, partial = kernel_call(
        own_gates_kernel, [field_taps, partials], [hidden_1, motion, gate_weight], 0, [], 4 * unit
    )
    update_1, reset_1, reset_hidden_1, grad_cand_1, grad_update_1, send_a, send_b = kernel_call(
        second_kernel,
        [field(4, F32), field(4, F32), field(4, BF16), field(2, BF16), field(2, BF16), field(3, BF16), field(3, BF16)],
        [place, hidden_1, hidden_1a, hidden_1b, *motions[1:], gate_weight, cand_pair, own_taps, partial, grads],
        1,
        fields,
        10 * unit,
    )
    got_a, got_b = exchanged_pair(send_a, send_b, "rows")
    pixels = pltpu.VMEM((4 * wide, 2 * LANES), BF16)
    taps = pltpu.VMEM((2 * wide, 3 * LANES), BF16)
    weights = array(cand_weight.shape, F32)
    cand_sum, update_sum = kernel_call(
        second_weights_kernel,
        [weights, weights],
        [place, reset_hidden_1, hidden_1, hidden_1a, hidden_1b, *motions, grad_cand_1, grad_update_1],
        1,
        [pixels, taps],
        4 * unit,
    )
    (partial,) = kernel_call(
        own_cand_kernel, [partials], [grad_cand_1, cand_wt], 0, [pltpu.VMEM((2, wide, 3 * LANES), BF16)], 2 * unit
    )
    got_a, got_b, cand_sum, update_sum = lax.optimization_barrier((got_a, got_b, cand_sum, update_sum))
    back_scratch = [
        pltpu.VMEM((6, wide, 3 * LANES), BF16),
        pltpu.VMEM((4, wide, 6 * LANES), BF16),
        pltpu.VMEM((4, wide, LANES), F32),
    ]
    grad_reset_1, grad_state, grad_motion_1, grad_cand_0, grad_update_0, send_a, send_b = kernel_call(
        lambda *refs: later_back_kernel(cols_axis, *refs),
        [field(2, BF16), field(2, F32), field(2, F32), field(2, BF16), field(2, BF16),
         field(3, BF16), field(3, BF16)],
        [place, partial, got_a, got_b, grad_update_1, hidden_1, hidden_1a, hidden_1b, reset_1, cand_wt, gate_wt,
         update_1, grads, hiddens_0, update_0, candidate_0],
        1,
        back_scratch,
        8 * unit,
    )
    got_a, got_b = exchanged_pair(send_a, send_b, "rows")
    depth = cand_weight.shape[0]
    total = rows_axis * cols_axis * CHUNK_ROWS // 2
    late = total - depth
    kept, given, reset_sum = kernel_call(
        first_weights_kernel,
        [array((depth, LANES), BF16), array((depth, LANES), BF16), weights],
        [place, reset_hidden_0, hiddens_0, hidden_1, hidden_1a, hidden_1b, *motions,
         grad_cand_0, grad_update_0, grad_reset_1, cand_sum, update_sum],
        1,
        [pixels, taps, pltpu.VMEM((2, depth, LANES), BF16)],
        6 * unit,
    )
    (partial,) = kernel_call(
        own_cand_kernel, [partials], [grad_cand_0, cand_wt], 0, [pltpu.VMEM((2, wide, 3 * LANES), BF16)], 2 * unit
    )
    got_a, got_b, kept, given, reset_sum, partial = lax.optimization_barrier(
        (got_a, got_b, kept, given, reset_sum, partial)
    )
    got = swapped(given)
    grad_first, grad_feats, last_kept, last_given = kernel_call(
        first_back_kernel,
        [array((2, cols, LANES), BF16), array((2, cols, LANES), F32), array((late, LANES), BF16), array((late, LANES), BF16)],
        [place, partial, got_a, got_b, grad_update_0, hiddens_0, reset_0, cand_wt, gate_wt,
         update_0, grad_state, grad_motion_1, motion_pre, feats, motion_w, *motions, reset_sum],
        1,
        back_scratch + [pltpu.VMEM((2, wide, LANES), F32), pltpu.VMEM((2, wide, LANES), BF16), pixels, taps,
                        pltpu.VMEM((2, late, LANES), BF16)],
        10 * unit,
    )
    last_kept, last_given, got = lax.optimization_barrier((last_kept, last_given, got))
    grad_left, back, own = kernel_call(
        band_back_kernel,
        [array((2, cols, channels), BF16), array((2, DISP, channels), BF16), array((2, cols, channels), F32)],
        [place, disp_init, level_offset, fmap_left, fmap_right, maps_a, maps_b, grad_feats],
        3,
        [pltpu.VMEM((768, channels), BF16), pltpu.VMEM((768, channels), F32)],
        3 * band_flops,
    )
    pieces = shared_out(kept, got, last_kept, last_given, ("rows", "cols"))
    pieces, grad_left, back, own = lax.optimization_barrier((pieces, grad_left, back, own))
    back_a, back_b = exchanged(back, "cols")
    (grad_right,) = kernel_call(
        right_kernel, [array((2, cols, channels), BF16)], [place, own, back_a, back_b], 1, [], 0
    )
    half = gathered(pieces, ("rows", "cols"))
    half, grad_right = lax.optimization_barrier((half, grad_right))
    normaliser = 1.0 / math.sqrt(rows * rows_axis * cols * cols_axis)
    other = swapped(half)
    results = [array(gate_weight.shape, F32), array(cand_weight.shape, F32)]
    own_parts = half_call(
        lambda *refs: own_half_kernel(normaliser, *refs), place, [half], results, depth, {}
    )
    other, *own_parts = lax.optimization_barrier((other, *own_parts))
    grad_motion_w, grad_gate_w, grad_cand_w = half_call(
        lambda *refs: other_half_kernel(normaliser, *refs), place, [half, other, *own_parts],
        [array((feats_count, LANES), F32)] + results, depth, {3: 1, 4: 2},
    )
    return (grad_left, grad_right, grad_first, grad_motion_w, grad_gate_w, grad_cand_w)


def solution(mesh):
    in_specs = (
        P("rows", "cols", None),
        P("rows", "cols", None),
        P("rows", "cols", None),
        P("rows"),
        P("rows", None),
        P(),
        P(),
        P(),
        P("rows", "cols", None),
    )
    out_specs = (
        P("rows", "cols", None),
        P("rows", "cols", None),
        P("rows", "cols", None),
        P(),
        P(),
        P(),
    )
    return jax.shard_map(
        on_device, mesh=mesh, in_specs=in_specs, out_specs=out_specs, check_vma=False
    )
```
